32 devices in a mesh: lx: 2 (over x), ly: 4 (over y, core), col: 4 (over z).
Axes of the slice: x: 2, y: 2, z: 4, core: 2. Of those that a mesh axis runs over, the one named last changes fastest.
Arguments:
- start: float32 [64, 128, 512], P('col', 'lx', 'ly'), may hold values from -360 to 360
- levels: int32 [128, 512], P('lx', 'ly'), may hold values from 0 to 15
Outputs:
- basis: float32 [64, 128, 512], P(None, ('lx', 'col'), 'ly')
The draws below stay inside these ranges and needn't reach their ends.
All inputs are finite; a program needn't handle non-finite values.
Results may differ from the reference program's by a relative error of at most 0.00014.
Values sent between devices are 32-bit elements; how exact they have to be, the bound alone decides.
No kernel may reach another device: no remote copies, remote signals or barrier semaphores. Data moves between devices by JAX's collectives and lax.ppermute only.
A program may use at most 64 MiB of HBM per device.

```python
import math
import jax
import jax.numpy as jnp
from jax import lax

NCOLS = 64
NX = 128
NY = 512


def draw_start(key, part):
    key_noise = jax.random.fold_in(key, 11)
    key_cols = jax.random.fold_in(key, 12)
    x_frac = jnp.arange(NX, dtype=jnp.float32)[:, None] / NX
    y_frac = jnp.arange(NY, dtype=jnp.float32)[None, :] / NY
    row_scale = jnp.exp(math.log(3.0) * (x_frac + y_frac))
    col_scale = jnp.exp(math.log(10.0) * jax.random.uniform(key_cols, (NCOLS, 1, 1), jnp.float32))
    noise_part = jnp.clip(jax.random.normal(key_noise, (NCOLS, NX, NY), jnp.float32), -4.0, 4.0)
    return noise_part * col_scale * row_scale


def place_ends(values, rng, least, high):
    longest = values.shape.index(max(values.shape))
    spots = []
    for shift in (0, 1):
        where = [jax.random.randint(jax.random.fold_in(rng, axis), (), 0, length) for axis, length in enumerate(values.shape)]
        where[longest] = (where[longest] + shift) % values.shape[longest]
        spots.append(tuple(where))
    return values.at[spots[0]].set(least).at[spots[1]].set(high)


def setup_inputs(seed: int = 0) -> dict:
    streams_of = jax.random.split(jax.random.key(seed), 3)
    return {
        "start": draw_start(jax.random.fold_in(streams_of[2], 71), 0),
        "levels": place_ends(jax.random.randint(streams_of[1], (NX, NY), 0, 16), jax.random.fold_in(streams_of[1], 1), 0, 15).astype(jnp.int32),
    }


center = 2.1
half_width = 3.1
spread_width = 4.0
level_top = 15.0

def onsite_of(levels):
    return spread_width * (levels.astype(jnp.float32) / level_top - 0.5)

def hop_field(field, onsite, even_sites):
    above = jnp.roll(field, -1, 0)
    below = jnp.roll(field, 1, 0)
    left_side = jnp.roll(field, 1, 1)
    right_side = jnp.roll(field, -1, 1)
    vertical = jnp.where(even_sites, above, below)
    return ((onsite - center) * field - (left_side + right_side + vertical)) / half_width

def reference(start, levels):
    onsite = onsite_of(levels)
    grid_x = jnp.arange(NX, dtype=jnp.int32)[:, None]
    grid_y = jnp.arange(NY, dtype=jnp.int32)[None, :]
    even_sites = (grid_x + grid_y) % 2 == 0

    def filter_column(column):
        first_term = hop_field(column, onsite, even_sites)
        return 2.0 * hop_field(first_term, onsite, even_sites) - column
    filtered = lax.map(filter_column, start)
    flat_rows = filtered.reshape(NCOLS, NX * NY)
    gram_matrix = jnp.dot(flat_rows.astype(jnp.float32), flat_rows.T.astype(jnp.float32), precision=lax.Precision.HIGHEST, preferred_element_type=jnp.float32)
    upper_tri = jnp.linalg.cholesky(gram_matrix).T
    solved = lax.linalg.triangular_solve(upper_tri.T, flat_rows, left_side=True, lower=True)
    return (solved * math.sqrt(NX * NY)).reshape(NCOLS, NX, NY)
```

```python
import functools
import math

import jax
import jax.numpy as jnp
from jax import lax
from jax.experimental import pallas as pl
from jax.experimental.pallas import tpu as pltpu
from jax.sharding import PartitionSpec as P

center = 2.1
half_width = 3.1
spread_width = 4.0
level_top = 15.0
lanes = 128
tile = 8
per_pack = lanes // 4


def iota(shape, dim):
    return lax.broadcasted_iota(jnp.int32, shape, dim)


def site_factor(levels):
    onsite = spread_width * (levels / level_top - 0.5)
    return (onsite - center) / half_width


def packing(rows, chunks):
    order = [0, rows - 1] + list(range(1, rows - 1))
    return [(row, chunk) for row in order for chunk in range(chunks)]


def pack_kernel(cols, rows, start_ref, levels_ref, edges_ref, outer_ref):
    chunks = cols // tile
    lane = iota((tile, lanes), 1)
    slots = packing(rows, chunks)
    groups = len(slots) // per_pack

    def tile_of(row, chunk):
        return start_ref[pl.ds(chunk * tile * rows + row, tile, stride=rows), :]

    for group in range(groups):
        packed = jnp.zeros((tile, lanes), jnp.float32)
        for k in range(per_pack):
            row, chunk = slots[group * per_pack + k]
            moved = pltpu.roll(tile_of(row, chunk), (4 * k + 2) % lanes, 1)
            packed = jnp.where(lane // 4 == k, moved, packed)
        edges_ref[group] = packed
    packed = jnp.zeros((tile, lanes), jnp.float32)
    for k in range(rows // tile):
        moved = pltpu.roll(levels_ref[k * tile : (k + 1) * tile, :].astype(jnp.float32), 4 * k + 2, 1)
        packed = jnp.where(lane // 4 == k, moved, packed)
    edges_ref[groups] = packed
    for chunk in range(chunks):
        outer_ref[chunk] = tile_of(0, chunk)
        outer_ref[chunks + chunk] = tile_of(rows - 1, chunk)
    first = levels_ref[0:1, :].astype(jnp.float32)
    last = levels_ref[rows - 1 : rows, :].astype(jnp.float32)
    outer_ref[2 * chunks] = jnp.where(iota((tile, lanes), 0) == 0, first, last)


def filter_kernel(
    cols, rows, parts, start_ref, levels_ref, edges_ref, before_ref, after_ref, *rest
):
    out_refs = rest[:parts]
    field, edge, once, once_edge, done, factor, factor_edge = rest[parts:]
    chunks = cols // tile
    slots = packing(rows, chunks)
    groups = len(slots) // per_pack
    lane = iota((cols, lanes), 1)
    first_lane, last_lane = lane == 0, lane == lanes - 1
    even_lane = lane % 2 == 0
    inverse = 1.0 / half_width

    factor[0:rows, :] = site_factor(levels_ref[...].astype(jnp.float32))
    factor[rows : rows + 1, :] = site_factor(before_ref[2 * chunks, 1:2, :])
    factor[rows + 1 : rows + 2, :] = site_factor(after_ref[2 * chunks, 0:1, :])
    packed = edges_ref[groups]
    for k in range(rows // tile):
        factor_edge[k * tile : (k + 1) * tile, :] = site_factor(
            pltpu.roll(packed, lanes - (4 * k + 2), 1)
        )
    for row in range(rows):
        field[row + 1] = start_ref[pl.ds(row, cols, stride=rows), :]
    for chunk in range(chunks):
        part = pl.ds(chunk * tile, tile)
        field[0, part, :] = before_ref[chunks + chunk]
        field[rows + 1, part, :] = after_ref[chunk]
        edge[0, part, :] = pltpu.roll(
            before_ref[2 * chunks + 1], lanes - (4 * (chunks + chunk) + 2), 1
        )
        edge[rows + 1, part, :] = pltpu.roll(
            after_ref[2 * chunks + 1], lanes - (4 * chunk + 2), 1
        )
    for slot, (row, chunk) in enumerate(slots):
        edge[row + 1, pl.ds(chunk * tile, tile), :] = pltpu.roll(
            edges_ref[slot // per_pack], lanes - (4 * (slot % per_pack) + 2), 1
        )

    def sides(main, other):
        return pltpu.roll(jnp.where(last_lane, other, main), 1, 1) + pltpu.roll(
            jnp.where(first_lane, other, main), lanes - 1, 1
        )

    def factor_at(ref, row):
        return jnp.broadcast_to(ref[row : row + 1, :], (cols, lanes))

    for row in range(-1, rows + 1):
        here, beside = field[row + 1], edge[row + 1]
        even = even_lane if row % 2 == 0 else jnp.logical_not(even_lane)
        if row == -1:
            vertical, where = field[1], rows
        elif row == rows:
            vertical, where = field[rows], rows + 1
        else:
            vertical, where = jnp.where(even, field[row + 2], field[row]), row
        once[row + 1] = factor_at(factor, where) * here - inverse * (
            sides(here, beside) + vertical
        )
        if 0 <= row < rows:
            vertical = jnp.where(even, edge[row + 2], edge[row])
            once_edge[row] = factor_at(factor_edge, row) * beside - inverse * (
                sides(beside, here) + vertical
            )
    for row in range(rows):
        here = once[row + 1]
        even = even_lane if row % 2 == 0 else jnp.logical_not(even_lane)
        vertical = jnp.where(even, once[row + 2], once[row])
        twice = factor_at(factor, row) * here - inverse * (
            sides(here, once_edge[row]) + vertical
        )
        done[row] = 2.0 * twice - field[row + 1]
    place = lax.axis_index("col")
    part_rows = rows // parts
    for k in range(parts):
        out_refs[k][...] = done[pl.ds((place ^ k) * part_rows, part_rows)]


def split(values):
    high = values.astype(jnp.bfloat16)
    rest = values - high.astype(jnp.float32)
    middle = rest.astype(jnp.bfloat16)
    low = (rest - middle.astype(jnp.float32)).astype(jnp.bfloat16)
    return high, middle, low


def gram_kernel(cols, parts, *refs):
    piece_refs, (whole_ref, gram_ref) = refs[:parts], refs[parts:]
    part_rows = whole_ref.shape[0]
    total = cols * parts
    place = lax.axis_index("col")
    for k in range(parts):
        whole_ref[:, pl.ds(pl.multiple_of((place ^ k) * cols, tile), cols), :] = piece_refs[k][...]
    products = jnp.zeros((3 * total, 3 * total), jnp.float32)
    for row in range(0, part_rows, 2):
        values = jnp.concatenate([whole_ref[row], whole_ref[row + 1]], axis=1)
        stack = jnp.concatenate(split(values), axis=0)
        products += lax.dot_general(
            stack, stack, (((1,), (1,)), ((), ())), preferred_element_type=jnp.float32
        )
    gram = jnp.zeros((total, total), jnp.float32)
    for i in reversed(range(3)):
        for j in reversed(range(3)):
            gram += products[i * total : (i + 1) * total, j * total : (j + 1) * total]
    half = total // 2
    gram_ref[...] = jnp.concatenate([gram[:half], gram[half:]], axis=1)


def solve_kernel(scale, whole_ref, gram_ref, other_ref, out_ref):
    part_rows, total, _ = whole_ref.shape
    blocks = total // tile
    half = total // 2
    packed = gram_ref[...] + other_ref[...]
    lane = iota((tile, lanes), 1)
    sub = iota((tile, lanes), 0)
    shape = (tile, lanes)
    work = []
    for i in range(blocks):
        at = i * tile % half
        block = packed[at : at + tile, :]
        if i * tile >= half:
            block = pltpu.roll(block, total, 1)
        unit = jnp.where(lane - total == sub + i * tile, 1.0, 0.0)
        work.append(jnp.where(lane < total, block, unit))
    for b in range(blocks):
        column = {
            i: [
                jnp.broadcast_to(work[i][:, b * tile + m : b * tile + m + 1], shape)
                for m in range(tile)
            ]
            for i in range(b, blocks)
        }
        for m in range(tile):
            pivot = jnp.broadcast_to(column[b][m][m : m + 1, :], shape)
            root = lax.rsqrt(pivot)
            root = root * (1.5 - 0.5 * (pivot * root) * root)
            row = jnp.broadcast_to(work[b][m : m + 1, :], shape) * root
            heads = [
                jnp.broadcast_to(column[b][p][m : m + 1, :], shape) * root
                for p in range(m + 1, tile)
            ]
            for i in range(b, blocks):
                ratio = column[i][m] * root
                if i == b:
                    ratio = jnp.where(sub > m, ratio, 0.0)
                    work[i] = jnp.where(sub == m, row, work[i] - ratio * row)
                else:
                    work[i] = work[i] - ratio * row
                for p in range(m + 1, tile):
                    column[i][p] = column[i][p] - ratio * heads[p - m - 1]
    solver = jnp.concatenate(work, axis=0) * scale
    wide = iota((total, lanes), 1)
    high, middle, low = (piece.astype(jnp.float32) for piece in split(solver))

    def pair(left, right):
        return jnp.where(wide < total, pltpu.roll(left, total, 1), right).astype(jnp.bfloat16)

    left_main = jnp.concatenate([pair(high, high), pair(middle, middle)], axis=1)
    left_rest = pair(high, low)
    for row in range(0, part_rows, 2):
        values = jnp.concatenate([whole_ref[row], whole_ref[row + 1]], axis=1)
        f_high, f_middle, f_low = split(values)
        right_main = jnp.concatenate([f_high, f_middle, f_high, f_middle], axis=0)
        right_rest = jnp.concatenate([f_low, f_high], axis=0)
        result = jnp.dot(left_rest, right_rest, preferred_element_type=jnp.float32) + jnp.dot(
            left_main, right_main, preferred_element_type=jnp.float32
        )
        out_ref[pl.ds(row, total, stride=part_rows), :] = result[:, :lanes]
        out_ref[pl.ds(row + 1, total, stride=part_rows), :] = result[:, lanes:]


def call(kernel, outs, *operands, scratch=()):
    return pl.pallas_call(
        kernel,
        out_shape=[jax.ShapeDtypeStruct(shape, jnp.float32) for shape in outs],
        scratch_shapes=[pltpu.VMEM(shape, jnp.float32) for shape in scratch],
        compiler_params=pltpu.CompilerParams(vmem_limit_bytes=32 * 1024 * 1024),
    )(*operands)


def exchange(values, axis, distance):
    count = lax.axis_size(axis)
    return lax.ppermute(values, axis, [(i, i ^ distance) for i in range(count)])


def shards(start, levels):
    cols, rows, _ = start.shape
    parts = lax.axis_size("col")
    chunks = cols // tile
    groups = rows * chunks // per_pack
    total = cols * parts
    part_rows = rows // parts
    flat = start.reshape(cols * rows, lanes)
    edges, outer = call(
        functools.partial(pack_kernel, cols, rows),
        [(groups + 1, tile, lanes), (2 * chunks + 1, tile, lanes)],
        flat,
        levels,
    )
    count = lax.axis_size("ly")
    near = exchange(edges, "ly", 1)
    far_pairs = [(i, (i + 1) % count if i % 2 else (i - 1) % count) for i in range(count)]
    far = lax.ppermute(edges, "ly", far_pairs)
    even_place = lax.axis_index("ly") % 2 == 0
    from_left = lax.broadcasted_iota(jnp.int32, edges.shape, 2) % 4 < 2
    beside = jnp.where(from_left == even_place, far, near)
    outer = jnp.concatenate([outer, beside[:1]], axis=0)
    count = lax.axis_size("lx")
    before = lax.ppermute(outer, "lx", [(i, (i + 1) % count) for i in range(count)])
    after = before
    if count > 2:
        after = lax.ppermute(outer, "lx", [((i + 1) % count, i) for i in range(count)])
    pieces = call(
        functools.partial(filter_kernel, cols, rows, parts),
        [(part_rows, cols, lanes)] * parts,
        flat,
        levels,
        beside,
        before,
        after,
        scratch=[
            (rows + 2, cols, lanes),
            (rows + 2, cols, lanes),
            (rows + 2, cols, lanes),
            (rows, cols, lanes),
            (rows, cols, lanes),
            (rows + tile, lanes),
            (rows, lanes),
        ],
    )
    arrived = {0: pieces[0]}
    for k in sorted(range(1, parts), key=lambda k: -(k & -k) if k != parts - 1 else 0):
        arrived[k] = exchange(pieces[k], "col", k)
    whole, gram = call(
        functools.partial(gram_kernel, cols, parts),
        [(part_rows, total, lanes), (total // 2, 2 * total)],
        *(arrived[k] for k in range(parts)),
    )
    steps = []
    for axis in ("ly", "lx", "col"):
        bit = 1
        while bit < lax.axis_size(axis):
            steps.append((axis, bit))
            bit *= 2
    for axis, bit in steps[:-1]:
        gram = gram + exchange(gram, axis, bit)
    scale = math.sqrt(rows * lax.axis_size("lx") * lanes * lax.axis_size("ly"))
    (basis,) = call(
        functools.partial(solve_kernel, scale),
        [(total * part_rows, lanes)],
        whole,
        gram,
        exchange(gram, *steps[-1]),
    )
    return basis.reshape(total, part_rows, lanes)


def solution(mesh):
    placed = (P("col", "lx", "ly"), P("lx", "ly"))
    return jax.shard_map(
        shards, mesh=mesh, in_specs=placed, out_specs=P(None, ("lx", "col"), "ly"), check_vma=False
    )
```

```python
import functools
import math

import jax
import jax.numpy as jnp
from jax import lax
from jax.experimental import pallas as pl
from jax.experimental.pallas import tpu as pltpu
from jax.sharding import PartitionSpec as P

center = 2.1
half_width = 3.1
spread_width = 4.0
level_top = 15.0
lanes = 128
tile = 8


def iota(shape, dim):
    return lax.broadcasted_iota(jnp.int32, shape, dim)


def site_factor(levels):
    onsite = spread_width * (levels / level_top - 0.5)
    return (onsite - center) / half_width


def tile_at(ref, rows, row, chunk):
    return ref[pl.ds(chunk * tile * rows + row, tile, stride=rows), :]


def pack_edges(tiles):
    lane = iota((tile, lanes), 1)
    packed = jnp.zeros((tile, lanes), jnp.float32)
    for k, values in enumerate(tiles):
        moved = pltpu.roll(values, (4 * k + 2) % lanes, 1)
        packed = jnp.where(lane // 4 == k, moved, packed)
    return packed


def unpack_edges(packed, k):
    return pltpu.roll(packed, lanes - (4 * k + 2), 1)


def pack_kernel(cols, rows, parts, early, start_ref, levels_ref, edges_ref, outer_ref, *piece_refs):
    chunks = cols // tile
    part_rows = rows // parts
    for group in range(parts):
        edges_ref[group] = pack_edges(
            tile_at(start_ref, rows, group * part_rows + row, chunk)
            for row in range(part_rows)
            for chunk in range(chunks)
        )
    edges_ref[parts] = pack_edges(
        levels_ref[k * tile : (k + 1) * tile, :].astype(jnp.float32) for k in range(rows // tile)
    )
    for chunk in range(chunks):
        outer_ref[chunk] = tile_at(start_ref, rows, 0, chunk)
        outer_ref[chunks + chunk] = tile_at(start_ref, rows, rows - 1, chunk)
    first = levels_ref[0:1, :].astype(jnp.float32)
    last = levels_ref[rows - 1 : rows, :].astype(jnp.float32)
    outer_ref[2 * chunks] = jnp.where(iota((tile, lanes), 0) == 0, first, last)
    for k, piece_ref in zip(early, piece_refs):
        copy_piece(cols, rows, parts, k, start_ref, piece_ref)


def copy_piece(cols, rows, parts, k, start_ref, piece_ref):
    chunks = cols // tile
    part_rows = rows // parts
    base = (lax.axis_index("col") ^ k) * part_rows
    for row in range(part_rows):
        for chunk in range(chunks):
            piece_ref[row * chunks + chunk] = tile_at(start_ref, rows, base + row, chunk)


def outer_kernel(cols, rows, parts, early, start_ref, outer_ref, near_ref, far_ref, beside_ref, send_ref, *piece_refs):
    from_left = iota((tile, lanes), 1) % 4 < 2
    even_place = lax.axis_index("ly") % 2 == 0
    for group in range(parts + 1):
        near, far = near_ref[group], far_ref[group]
        beside_ref[group] = jnp.where(
            even_place, jnp.where(from_left, far, near), jnp.where(from_left, near, far)
        )
    count = outer_ref.shape[0]
    send_ref[:count] = outer_ref[...]
    send_ref[count] = beside_ref[0]
    send_ref[count + 1] = beside_ref[parts - 1]
    for k, piece_ref in zip(early, piece_refs):
        copy_piece(cols, rows, parts, k, start_ref, piece_ref)


def rim_kernel(cols, rows, parts, late, start_ref, beside_ref, before_ref, after_ref, *out_refs):
    chunks = cols // tile
    part_rows = rows // parts
    place = lax.axis_index("col")
    for k, out_ref in enumerate(out_refs):
        target = place ^ k
        at = 0
        if k in late:
            at = part_rows * chunks
            copy_piece(cols, rows, parts, k, start_ref, out_ref)
        lowest, highest = target == 0, target == parts - 1
        above = jnp.maximum(target * part_rows - 1, 0)
        below = jnp.minimum((target + 1) * part_rows, rows - 1)
        for chunk in range(chunks):
            out_ref[at + chunk] = jnp.where(
                lowest, before_ref[chunks + chunk], tile_at(start_ref, rows, above, chunk)
            )
            out_ref[at + chunks + chunk] = jnp.where(
                highest, after_ref[chunk], tile_at(start_ref, rows, below, chunk)
            )
        at += 2 * chunks
        out_ref[at] = beside_ref[target]
        out_ref[at + 1] = jnp.where(
            lowest, before_ref[2 * chunks + 2], beside_ref[jnp.maximum(target - 1, 0)]
        )
        out_ref[at + 2] = jnp.where(
            highest, after_ref[2 * chunks + 1], beside_ref[jnp.minimum(target + 1, parts - 1)]
        )


def filter_kernel(cols, rows, parts, late, start_ref, levels_ref, beside_ref, before_ref, after_ref, *refs):
    rim_refs, refs = refs[:parts], refs[parts:]
    piece_refs = dict(zip([k for k in range(1, parts) if k not in late], refs))
    whole_ref, gram_ref, field, edge, once, once_edge, factor, factor_edge = refs[len(piece_refs) :]
    chunks = cols // tile
    part_rows = rows // parts
    total = cols * parts
    place = lax.axis_index("col")
    lane = iota((total, lanes), 1)
    first_lane, last_lane = lane == 0, lane == lanes - 1
    even_lane = lane % 2 == 0
    inverse = 1.0 / half_width

    factor[tile : tile + rows, :] = site_factor(levels_ref[...].astype(jnp.float32))
    factor[tile - 1 : tile, :] = site_factor(before_ref[2 * chunks, 1:2, :])
    factor[tile + rows : tile + rows + 1, :] = site_factor(after_ref[2 * chunks, 0:1, :])
    packed = beside_ref[parts]
    for k in range(rows // tile):
        factor_edge[k * tile : (k + 1) * tile, :] = site_factor(unpack_edges(packed, k))
    for k in range(parts):
        base = (place ^ k) * cols
        at = part_rows * chunks if k in late else 0
        rim_ref = rim_refs[k]
        for chunk in range(chunks):
            part = pl.ds(pl.multiple_of(base + chunk * tile, tile), tile)
            for row in range(part_rows):
                if k == 0:
                    values = tile_at(start_ref, rows, place * part_rows + row, chunk)
                else:
                    values = (rim_ref if k in late else piece_refs[k])[row * chunks + chunk]
                field[row + 1, part, :] = values
                edge[row + 1, part, :] = unpack_edges(
                    rim_ref[at + 2 * chunks], row * chunks + chunk
                )
            field[0, part, :] = rim_ref[at + chunk]
            field[part_rows + 1, part, :] = rim_ref[at + chunks + chunk]
            edge[0, part, :] = unpack_edges(
                rim_ref[at + 2 * chunks + 1], (part_rows - 1) * chunks + chunk
            )
            edge[part_rows + 1, part, :] = unpack_edges(rim_ref[at + 2 * chunks + 2], chunk)

    def sides(main, other):
        return pltpu.roll(jnp.where(last_lane, other, main), 1, 1) + pltpu.roll(
            jnp.where(first_lane, other, main), lanes - 1, 1
        )

    def factor_at(ref, row):
        return jnp.broadcast_to(ref[pl.ds(row, 1), :], (total, lanes))

    base = place * part_rows
    for row in range(-1, part_rows + 1):
        here, beside = field[row + 1], edge[row + 1]
        even = even_lane if row % 2 == 0 else jnp.logical_not(even_lane)
        if row == -1:
            vertical = field[1]
        elif row == part_rows:
            vertical = field[part_rows]
        else:
            vertical = jnp.where(even, field[row + 2], field[row])
        once[row + 1] = factor_at(factor, tile + base + row) * here - inverse * (
            sides(here, beside) + vertical
        )
        if 0 <= row < part_rows:
            vertical = jnp.where(even, edge[row + 2], edge[row])
            once_edge[row] = factor_at(factor_edge, base + row) * beside - inverse * (
                sides(beside, here) + vertical
            )
    products = jnp.zeros((3 * total, 3 * total), jnp.float32)
    for row in range(part_rows):
        here = once[row + 1]
        even = even_lane if row % 2 == 0 else jnp.logical_not(even_lane)
        vertical = jnp.where(even, once[row + 2], once[row])
        twice = factor_at(factor, tile + base + row) * here - inverse * (
            sides(here, once_edge[row]) + vertical
        )
        whole_ref[row] = 2.0 * twice - field[row + 1]
        if row % 2:
            values = jnp.concatenate([whole_ref[row - 1], whole_ref[row]], axis=1)
            stack = jnp.concatenate(split(values), axis=0)
            products += lax.dot_general(
                stack, stack, (((1,), (1,)), ((), ())), preferred_element_type=jnp.float32
            )
    gram = jnp.zeros((total, total), jnp.float32)
    for i in reversed(range(3)):
        for j in reversed(range(3)):
            gram += products[i * total : (i + 1) * total, j * total : (j + 1) * total]
    half = total // 2
    gram_ref[...] = jnp.concatenate([gram[:half], gram[half:]], axis=1)


def split(values):
    high = values.astype(jnp.bfloat16)
    rest = values - high.astype(jnp.float32)
    middle = rest.astype(jnp.bfloat16)
    low = (rest - middle.astype(jnp.float32)).astype(jnp.bfloat16)
    return high, middle, low


def solve_kernel(scale, whole_ref, gram_ref, other_ref, out_ref):
    part_rows, total, _ = whole_ref.shape
    blocks = total // tile
    half = total // 2
    packed = gram_ref[...] + other_ref[...]
    lane = iota((tile, lanes), 1)
    sub = iota((tile, lanes), 0)
    shape = (tile, lanes)
    work = []
    for i in range(blocks):
        at = i * tile % half
        block = packed[at : at + tile, :]
        if i * tile >= half:
            block = pltpu.roll(block, total, 1)
        unit = jnp.where(lane - total == sub + i * tile, 1.0, 0.0)
        work.append(jnp.where(lane < total, block, unit))
    for b in range(blocks):
        column = {
            i: [
                jnp.broadcast_to(work[i][:, b * tile + m : b * tile + m + 1], shape)
                for m in range(tile)
            ]
            for i in range(b, blocks)
        }
        for m in range(tile):
            pivot = jnp.broadcast_to(column[b][m][m : m + 1, :], shape)
            root = lax.rsqrt(pivot)
            root = root * (1.5 - 0.5 * (pivot * root) * root)
            row = jnp.broadcast_to(work[b][m : m + 1, :], shape) * root
            heads = [
                jnp.broadcast_to(column[b][p][m : m + 1, :], shape) * root
                for p in range(m + 1, tile)
            ]
            for i in range(b, blocks):
                ratio = column[i][m] * root
                if i == b:
                    ratio = jnp.where(sub > m, ratio, 0.0)
                    work[i] = jnp.where(sub == m, row, work[i] - ratio * row)
                else:
                    work[i] = work[i] - ratio * row
                for p in range(m + 1, tile):
                    column[i][p] = column[i][p] - ratio * heads[p - m - 1]
    solver = jnp.concatenate(work, axis=0) * scale
    wide = iota((total, lanes), 1)
    high, middle, low = (piece.astype(jnp.float32) for piece in split(solver))

    def pair(left, right):
        return jnp.where(wide < total, pltpu.roll(left, total, 1), right).astype(jnp.bfloat16)

    left_main = jnp.concatenate([pair(high, high), pair(middle, middle)], axis=1)
    left_rest = pair(high, low)
    for row in range(0, part_rows, 2):
        values = jnp.concatenate([whole_ref[row], whole_ref[row + 1]], axis=1)
        f_high, f_middle, f_low = split(values)
        right_main = jnp.concatenate([f_high, f_middle, f_high, f_middle], axis=0)
        right_rest = jnp.concatenate([f_low, f_high], axis=0)
        result = jnp.dot(left_rest, right_rest, preferred_element_type=jnp.float32) + jnp.dot(
            left_main, right_main, preferred_element_type=jnp.float32
        )
        out_ref[pl.ds(row, total, stride=part_rows), :] = result[:, :lanes]
        out_ref[pl.ds(row + 1, total, stride=part_rows), :] = result[:, lanes:]


def call(kernel, outs, *operands, scratch=()):
    return pl.pallas_call(
        kernel,
        out_shape=[jax.ShapeDtypeStruct(shape, jnp.float32) for shape in outs],
        scratch_shapes=[pltpu.VMEM(shape, jnp.float32) for shape in scratch],
        compiler_params=pltpu.CompilerParams(vmem_limit_bytes=32 * 1024 * 1024),
    )(*operands)


def exchange(values, axis, distance):
    count = lax.axis_size(axis)
    return lax.ppermute(values, axis, [(i, i ^ distance) for i in range(count)])


def sending_order(parts):
    if parts == 4:
        return (2,), (3,), (1,)
    far = tuple(k for k in range(parts // 2, parts))
    return far, tuple(k for k in range(2, parts // 2)), (1,)


def shards(start, levels):
    cols, rows, _ = start.shape
    parts = lax.axis_size("col")
    chunks = cols // tile
    total = cols * parts
    part_rows = rows // parts
    sizes = (cols, rows, parts)
    first, second, late = sending_order(parts)
    flat = start.reshape(cols * rows, lanes)
    piece = (part_rows * chunks, tile, lanes)
    edges, outer, *firsts = call(
        functools.partial(pack_kernel, *sizes, first),
        [(parts + 1, tile, lanes), (2 * chunks + 1, tile, lanes)] + [piece] * len(first),
        flat,
        levels,
    )
    arrived = {}
    count = lax.axis_size("ly")
    near = exchange(edges, "ly", 1)
    far_pairs = [(i, (i + 1) % count if i % 2 else (i - 1) % count) for i in range(count)]
    far = lax.ppermute(edges, "ly", far_pairs)
    for k, values in zip(first, firsts):
        arrived[k] = exchange(values, "col", k)
    beside, outer, *seconds = call(
        functools.partial(outer_kernel, *sizes, second),
        [(parts + 1, tile, lanes), (2 * chunks + 3, tile, lanes)] + [piece] * len(second),
        flat,
        outer,
        near,
        far,
    )
    count = lax.axis_size("lx")
    before = lax.ppermute(outer, "lx", [(i, (i + 1) % count) for i in range(count)])
    after = before
    if count > 2:
        after = lax.ppermute(outer, "lx", [((i + 1) % count, i) for i in range(count)])
    for k, values in zip(second, seconds):
        arrived[k] = exchange(values, "col", k)
    rims = call(
        functools.partial(rim_kernel, *sizes, late),
        [
            (2 * chunks + 3 + (part_rows * chunks if k in late else 0), tile, lanes)
            for k in range(parts)
        ],
        flat,
        beside,
        before,
        after,
    )
    rims = [exchange(values, "col", k) if k else values for k, values in enumerate(rims)]
    whole, gram = call(
        functools.partial(filter_kernel, *sizes, late),
        [(part_rows, total, lanes), (total // 2, 2 * total)],
        flat,
        levels,
        beside,
        before,
        after,
        *rims,
        *(arrived[k] for k in sorted(arrived)),
        scratch=[
            (part_rows + 2, total, lanes),
            (part_rows + 2, total, lanes),
            (part_rows + 2, total, lanes),
            (part_rows, total, lanes),
            (rows + 2 * tile, lanes),
            (rows, lanes),
        ],
    )
    steps = []
    for axis in ("ly", "lx", "col"):
        bit = 1
        while bit < lax.axis_size(axis):
            steps.append((axis, bit))
            bit *= 2
    for axis, bit in steps[:-1]:
        gram = gram + exchange(gram, axis, bit)
    scale = math.sqrt(rows * lax.axis_size("lx") * lanes * lax.axis_size("ly"))
    (basis,) = call(
        functools.partial(solve_kernel, scale),
        [(total * part_rows, lanes)],
        whole,
        gram,
        exchange(gram, *steps[-1]),
    )
    return basis.reshape(total, part_rows, lanes)


def solution(mesh):
    placed = (P("col", "lx", "ly"), P("lx", "ly"))
    return jax.shard_map(
        shards, mesh=mesh, in_specs=placed, out_specs=P(None, ("lx", "col"), "ly"), check_vma=False
    )
```

```python
import functools
import math

import jax
import jax.numpy as jnp
from jax import lax
from jax.experimental import pallas as pl
from jax.experimental.pallas import tpu as pltpu
from jax.sharding import PartitionSpec as P

center = 2.1
half_width = 3.1
spread_width = 4.0
level_top = 15.0
lanes = 128
tile = 8


def iota(shape, dim):
    return lax.broadcasted_iota(jnp.int32, shape, dim)


def site_factor(levels):
    onsite = spread_width * (levels / level_top - 0.5)
    return (onsite - center) / half_width


def tile_at(ref, rows, row, chunk):
    return ref[pl.ds(chunk * tile * rows + row, tile, stride=rows), :]


def pack_edges(tiles):
    lane = iota((tile, lanes), 1)
    packed = jnp.zeros((tile, lanes), jnp.float32)
    for k, values in enumerate(tiles):
        moved = pltpu.roll(values, (4 * k + 2) % lanes, 1)
        packed = jnp.where(lane // 4 == k, moved, packed)
    return packed


def unpack_edges(packed, k):
    return pltpu.roll(packed, lanes - (4 * k + 2), 1)


def pack_kernel(cols, rows, parts, early, start_ref, levels_ref, edges_ref, outer_ref, *piece_refs):
    chunks = cols // tile
    part_rows = rows // parts
    for group in range(parts):
        edges_ref[group] = pack_edges(
            tile_at(start_ref, rows, group * part_rows + row, chunk)
            for row in range(part_rows)
            for chunk in range(chunks)
        )
    edges_ref[parts] = pack_edges(
        levels_ref[k * tile : (k + 1) * tile, :].astype(jnp.float32) for k in range(rows // tile)
    )
    for chunk in range(chunks):
        outer_ref[chunk] = tile_at(start_ref, rows, 0, chunk)
        outer_ref[chunks + chunk] = tile_at(start_ref, rows, rows - 1, chunk)
    first = levels_ref[0:1, :].astype(jnp.float32)
    last = levels_ref[rows - 1 : rows, :].astype(jnp.float32)
    outer_ref[2 * chunks] = jnp.where(iota((tile, lanes), 0) == 0, first, last)
    for k, piece_ref in zip(early, piece_refs):
        copy_piece(cols, rows, parts, k, start_ref, piece_ref)


def copy_piece(cols, rows, parts, k, start_ref, piece_ref):
    chunks = cols // tile
    part_rows = rows // parts
    base = (lax.axis_index("col") ^ k) * part_rows
    for row in range(part_rows):
        for chunk in range(chunks):
            piece_ref[row, chunk * tile : (chunk + 1) * tile, :] = tile_at(
                start_ref, rows, base + row, chunk
            )


def outer_kernel(parts, outer_ref, near_ref, far_ref, beside_ref, send_ref):
    from_left = iota((tile, lanes), 1) % 4 < 2
    even_place = lax.axis_index("ly") % 2 == 0
    for group in range(parts + 1):
        near, far = near_ref[group], far_ref[group]
        beside_ref[group] = jnp.where(
            even_place, jnp.where(from_left, far, near), jnp.where(from_left, near, far)
        )
    count = outer_ref.shape[0]
    send_ref[:count] = outer_ref[...]
    send_ref[count] = beside_ref[0]
    send_ref[count + 1] = beside_ref[parts - 1]


inverse = 1.0 / half_width


def sides(main, other):
    lane = iota(main.shape, 1)
    return pltpu.roll(jnp.where(lane == lanes - 1, other, main), 1, 1) + pltpu.roll(
        jnp.where(lane == 0, other, main), lanes - 1, 1
    )


def upward(row, above, below):
    even = iota(above.shape, 1) % 2 == row % 2
    return jnp.where(even, above, below)


def factor_at(ref, row, height):
    return jnp.broadcast_to(ref[pl.ds(row, 1), :], (height, lanes))


def filter_kernel(
    cols, rows, parts, early, start_ref, levels_ref, beside_ref, before_ref, after_ref, *refs
):
    out_refs, (field, edge, once, once_edge, done, factor, factor_edge) = refs[:parts], refs[parts:]
    chunks = cols // tile
    part_rows = rows // parts
    factor[0:rows, :] = site_factor(levels_ref[...].astype(jnp.float32))
    factor[rows : rows + 1, :] = site_factor(before_ref[2 * chunks, 1:2, :])
    factor[rows + 1 : rows + 2, :] = site_factor(after_ref[2 * chunks, 0:1, :])
    for k in range(rows // tile):
        factor_edge[k * tile : (k + 1) * tile, :] = site_factor(unpack_edges(beside_ref[parts], k))
    for chunk in range(chunks):
        part = pl.ds(chunk * tile, tile)
        for row in range(rows):
            field[row + 1, part, :] = tile_at(start_ref, rows, row, chunk)
            edge[row + 1, part, :] = unpack_edges(
                beside_ref[row // part_rows], row % part_rows * chunks + chunk
            )
        field[0, part, :] = before_ref[chunks + chunk]
        field[rows + 1, part, :] = after_ref[chunk]
        edge[0, part, :] = unpack_edges(
            before_ref[2 * chunks + 2], (part_rows - 1) * chunks + chunk
        )
        edge[rows + 1, part, :] = unpack_edges(after_ref[2 * chunks + 1], chunk)
    for row in range(-1, rows + 1):
        here, beside = field[row + 1], edge[row + 1]
        if row == -1:
            vertical, where = field[1], rows
        elif row == rows:
            vertical, where = field[rows], rows + 1
        else:
            vertical, where = upward(row, field[row + 2], field[row]), row
        once[row + 1] = factor_at(factor, where, cols) * here - inverse * (
            sides(here, beside) + vertical
        )
        if 0 <= row < rows:
            vertical = upward(row, edge[row + 2], edge[row])
            once_edge[row] = factor_at(factor_edge, row, cols) * beside - inverse * (
                sides(beside, here) + vertical
            )
    for row in range(rows):
        here = once[row + 1]
        twice = factor_at(factor, row, cols) * here - inverse * (
            sides(here, once_edge[row]) + upward(row, once[row + 2], once[row])
        )
        done[row] = 2.0 * twice - field[row + 1]
    for k, out_ref in enumerate(out_refs):
        base = (lax.axis_index("col") ^ k) * part_rows
        if k not in early:
            out_ref[...] = done[pl.ds(base, part_rows)]
            continue
        for chunk in range(chunks):
            part = pl.ds(chunk * tile, tile)
            out_ref[chunk] = done[base, part, :]
            out_ref[chunks + chunk] = done[base + part_rows - 1, part, :]
        out_ref[2 * chunks] = pack_edges(
            done[base + row, chunk * tile : (chunk + 1) * tile, :]
            for row in range(part_rows)
            for chunk in range(chunks)
        )


def gram_kernel(cols, parts, early, levels_ref, *refs):
    late_refs, refs = refs[:parts], refs[parts:]
    raw_refs = dict(zip(early, refs))
    whole_ref, gram_ref, once, factor = refs[len(early) :]
    chunks = cols // tile
    part_rows = whole_ref.shape[0]
    total = cols * parts
    place = lax.axis_index("col")
    factor[...] = site_factor(levels_ref[...].astype(jnp.float32))
    lane = iota((cols, lanes), 1)
    outer_lanes = (lane < 2) | (lane >= lanes - 2)
    for k in range(parts):
        part = pl.ds(pl.multiple_of((place ^ k) * cols, tile), cols)
        late_ref = late_refs[k]
        if k not in early:
            whole_ref[:, part, :] = late_ref[...]
            continue
        raw_ref = raw_refs[k]
        base = place * part_rows
        for row in range(part_rows):
            above, below = raw_ref[min(row + 1, part_rows - 1)], raw_ref[max(row - 1, 0)]
            here = raw_ref[row]
            once[row] = factor_at(factor, base + row, cols) * here - inverse * (
                sides(here, here) + upward(row, above, below)
            )
        packed = late_ref[2 * chunks]
        for row in range(part_rows):
            if row in (0, part_rows - 1):
                at = 0 if row == 0 else chunks
                whole_ref[row, part, :] = jnp.concatenate(
                    [late_ref[at + chunk] for chunk in range(chunks)], axis=0
                )
                continue
            here = once[row]
            twice = factor_at(factor, base + row, cols) * here - inverse * (
                sides(here, here) + upward(row, once[row + 1], once[row - 1])
            )
            sent = jnp.concatenate(
                [unpack_edges(packed, row * chunks + chunk) for chunk in range(chunks)], axis=0
            )
            whole_ref[row, part, :] = jnp.where(outer_lanes, sent, 2.0 * twice - raw_ref[row])
    products = jnp.zeros((3 * total, 3 * total), jnp.float32)
    for row in range(0, part_rows, 2):
        values = jnp.concatenate([whole_ref[row], whole_ref[row + 1]], axis=1)
        stack = jnp.concatenate(split(values), axis=0)
        products += lax.dot_general(
            stack, stack, (((1,), (1,)), ((), ())), preferred_element_type=jnp.float32
        )
    gram = jnp.zeros((total, total), jnp.float32)
    for i in reversed(range(3)):
        for j in reversed(range(3)):
            gram += products[i * total : (i + 1) * total, j * total : (j + 1) * total]
    half = total // 2
    gram_ref[...] = jnp.concatenate([gram[:half], gram[half:]], axis=1)


def split(values):
    high = values.astype(jnp.bfloat16)
    rest = values - high.astype(jnp.float32)
    middle = rest.astype(jnp.bfloat16)
    low = (rest - middle.astype(jnp.float32)).astype(jnp.bfloat16)
    return high, middle, low


def solve_kernel(scale, whole_ref, gram_ref, other_ref, out_ref):
    part_rows, total, _ = whole_ref.shape
    blocks = total // tile
    half = total // 2
    packed = gram_ref[...] + other_ref[...]
    lane = iota((tile, lanes), 1)
    sub = iota((tile, lanes), 0)
    shape = (tile, lanes)
    work = []
    for i in range(blocks):
        at = i * tile % half
        block = packed[at : at + tile, :]
        if i * tile >= half:
            block = pltpu.roll(block, total, 1)
        unit = jnp.where(lane - total == sub + i * tile, 1.0, 0.0)
        work.append(jnp.where(lane < total, block, unit))
    for b in range(blocks):
        column = {
            i: [
                jnp.broadcast_to(work[i][:, b * tile + m : b * tile + m + 1], shape)
                for m in range(tile)
            ]
            for i in range(b, blocks)
        }
        for m in range(tile):
            pivot = jnp.broadcast_to(column[b][m][m : m + 1, :], shape)
            root = lax.rsqrt(pivot)
            root = root * (1.5 - 0.5 * (pivot * root) * root)
            row = jnp.broadcast_to(work[b][m : m + 1, :], shape) * root
            heads = [
                jnp.broadcast_to(column[b][p][m : m + 1, :], shape) * root
                for p in range(m + 1, tile)
            ]
            for i in range(b, blocks):
                ratio = column[i][m] * root
                if i == b:
                    ratio = jnp.where(sub > m, ratio, 0.0)
                    work[i] = jnp.where(sub == m, row, work[i] - ratio * row)
                else:
                    work[i] = work[i] - ratio * row
                for p in range(m + 1, tile):
                    column[i][p] = column[i][p] - ratio * heads[p - m - 1]
    solver = jnp.concatenate(work, axis=0) * scale
    wide = iota((total, lanes), 1)
    high, middle, low = (piece.astype(jnp.float32) for piece in split(solver))

    def pair(left, right):
        return jnp.where(wide < total, pltpu.roll(left, total, 1), right).astype(jnp.bfloat16)

    left_main = jnp.concatenate([pair(high, high), pair(middle, middle)], axis=1)
    left_rest = pair(high, low)
    for row in range(0, part_rows, 2):
        values = jnp.concatenate([whole_ref[row], whole_ref[row + 1]], axis=1)
        f_high, f_middle, f_low = split(values)
        right_main = jnp.concatenate([f_high, f_middle, f_high, f_middle], axis=0)
        right_rest = jnp.concatenate([f_low, f_high], axis=0)
        result = jnp.dot(left_rest, right_rest, preferred_element_type=jnp.float32) + jnp.dot(
            left_main, right_main, preferred_element_type=jnp.float32
        )
        out_ref[pl.ds(row, total, stride=part_rows), :] = result[:, :lanes]
        out_ref[pl.ds(row + 1, total, stride=part_rows), :] = result[:, lanes:]


def call(kernel, outs, *operands, scratch=()):
    return pl.pallas_call(
        kernel,
        out_shape=[jax.ShapeDtypeStruct(shape, jnp.float32) for shape in outs],
        scratch_shapes=[pltpu.VMEM(shape, jnp.float32) for shape in scratch],
        compiler_params=pltpu.CompilerParams(vmem_limit_bytes=32 * 1024 * 1024),
    )(*operands)


def exchange(values, axis, distance):
    count = lax.axis_size(axis)
    return lax.ppermute(values, axis, [(i, i ^ distance) for i in range(count)])


def shards(start, levels):
    cols, rows, _ = start.shape
    parts = lax.axis_size("col")
    chunks = cols // tile
    total = cols * parts
    part_rows = rows // parts
    sizes = (cols, rows, parts)
    early = (parts // 2,)
    flat = start.reshape(cols * rows, lanes)
    piece = (part_rows, cols, lanes)
    edges, outer, *raws = call(
        functools.partial(pack_kernel, *sizes, early),
        [(parts + 1, tile, lanes), (2 * chunks + 1, tile, lanes)] + [piece] * len(early),
        flat,
        levels,
    )
    count = lax.axis_size("ly")
    near = exchange(edges, "ly", 1)
    far_pairs = [(i, (i + 1) % count if i % 2 else (i - 1) % count) for i in range(count)]
    far = lax.ppermute(edges, "ly", far_pairs)
    raws = [exchange(values, "col", k) for k, values in zip(early, raws)]
    beside, outer = call(
        functools.partial(outer_kernel, parts),
        [(parts + 1, tile, lanes), (2 * chunks + 3, tile, lanes)],
        outer,
        near,
        far,
    )
    count = lax.axis_size("lx")
    before = lax.ppermute(outer, "lx", [(i, (i + 1) % count) for i in range(count)])
    after = before
    if count > 2:
        after = lax.ppermute(outer, "lx", [((i + 1) % count, i) for i in range(count)])
    lates = call(
        functools.partial(filter_kernel, *sizes, early),
        [(2 * chunks + 1, tile, lanes) if k in early else piece for k in range(parts)],
        flat,
        levels,
        beside,
        before,
        after,
        scratch=[
            (rows + 2, cols, lanes),
            (rows + 2, cols, lanes),
            (rows + 2, cols, lanes),
            (rows, cols, lanes),
            (rows, cols, lanes),
            (rows + tile, lanes),
            (rows, lanes),
        ],
    )
    lates = [exchange(values, "col", k) if k else values for k, values in enumerate(lates)]
    whole, gram = call(
        functools.partial(gram_kernel, cols, parts, early),
        [(part_rows, total, lanes), (total // 2, 2 * total)],
        levels,
        *lates,
        *raws,
        scratch=[piece, (rows, lanes)],
    )
    steps = []
    for axis in ("ly", "lx", "col"):
        bit = 1
        while bit < lax.axis_size(axis):
            steps.append((axis, bit))
            bit *= 2
    for axis, bit in steps[:-1]:
        gram = gram + exchange(gram, axis, bit)
    scale = math.sqrt(rows * lax.axis_size("lx") * lanes * lax.axis_size("ly"))
    (basis,) = call(
        functools.partial(solve_kernel, scale),
        [(total * part_rows, lanes)],
        whole,
        gram,
        exchange(gram, *steps[-1]),
    )
    return basis.reshape(total, part_rows, lanes)


def solution(mesh):
    placed = (P("col", "lx", "ly"), P("lx", "ly"))
    return jax.shard_map(
        shards, mesh=mesh, in_specs=placed, out_specs=P(None, ("lx", "col"), "ly"), check_vma=False
    )
```

```python
import functools
import math

import jax
import jax.numpy as jnp
from jax import lax
from jax.experimental import pallas as pl
from jax.experimental.pallas import tpu as pltpu
from jax.sharding import PartitionSpec as P

center = 2.1
half_width = 3.1
spread_width = 4.0
level_top = 15.0
lanes = 128
tile = 8


def iota(shape, dim):
    return lax.broadcasted_iota(jnp.int32, shape, dim)


def site_factor(levels):
    onsite = spread_width * (levels / level_top - 0.5)
    return (onsite - center) / half_width


def tile_at(ref, rows, row, chunk):
    return ref[pl.ds(chunk * tile * rows + row, tile, stride=rows), :]


def pack_edges(tiles):
    lane = iota((tile, lanes), 1)
    packed = jnp.zeros((tile, lanes), jnp.float32)
    for k, values in enumerate(tiles):
        moved = pltpu.roll(values, (4 * k + 2) % lanes, 1)
        packed = jnp.where(lane // 4 == k, moved, packed)
    return packed


def unpack_edges(packed, k):
    return pltpu.roll(packed, lanes - (4 * k + 2), 1)


def pack_kernel(cols, rows, parts, early, start_hbm, levels_hbm, edges_ref, outer_ref, *refs):
    piece_refs, (start_ref, levels_ref, arrived) = refs[: len(early)], refs[len(early) :]
    chunks = cols // tile
    part_rows = rows // parts
    copies = [
        pltpu.make_async_copy(start_hbm, start_ref, arrived.at[0]),
        pltpu.make_async_copy(levels_hbm, levels_ref, arrived.at[1]),
    ]
    for copy in copies:
        copy.start()
    for copy in copies:
        copy.wait()
    for group in range(parts):
        edges_ref[group] = pack_edges(
            tile_at(start_ref, rows, group * part_rows + row, chunk)
            for row in range(part_rows)
            for chunk in range(chunks)
        )
    edges_ref[parts] = pack_edges(
        levels_ref[k * tile : (k + 1) * tile, :].astype(jnp.float32) for k in range(rows // tile)
    )
    for chunk in range(chunks):
        outer_ref[chunk] = tile_at(start_ref, rows, 0, chunk)
        outer_ref[chunks + chunk] = tile_at(start_ref, rows, rows - 1, chunk)
    first = levels_ref[0:1, :].astype(jnp.float32)
    last = levels_ref[rows - 1 : rows, :].astype(jnp.float32)
    outer_ref[2 * chunks] = jnp.where(iota((tile, lanes), 0) == 0, first, last)
    for k, piece_ref in zip(early, piece_refs):
        copy_piece(cols, rows, parts, k, start_ref, piece_ref)


def copy_piece(cols, rows, parts, k, start_ref, piece_ref):
    chunks = cols // tile
    part_rows = rows // parts
    base = (lax.axis_index("col") ^ k) * part_rows
    for row in range(part_rows):
        for chunk in range(chunks):
            piece_ref[row, chunk * tile : (chunk + 1) * tile, :] = tile_at(
                start_ref, rows, base + row, chunk
            )


def outer_kernel(parts, outer_ref, near_ref, far_ref, beside_ref, send_ref):
    from_left = iota((tile, lanes), 1) % 4 < 2
    even_place = lax.axis_index("ly") % 2 == 0
    for group in range(parts + 1):
        near, far = near_ref[group], far_ref[group]
        beside_ref[group] = jnp.where(
            even_place, jnp.where(from_left, far, near), jnp.where(from_left, near, far)
        )
    count = outer_ref.shape[0]
    send_ref[:count] = outer_ref[...]
    send_ref[count] = beside_ref[0]
    send_ref[count + 1] = beside_ref[parts - 1]


inverse = 1.0 / half_width


def sides(main, other):
    lane = iota(main.shape, 1)
    return pltpu.roll(jnp.where(lane == lanes - 1, other, main), 1, 1) + pltpu.roll(
        jnp.where(lane == 0, other, main), lanes - 1, 1
    )


def upward(row, above, below):
    even = iota(above.shape, 1) % 2 == row % 2
    return jnp.where(even, above, below)


def factor_at(ref, row, height):
    return jnp.broadcast_to(ref[pl.ds(row, 1), :], (height, lanes))


def inner_kernel(
    cols, rows, parts, early, start_ref, levels_ref, beside_ref, done_ref, next_ref, packed_ref, *refs
):
    field, edge, once, once_edge, factor, factor_edge = refs
    chunks = cols // tile
    part_rows = rows // parts
    factor[...] = site_factor(levels_ref[...].astype(jnp.float32))
    for k in range(rows // tile):
        factor_edge[k * tile : (k + 1) * tile, :] = site_factor(unpack_edges(beside_ref[parts], k))
    for row in range(rows):
        for chunk in range(chunks):
            part = pl.ds(chunk * tile, tile)
            field[row, part, :] = tile_at(start_ref, rows, row, chunk)
            edge[row, part, :] = unpack_edges(
                beside_ref[row // part_rows], row % part_rows * chunks + chunk
            )
    for row in range(rows):
        here, beside = field[row], edge[row]
        up, down = min(row + 1, rows - 1), max(row - 1, 0)
        once[row] = factor_at(factor, row, cols) * here - inverse * (
            sides(here, beside) + upward(row, field[up], field[down])
        )
        once_edge[row] = factor_at(factor_edge, row, cols) * beside - inverse * (
            sides(beside, here) + upward(row, edge[up], edge[down])
        )
    for row in range(1, rows - 1):
        here = once[row]
        twice = factor_at(factor, row, cols) * here - inverse * (
            sides(here, once_edge[row]) + upward(row, once[row + 1], once[row - 1])
        )
        done_ref[row] = 2.0 * twice - field[row]
    done_ref[0] = once[0]
    done_ref[rows - 1] = once[rows - 1]
    next_ref[0] = once[1]
    next_ref[1] = once[rows - 2]
    for at, k in enumerate(early):
        base = (lax.axis_index("col") ^ k) * part_rows
        packed_ref[at] = pack_edges(
            done_ref[base + row, chunk * tile : (chunk + 1) * tile, :]
            for row in range(part_rows)
            for chunk in range(chunks)
        )


def outer_rows(cols, rows, start_ref, levels_ref, beside_ref, parts, before_ref, after_ref, next_ref):
    chunks = cols // tile
    part_rows = rows // parts

    def joined(tiles):
        return jnp.concatenate(list(tiles), axis=0)

    def field(row):
        return joined(tile_at(start_ref, rows, row, chunk) for chunk in range(chunks))

    def edge(row):
        return joined(
            unpack_edges(beside_ref[row // part_rows], row % part_rows * chunks + chunk)
            for chunk in range(chunks)
        )

    def factor(values):
        return jnp.broadcast_to(site_factor(values), (cols, lanes))

    for outer in (0, 1):
        if outer == 0:
            row, inside = 0, 1
            field_out = joined(before_ref[chunks + chunk] for chunk in range(chunks))
            edge_out = joined(
                unpack_edges(before_ref[2 * chunks + 2], (part_rows - 1) * chunks + chunk)
                for chunk in range(chunks)
            )
            factor_out = factor(before_ref[2 * chunks, 1:2, :])
        else:
            row, inside = rows - 1, rows - 2
            field_out = joined(after_ref[chunk] for chunk in range(chunks))
            edge_out = joined(
                unpack_edges(after_ref[2 * chunks + 1], chunk) for chunk in range(chunks)
            )
            factor_out = factor(after_ref[2 * chunks, 0:1, :])

        def vertical(within, without):
            return upward(row, *((within, without) if outer == 0 else (without, within)))

        here, beside = field(row), edge(row)
        here_factor = factor(levels_ref[row : row + 1, :].astype(jnp.float32))
        levels_edge = unpack_edges(beside_ref[parts], row // tile)
        edge_factor = factor(levels_edge[row % tile : row % tile + 1, :])
        once = here_factor * here - inverse * (
            sides(here, beside) + vertical(field(inside), field_out)
        )
        once_edge = edge_factor * beside - inverse * (
            sides(beside, here) + vertical(edge(inside), edge_out)
        )
        once_out = factor_out * field_out - inverse * (sides(field_out, edge_out) + here)
        twice = here_factor * once - inverse * (
            sides(once, once_edge) + vertical(next_ref[outer], once_out)
        )
        yield 2.0 * twice - here


def late_kernel(
    cols,
    rows,
    parts,
    early,
    start_ref,
    levels_ref,
    beside_ref,
    done_ref,
    next_ref,
    packed_ref,
    before_ref,
    after_ref,
    *out_refs,
):
    chunks = cols // tile
    part_rows = rows // parts
    first, last = outer_rows(
        cols, rows, start_ref, levels_ref, beside_ref, parts, before_ref, after_ref, next_ref
    )
    for k, out_ref in enumerate(out_refs):
        target = lax.axis_index("col") ^ k
        base = target * part_rows
        top = jnp.where(target == 0, first, done_ref[base])
        bottom = jnp.where(target == parts - 1, last, done_ref[base + part_rows - 1])
        if k not in early:
            out_ref[0] = top
            out_ref[1 : part_rows - 1] = done_ref[pl.ds(base + 1, part_rows - 2)]
            out_ref[part_rows - 1] = bottom
            continue
        for chunk in range(chunks):
            part = slice(chunk * tile, (chunk + 1) * tile)
            out_ref[chunk] = top[part]
            out_ref[chunks + chunk] = bottom[part]
        out_ref[2 * chunks] = packed_ref[early.index(k)]


def gram_kernel(cols, parts, early, levels_ref, *refs):
    late_refs, refs = refs[:parts], refs[parts:]
    raw_refs = dict(zip(early, refs))
    whole_ref, gram_ref, once, factor = refs[len(early) :]
    chunks = cols // tile
    part_rows = whole_ref.shape[0]
    total = cols * parts
    place = lax.axis_index("col")
    factor[...] = site_factor(levels_ref[...].astype(jnp.float32))
    lane = iota((cols, lanes), 1)
    outer_lanes = (lane < 2) | (lane >= lanes - 2)
    for k in range(parts):
        part = pl.ds(pl.multiple_of((place ^ k) * cols, tile), cols)
        late_ref = late_refs[k]
        if k not in early:
            whole_ref[:, part, :] = late_ref[...]
            continue
        raw_ref = raw_refs[k]
        base = place * part_rows
        for row in range(part_rows):
            above, below = raw_ref[min(row + 1, part_rows - 1)], raw_ref[max(row - 1, 0)]
            here = raw_ref[row]
            once[row] = factor_at(factor, base + row, cols) * here - inverse * (
                sides(here, here) + upward(row, above, below)
            )
        packed = late_ref[2 * chunks]
        for row in range(part_rows):
            if row in (0, part_rows - 1):
                at = 0 if row == 0 else chunks
                whole_ref[row, part, :] = jnp.concatenate(
                    [late_ref[at + chunk] for chunk in range(chunks)], axis=0
                )
                continue
            here = once[row]
            twice = factor_at(factor, base + row, cols) * here - inverse * (
                sides(here, here) + upward(row, once[row + 1], once[row - 1])
            )
            sent = jnp.concatenate(
                [unpack_edges(packed, row * chunks + chunk) for chunk in range(chunks)], axis=0
            )
            whole_ref[row, part, :] = jnp.where(outer_lanes, sent, 2.0 * twice - raw_ref[row])
    products = jnp.zeros((3 * total, 3 * total), jnp.float32)
    for row in range(0, part_rows, 2):
        values = jnp.concatenate([whole_ref[row], whole_ref[row + 1]], axis=1)
        stack = jnp.concatenate(split(values), axis=0)
        products += lax.dot_general(
            stack, stack, (((1,), (1,)), ((), ())), preferred_element_type=jnp.float32
        )
    gram = jnp.zeros((total, total), jnp.float32)
    for i in reversed(range(3)):
        for j in reversed(range(3)):
            gram += products[i * total : (i + 1) * total, j * total : (j + 1) * total]
    half = total // 2
    gram_ref[...] = jnp.concatenate([gram[:half], gram[half:]], axis=1)


def split(values):
    high = values.astype(jnp.bfloat16)
    rest = values - high.astype(jnp.float32)
    middle = rest.astype(jnp.bfloat16)
    low = (rest - middle.astype(jnp.float32)).astype(jnp.bfloat16)
    return high, middle, low


def solve_kernel(scale, whole_ref, gram_ref, other_ref, out_ref):
    part_rows, total, _ = whole_ref.shape
    blocks = total // tile
    half = total // 2
    packed = gram_ref[...] + other_ref[...]
    lane = iota((tile, lanes), 1)
    sub = iota((tile, lanes), 0)
    shape = (tile, lanes)
    work = []
    for i in range(blocks):
        at = i * tile % half
        block = packed[at : at + tile, :]
        if i * tile >= half:
            block = pltpu.roll(block, total, 1)
        unit = jnp.where(lane - total == sub + i * tile, 1.0, 0.0)
        work.append(jnp.where(lane < total, block, unit))
    for b in range(blocks):
        column = {
            i: [
                jnp.broadcast_to(work[i][:, b * tile + m : b * tile + m + 1], shape)
                for m in range(tile)
            ]
            for i in range(b, blocks)
        }
        for m in range(tile):
            pivot = jnp.broadcast_to(column[b][m][m : m + 1, :], shape)
            root = lax.rsqrt(pivot)
            row = jnp.broadcast_to(work[b][m : m + 1, :], shape) * root
            heads = [
                jnp.broadcast_to(column[b][p][m : m + 1, :], shape) * root
                for p in range(m + 1, tile)
            ]
            for i in range(b, blocks):
                ratio = column[i][m] * root
                if i == b:
                    ratio = jnp.where(sub > m, ratio, 0.0)
                    work[i] = jnp.where(sub == m, row, work[i] - ratio * row)
                else:
                    work[i] = work[i] - ratio * row
                for p in range(m + 1, tile):
                    column[i][p] = column[i][p] - ratio * heads[p - m - 1]
    solver = jnp.concatenate(work, axis=0) * scale
    wide = iota((total, lanes), 1)
    high, middle, low = (piece.astype(jnp.float32) for piece in split(solver))

    def pair(left, right):
        return jnp.where(wide < total, pltpu.roll(left, total, 1), right).astype(jnp.bfloat16)

    left_main = jnp.concatenate([pair(high, high), pair(middle, middle)], axis=1)
    left_rest = pair(high, low)
    for row in range(0, part_rows, 2):
        values = jnp.concatenate([whole_ref[row], whole_ref[row + 1]], axis=1)
        f_high, f_middle, f_low = split(values)
        right_main = jnp.concatenate([f_high, f_middle, f_high, f_middle], axis=0)
        right_rest = jnp.concatenate([f_low, f_high], axis=0)
        result = jnp.dot(left_rest, right_rest, preferred_element_type=jnp.float32) + jnp.dot(
            left_main, right_main, preferred_element_type=jnp.float32
        )
        out_ref[pl.ds(row, total, stride=part_rows), :] = result[:, :lanes]
        out_ref[pl.ds(row + 1, total, stride=part_rows), :] = result[:, lanes:]


def call(kernel, outs, *operands, scratch=(), limit=32, **specs):
    return pl.pallas_call(
        kernel,
        out_shape=[jax.ShapeDtypeStruct(shape, jnp.float32) for shape in outs],
        scratch_shapes=[
            pltpu.VMEM(shape, jnp.float32) if isinstance(shape, tuple) else shape
            for shape in scratch
        ],
        compiler_params=pltpu.CompilerParams(vmem_limit_bytes=limit * 1024 * 1024),
        **specs,
    )(*operands)


def exchange(values, axis, distance):
    count = lax.axis_size(axis)
    return lax.ppermute(values, axis, [(i, i ^ distance) for i in range(count)])


def shards(start, levels):
    cols, rows, _ = start.shape
    parts = lax.axis_size("col")
    chunks = cols // tile
    total = cols * parts
    part_rows = rows // parts
    sizes = (cols, rows, parts)
    early = (parts // 2,)
    flat = start.reshape(cols * rows, lanes)
    piece = (part_rows, cols, lanes)
    edges, outer, *raws = call(
        functools.partial(pack_kernel, *sizes, early),
        [(parts + 1, tile, lanes), (2 * chunks + 1, tile, lanes)] + [piece] * len(early),
        pltpu.with_memory_space_constraint(flat, pltpu.HBM),
        pltpu.with_memory_space_constraint(levels, pltpu.HBM),
        scratch=[
            flat.shape,
            pltpu.VMEM(levels.shape, levels.dtype),
            pltpu.SemaphoreType.DMA((2,)),
        ],
        limit=32,
        in_specs=[pl.BlockSpec(memory_space=pl.ANY)] * 2,
    )
    count = lax.axis_size("ly")
    near = exchange(edges, "ly", 1)
    far_pairs = [(i, (i + 1) % count if i % 2 else (i - 1) % count) for i in range(count)]
    far = lax.ppermute(edges, "ly", far_pairs)
    raws = [exchange(values, "col", k) for k, values in zip(early, raws)]
    beside, outer = call(
        functools.partial(outer_kernel, parts),
        [(parts + 1, tile, lanes), (2 * chunks + 3, tile, lanes)],
        outer,
        near,
        far,
    )
    count = lax.axis_size("lx")
    before = lax.ppermute(outer, "lx", [(i, (i + 1) % count) for i in range(count)])
    after = before
    if count > 2:
        after = lax.ppermute(outer, "lx", [((i + 1) % count, i) for i in range(count)])
    inner = call(
        functools.partial(inner_kernel, *sizes, early),
        [(rows, cols, lanes), (2, cols, lanes), (len(early), tile, lanes)],
        flat,
        levels,
        beside,
        scratch=[(rows, cols, lanes)] * 4 + [(rows, lanes)] * 2,
        cost_estimate=pl.CostEstimate(flops=10**11, bytes_accessed=10**9, transcendentals=0),
    )
    lates = call(
        functools.partial(late_kernel, *sizes, early),
        [(2 * chunks + 1, tile, lanes) if k in early else piece for k in range(parts)],
        flat,
        levels,
        beside,
        *inner,
        before,
        after,
    )
    lates = [exchange(values, "col", k) if k else values for k, values in enumerate(lates)]
    whole, gram = call(
        functools.partial(gram_kernel, cols, parts, early),
        [(part_rows, total, lanes), (total // 2, 2 * total)],
        levels,
        *lates,
        *raws,
        scratch=[piece, (rows, lanes)],
    )
    steps = []
    for axis in ("ly", "lx", "col"):
        bit = 1
        while bit < lax.axis_size(axis):
            steps.append((axis, bit))
            bit *= 2
    for axis, bit in steps[:-1]:
        gram = gram + exchange(gram, axis, bit)
    scale = math.sqrt(rows * lax.axis_size("lx") * lanes * lax.axis_size("ly"))
    (basis,) = call(
        functools.partial(solve_kernel, scale),
        [(total * part_rows, lanes)],
        whole,
        gram,
        exchange(gram, *steps[-1]),
    )
    return basis.reshape(total, part_rows, lanes)


def solution(mesh):
    placed = (P("col", "lx", "ly"), P("lx", "ly"))
    return jax.shard_map(
        shards, mesh=mesh, in_specs=placed, out_specs=P(None, ("lx", "col"), "ly"), check_vma=False
    )
```

```python
import functools
import itertools
import math

import jax
import jax.numpy as jnp
from jax import lax
from jax.experimental import pallas as pl
from jax.experimental.pallas import tpu as pltpu
from jax.sharding import PartitionSpec as P

center = 2.1
half_width = 3.1
spread_width = 4.0
level_top = 15.0
lanes = 128
tile = 8


def iota(shape, dim):
    return lax.broadcasted_iota(jnp.int32, shape, dim)


def site_factor(levels):
    onsite = spread_width * (levels / level_top - 0.5)
    return (onsite - center) / half_width


def tile_at(ref, rows, row, chunk):
    return ref[pl.ds(chunk * tile * rows + row, tile, stride=rows), :]


def pack_edges(tiles):
    lane = iota((tile, lanes), 1)
    packed = jnp.zeros((tile, lanes), jnp.float32)
    for k, values in enumerate(tiles):
        moved = pltpu.roll(values, (4 * k + 2) % lanes, 1)
        packed = jnp.where(lane // 4 == k, moved, packed)
    return packed


def unpack_edges(packed, k):
    return pltpu.roll(packed, lanes - (4 * k + 2), 1)


def pack_kernel(cols, rows, parts, early, start_hbm, levels_hbm, edges_ref, outer_ref, *refs):
    piece_refs, (start_ref, levels_ref, arrived) = refs[: len(early)], refs[len(early) :]
    chunks = cols // tile
    part_rows = rows // parts
    copies = [
        pltpu.make_async_copy(start_hbm, start_ref, arrived.at[0]),
        pltpu.make_async_copy(levels_hbm, levels_ref, arrived.at[1]),
    ]
    for copy in copies:
        copy.start()
    for copy in copies:
        copy.wait()
    for group in range(parts):
        edges_ref[group] = pack_edges(
            tile_at(start_ref, rows, group * part_rows + row, chunk)
            for row in range(part_rows)
            for chunk in range(chunks)
        )
    edges_ref[parts] = pack_edges(
        levels_ref[k * tile : (k + 1) * tile, :].astype(jnp.float32) for k in range(rows // tile)
    )
    for chunk in range(chunks):
        outer_ref[chunk] = tile_at(start_ref, rows, 0, chunk)
        outer_ref[chunks + chunk] = tile_at(start_ref, rows, rows - 1, chunk)
    first = levels_ref[0:1, :].astype(jnp.float32)
    last = levels_ref[rows - 1 : rows, :].astype(jnp.float32)
    outer_ref[2 * chunks] = jnp.where(iota((tile, lanes), 0) == 0, first, last)
    for k, piece_ref in zip(early, piece_refs):
        copy_piece(cols, rows, parts, k, start_ref, piece_ref)


def copy_piece(cols, rows, parts, k, start_ref, piece_ref):
    chunks = cols // tile
    part_rows = rows // parts
    base = (lax.axis_index("col") ^ k) * part_rows
    for row in range(part_rows):
        for chunk in range(chunks):
            piece_ref[row, chunk * tile : (chunk + 1) * tile, :] = tile_at(
                start_ref, rows, base + row, chunk
            )


def outer_kernel(parts, outer_ref, near_ref, far_ref, beside_ref, send_ref):
    from_left = iota((tile, lanes), 1) % 4 < 2
    even_place = lax.axis_index("ly") % 2 == 0
    for group in range(parts + 1):
        near, far = near_ref[group], far_ref[group]
        beside_ref[group] = jnp.where(
            even_place, jnp.where(from_left, far, near), jnp.where(from_left, near, far)
        )
    count = outer_ref.shape[0]
    send_ref[:count] = outer_ref[...]
    send_ref[count] = beside_ref[0]
    send_ref[count + 1] = beside_ref[parts - 1]


inverse = 1.0 / half_width


def sides(main, other):
    lane = iota(main.shape, 1)
    return pltpu.roll(jnp.where(lane == lanes - 1, other, main), 1, 1) + pltpu.roll(
        jnp.where(lane == 0, other, main), lanes - 1, 1
    )


def upward(row, above, below):
    even = iota(above.shape, 1) % 2 == row % 2
    return jnp.where(even, above, below)


def factor_at(ref, row, height):
    return jnp.broadcast_to(ref[pl.ds(row, 1), :], (height, lanes))


def inner_kernel(
    cols, rows, parts, early, start_ref, levels_ref, beside_ref, done_ref, next_ref, packed_ref, *refs
):
    field, edge, once, once_edge, factor, factor_edge = refs
    chunks = cols // tile
    part_rows = rows // parts
    factor[...] = site_factor(levels_ref[...].astype(jnp.float32))
    for k in range(rows // tile):
        factor_edge[k * tile : (k + 1) * tile, :] = site_factor(unpack_edges(beside_ref[parts], k))
    for row in range(rows):
        for chunk in range(chunks):
            part = pl.ds(chunk * tile, tile)
            field[row, part, :] = tile_at(start_ref, rows, row, chunk)
            edge[row, part, :] = unpack_edges(
                beside_ref[row // part_rows], row % part_rows * chunks + chunk
            )
    for row in range(rows):
        here, beside = field[row], edge[row]
        up, down = min(row + 1, rows - 1), max(row - 1, 0)
        once[row] = factor_at(factor, row, cols) * here - inverse * (
            sides(here, beside) + upward(row, field[up], field[down])
        )
        once_edge[row] = factor_at(factor_edge, row, cols) * beside - inverse * (
            sides(beside, here) + upward(row, edge[up], edge[down])
        )
    for row in range(1, rows - 1):
        here = once[row]
        twice = factor_at(factor, row, cols) * here - inverse * (
            sides(here, once_edge[row]) + upward(row, once[row + 1], once[row - 1])
        )
        done_ref[row] = 2.0 * twice - field[row]
    done_ref[0] = once[0]
    done_ref[rows - 1] = once[rows - 1]
    next_ref[0] = once[1]
    next_ref[1] = once[rows - 2]
    for at, k in enumerate(early):
        base = (lax.axis_index("col") ^ k) * part_rows
        packed_ref[at] = pack_edges(
            done_ref[base + row, chunk * tile : (chunk + 1) * tile, :]
            for row in range(part_rows)
            for chunk in range(chunks)
        )


def outer_rows(cols, rows, start_ref, levels_ref, beside_ref, parts, before_ref, after_ref, next_ref):
    chunks = cols // tile
    part_rows = rows // parts

    def joined(tiles):
        return jnp.concatenate(list(tiles), axis=0)

    def field(row):
        return joined(tile_at(start_ref, rows, row, chunk) for chunk in range(chunks))

    def edge(row):
        return joined(
            unpack_edges(beside_ref[row // part_rows], row % part_rows * chunks + chunk)
            for chunk in range(chunks)
        )

    def factor(values):
        return jnp.broadcast_to(site_factor(values), (cols, lanes))

    for outer in (0, 1):
        if outer == 0:
            row, inside = 0, 1
            field_out = joined(before_ref[chunks + chunk] for chunk in range(chunks))
            edge_out = joined(
                unpack_edges(before_ref[2 * chunks + 2], (part_rows - 1) * chunks + chunk)
                for chunk in range(chunks)
            )
            factor_out = factor(before_ref[2 * chunks, 1:2, :])
        else:
            row, inside = rows - 1, rows - 2
            field_out = joined(after_ref[chunk] for chunk in range(chunks))
            edge_out = joined(
                unpack_edges(after_ref[2 * chunks + 1], chunk) for chunk in range(chunks)
            )
            factor_out = factor(after_ref[2 * chunks, 0:1, :])

        def vertical(within, without):
            return upward(row, *((within, without) if outer == 0 else (without, within)))

        here, beside = field(row), edge(row)
        here_factor = factor(levels_ref[row : row + 1, :].astype(jnp.float32))
        levels_edge = unpack_edges(beside_ref[parts], row // tile)
        edge_factor = factor(levels_edge[row % tile : row % tile + 1, :])
        once = here_factor * here - inverse * (
            sides(here, beside) + vertical(field(inside), field_out)
        )
        once_edge = edge_factor * beside - inverse * (
            sides(beside, here) + vertical(edge(inside), edge_out)
        )
        once_out = factor_out * field_out - inverse * (sides(field_out, edge_out) + here)
        twice = here_factor * once - inverse * (
            sides(once, once_edge) + vertical(next_ref[outer], once_out)
        )
        yield 2.0 * twice - here


def late_kernel(
    cols,
    rows,
    parts,
    early,
    order,
    start_ref,
    levels_ref,
    beside_ref,
    done_ref,
    next_ref,
    packed_ref,
    before_ref,
    after_ref,
    *out_refs,
):
    chunks = cols // tile
    part_rows = rows // parts
    first, last = outer_rows(
        cols, rows, start_ref, levels_ref, beside_ref, parts, before_ref, after_ref, next_ref
    )
    for k, out_ref in zip(order, out_refs):
        target = lax.axis_index("col") ^ k
        base = target * part_rows
        top = jnp.where(target == 0, first, done_ref[base])
        bottom = jnp.where(target == parts - 1, last, done_ref[base + part_rows - 1])
        if k not in early:
            out_ref[0] = top
            out_ref[1 : part_rows - 1] = done_ref[pl.ds(base + 1, part_rows - 2)]
            out_ref[part_rows - 1] = bottom
            continue
        for chunk in range(chunks):
            part = slice(chunk * tile, (chunk + 1) * tile)
            out_ref[chunk] = top[part]
            out_ref[chunks + chunk] = bottom[part]
        out_ref[2 * chunks] = packed_ref[early.index(k)]


def gram_kernel(cols, parts, early, order, levels_ref, *refs):
    late_refs, refs = dict(zip(order, refs)), refs[parts:]
    raw_refs = dict(zip(early, refs))
    whole_ref, gram_ref, once, factor = refs[len(early) :]
    chunks = cols // tile
    part_rows = whole_ref.shape[0]
    total = cols * parts
    place = lax.axis_index("col")
    factor[...] = site_factor(levels_ref[...].astype(jnp.float32))
    lane = iota((cols, lanes), 1)
    outer_lanes = (lane < 2) | (lane >= lanes - 2)
    for k in range(parts):
        part = pl.ds(pl.multiple_of((place ^ k) * cols, tile), cols)
        late_ref = late_refs[k]
        if k not in early:
            whole_ref[:, part, :] = late_ref[...]
            continue
        raw_ref = raw_refs[k]
        base = place * part_rows
        for row in range(part_rows):
            above, below = raw_ref[min(row + 1, part_rows - 1)], raw_ref[max(row - 1, 0)]
            here = raw_ref[row]
            once[row] = factor_at(factor, base + row, cols) * here - inverse * (
                sides(here, here) + upward(row, above, below)
            )
        packed = late_ref[2 * chunks]
        for row in range(part_rows):
            if row in (0, part_rows - 1):
                at = 0 if row == 0 else chunks
                whole_ref[row, part, :] = jnp.concatenate(
                    [late_ref[at + chunk] for chunk in range(chunks)], axis=0
                )
                continue
            here = once[row]
            twice = factor_at(factor, base + row, cols) * here - inverse * (
                sides(here, here) + upward(row, once[row + 1], once[row - 1])
            )
            sent = jnp.concatenate(
                [unpack_edges(packed, row * chunks + chunk) for chunk in range(chunks)], axis=0
            )
            whole_ref[row, part, :] = jnp.where(outer_lanes, sent, 2.0 * twice - raw_ref[row])
    products = jnp.zeros((3 * total, 3 * total), jnp.float32)
    for row in range(0, part_rows, 2):
        values = jnp.concatenate([whole_ref[row], whole_ref[row + 1]], axis=1)
        stack = jnp.concatenate(split(values), axis=0)
        products += lax.dot_general(
            stack, stack, (((1,), (1,)), ((), ())), preferred_element_type=jnp.float32
        )
    gram = jnp.zeros((total, total), jnp.float32)
    for i in reversed(range(3)):
        for j in reversed(range(3)):
            gram += products[i * total : (i + 1) * total, j * total : (j + 1) * total]
    half = total // 2
    gram_ref[...] = jnp.concatenate([gram[:half], gram[half:]], axis=1)


def split(values):
    high = values.astype(jnp.bfloat16)
    rest = values - high.astype(jnp.float32)
    middle = rest.astype(jnp.bfloat16)
    low = (rest - middle.astype(jnp.float32)).astype(jnp.bfloat16)
    return high, middle, low


def solve_kernel(scale, holder, whole_ref, gram_ref, other_ref, out_ref):
    part_rows, total, _ = whole_ref.shape
    blocks = total // tile
    half = total // 2
    holds = lax.axis_index("ly") % 2 == holder
    packed = jnp.where(holds, gram_ref[...], other_ref[...])
    lane = iota((tile, lanes), 1)
    sub = iota((tile, lanes), 0)
    shape = (tile, lanes)
    work = []
    for i in range(blocks):
        at = i * tile % half
        block = packed[at : at + tile, :]
        if i * tile >= half:
            block = pltpu.roll(block, total, 1)
        unit = jnp.where(lane - total == sub + i * tile, 1.0, 0.0)
        work.append(jnp.where(lane < total, block, unit))
    for b in range(blocks):
        column = {
            i: [
                jnp.broadcast_to(work[i][:, b * tile + m : b * tile + m + 1], shape)
                for m in range(tile)
            ]
            for i in range(b, blocks)
        }
        for m in range(tile):
            pivot = jnp.broadcast_to(column[b][m][m : m + 1, :], shape)
            root = lax.rsqrt(pivot)
            row = jnp.broadcast_to(work[b][m : m + 1, :], shape) * root
            heads = [
                jnp.broadcast_to(column[b][p][m : m + 1, :], shape) * root
                for p in range(m + 1, tile)
            ]
            for i in range(b, blocks):
                ratio = column[i][m] * root
                if i == b:
                    ratio = jnp.where(sub > m, ratio, 0.0)
                    work[i] = jnp.where(sub == m, row, work[i] - ratio * row)
                else:
                    work[i] = work[i] - ratio * row
                for p in range(m + 1, tile):
                    column[i][p] = column[i][p] - ratio * heads[p - m - 1]
    solver = jnp.concatenate(work, axis=0) * scale
    wide = iota((total, lanes), 1)
    high, middle, low = (piece.astype(jnp.float32) for piece in split(solver))

    def pair(left, right):
        return jnp.where(wide < total, pltpu.roll(left, total, 1), right).astype(jnp.bfloat16)

    left_main = jnp.concatenate([pair(high, high), pair(middle, middle)], axis=1)
    left_rest = pair(high, low)
    for row in range(0, part_rows, 2):
        values = jnp.concatenate([whole_ref[row], whole_ref[row + 1]], axis=1)
        f_high, f_middle, f_low = split(values)
        right_main = jnp.concatenate([f_high, f_middle, f_high, f_middle], axis=0)
        right_rest = jnp.concatenate([f_low, f_high], axis=0)
        result = jnp.dot(left_rest, right_rest, preferred_element_type=jnp.float32) + jnp.dot(
            left_main, right_main, preferred_element_type=jnp.float32
        )
        out_ref[pl.ds(row, total, stride=part_rows), :] = result[:, :lanes]
        out_ref[pl.ds(row + 1, total, stride=part_rows), :] = result[:, lanes:]


def call(kernel, outs, *operands, scratch=(), limit=32, **specs):
    return pl.pallas_call(
        kernel,
        out_shape=[jax.ShapeDtypeStruct(shape, jnp.float32) for shape in outs],
        scratch_shapes=[
            pltpu.VMEM(shape, jnp.float32) if isinstance(shape, tuple) else shape
            for shape in scratch
        ],
        compiler_params=pltpu.CompilerParams(vmem_limit_bytes=limit * 1024 * 1024),
        **specs,
    )(*operands)


def exchange(values, axis, distance):
    count = lax.axis_size(axis)
    return lax.ppermute(values, axis, [(i, i ^ distance) for i in range(count)])


axes = ("lx", "ly", "col")


def pair_steps():
    steps = []
    for axis in ("ly", "lx", "col"):
        bit = 2 if axis == "ly" else 1
        while bit < lax.axis_size(axis):
            steps.append((axis, bit))
            bit *= 2
    return steps


def handover(holder, axis, bit):
    sizes = [lax.axis_size(name) for name in axes]
    pairs = []
    for at, (x, y, z) in enumerate(itertools.product(*map(range, sizes))):
        to = {"lx": x, "ly": y ^ 1, "col": z}
        if y % 2 == holder:
            to[axis] ^= bit
        pairs.append((at, (to["lx"] * sizes[1] + to["ly"]) * sizes[2] + to["col"]))
    return pairs


def shards(start, levels):
    cols, rows, _ = start.shape
    parts = lax.axis_size("col")
    chunks = cols // tile
    total = cols * parts
    part_rows = rows // parts
    sizes = (cols, rows, parts)
    early = (parts // 2,)
    order = (*sorted(range(1, parts), key=lambda k: (k in early, -k)), 0)
    flat = start.reshape(cols * rows, lanes)
    piece = (part_rows, cols, lanes)
    edges, outer, *raws = call(
        functools.partial(pack_kernel, *sizes, early),
        [(parts + 1, tile, lanes), (2 * chunks + 1, tile, lanes)] + [piece] * len(early),
        pltpu.with_memory_space_constraint(flat, pltpu.HBM),
        pltpu.with_memory_space_constraint(levels, pltpu.HBM),
        scratch=[
            flat.shape,
            pltpu.VMEM(levels.shape, levels.dtype),
            pltpu.SemaphoreType.DMA((2,)),
        ],
        limit=32,
        in_specs=[pl.BlockSpec(memory_space=pl.ANY)] * 2,
    )
    count = lax.axis_size("ly")
    near = exchange(edges, "ly", 1)
    far_pairs = [(i, (i + 1) % count if i % 2 else (i - 1) % count) for i in range(count)]
    far = lax.ppermute(edges, "ly", far_pairs)
    raws = [exchange(values, "col", k) for k, values in zip(early, raws)]
    beside, outer = call(
        functools.partial(outer_kernel, parts),
        [(parts + 1, tile, lanes), (2 * chunks + 3, tile, lanes)],
        outer,
        near,
        far,
    )
    count = lax.axis_size("lx")
    before = lax.ppermute(outer, "lx", [(i, (i + 1) % count) for i in range(count)])
    after = before
    if count > 2:
        after = lax.ppermute(outer, "lx", [((i + 1) % count, i) for i in range(count)])
    inner = call(
        functools.partial(inner_kernel, *sizes, early),
        [(rows, cols, lanes), (2, cols, lanes), (len(early), tile, lanes)],
        flat,
        levels,
        beside,
        scratch=[(rows, cols, lanes)] * 4 + [(rows, lanes)] * 2,
        cost_estimate=pl.CostEstimate(flops=10**11, bytes_accessed=10**9, transcendentals=0),
    )
    lates = call(
        functools.partial(late_kernel, *sizes, early, order),
        [(2 * chunks + 1, tile, lanes) if k in early else piece for k in order],
        flat,
        levels,
        beside,
        *inner,
        before,
        after,
    )
    lates = [exchange(values, "col", k) if k else values for k, values in zip(order, lates)]
    whole, gram = call(
        functools.partial(gram_kernel, cols, parts, early, order),
        [(part_rows, total, lanes), (total // 2, 2 * total)],
        levels,
        *lates,
        *raws,
        scratch=[piece, (rows, lanes)],
    )
    gram = gram + exchange(gram, "ly", 1)
    holder = 0
    for axis, bit in pair_steps():
        near = exchange(gram, "ly", 1)
        gram = near + lax.ppermute(gram, axes, handover(holder, axis, bit))
        holder = 1 - holder
    scale = math.sqrt(rows * lax.axis_size("lx") * lanes * lax.axis_size("ly"))
    (basis,) = call(
        functools.partial(solve_kernel, scale, holder),
        [(total * part_rows, lanes)],
        whole,
        gram,
        exchange(gram, "ly", 1),
    )
    return basis.reshape(total, part_rows, lanes)


def solution(mesh):
    placed = (P("col", "lx", "ly"), P("lx", "ly"))
    return jax.shard_map(
        shards, mesh=mesh, in_specs=placed, out_specs=P(None, ("lx", "col"), "ly"), check_vma=False
    )
```

```python
import functools
import itertools
import math

import jax
import jax.numpy as jnp
from jax import lax
from jax.experimental import pallas as pl
from jax.experimental.pallas import tpu as pltpu
from jax.sharding import PartitionSpec as P

center = 2.1
half_width = 3.1
spread_width = 4.0
level_top = 15.0
lanes = 128
tile = 8


def iota(shape, dim):
    return lax.broadcasted_iota(jnp.int32, shape, dim)


def site_factor(levels):
    onsite = spread_width * (levels / level_top - 0.5)
    return (onsite - center) / half_width


def tile_at(ref, rows, row, chunk):
    return ref[pl.ds(chunk * tile * rows + row, tile, stride=rows), :]


def pack_edges(tiles):
    lane = iota((tile, lanes), 1)
    packed = jnp.zeros((tile, lanes), jnp.float32)
    for k, values in tiles:
        moved = pltpu.roll(values, (4 * k + 2) % lanes, 1)
        packed = jnp.where(lane // 4 == k, moved, packed)
    return packed


def unpack_edges(packed, k):
    return pltpu.roll(packed, lanes - (4 * k + 2), 1)


def pack_kernel(
    cols, rows, parts, early, start_hbm, levels_hbm, start_ref, levels_ref, edges_ref, outer_ref, *refs
):
    piece_refs, (arrived,) = refs[: len(early)], refs[len(early) :]
    chunks = cols // tile
    part_rows = rows // parts
    span = tile * rows
    copies = [pltpu.make_async_copy(levels_hbm, levels_ref, arrived.at[chunks])] + [
        pltpu.make_async_copy(
            start_hbm.at[pl.ds(chunk * span, span)],
            start_ref.at[pl.ds(chunk * span, span)],
            arrived.at[chunk],
        )
        for chunk in range(chunks)
    ]
    for copy in copies:
        copy.start()
    copies[0].wait()
    edges_ref[parts] = pack_edges(
        (k, levels_ref[k * tile : (k + 1) * tile, :].astype(jnp.float32))
        for k in range(rows // tile)
    )
    first = levels_ref[0:1, :].astype(jnp.float32)
    last = levels_ref[rows - 1 : rows, :].astype(jnp.float32)
    outer_ref[2 * chunks] = jnp.where(iota((tile, lanes), 0) == 0, first, last)
    for chunk in range(chunks):
        copies[1 + chunk].wait()
        outer_ref[chunk] = tile_at(start_ref, rows, 0, chunk)
        outer_ref[chunks + chunk] = tile_at(start_ref, rows, rows - 1, chunk)
        for group in range(parts):
            packed = pack_edges(
                (row * chunks + chunk, tile_at(start_ref, rows, group * part_rows + row, chunk))
                for row in range(part_rows)
            )
            edges_ref[group] = packed if chunk == 0 else edges_ref[group] + packed
        for k, piece_ref in zip(early, piece_refs):
            copy_piece(cols, rows, parts, k, start_ref, piece_ref, (chunk,))


def copy_piece(cols, rows, parts, k, start_ref, piece_ref, which):
    part_rows = rows // parts
    base = (lax.axis_index("col") ^ k) * part_rows
    for row in range(part_rows):
        for chunk in which:
            piece_ref[row, chunk * tile : (chunk + 1) * tile, :] = tile_at(
                start_ref, rows, base + row, chunk
            )


def outer_kernel(parts, outer_ref, near_ref, far_ref, beside_ref, send_ref):
    from_left = iota((tile, lanes), 1) % 4 < 2
    even_place = lax.axis_index("ly") % 2 == 0
    for group in range(parts + 1):
        near, far = near_ref[group], far_ref[group]
        beside_ref[group] = jnp.where(
            even_place, jnp.where(from_left, far, near), jnp.where(from_left, near, far)
        )
    count = outer_ref.shape[0]
    send_ref[:count] = outer_ref[...]
    send_ref[count] = beside_ref[0]
    send_ref[count + 1] = beside_ref[parts - 1]


inverse = 1.0 / half_width


def sides(main, other):
    lane = iota(main.shape, 1)
    return pltpu.roll(jnp.where(lane == lanes - 1, other, main), 1, 1) + pltpu.roll(
        jnp.where(lane == 0, other, main), lanes - 1, 1
    )


def upward(row, above, below):
    even = iota(above.shape, 1) % 2 == row % 2
    return jnp.where(even, above, below)


def factor_at(ref, row, height):
    return jnp.broadcast_to(ref[pl.ds(row, 1), :], (height, lanes))


def inner_kernel(
    cols, rows, parts, early, start_ref, levels_ref, beside_ref, done_ref, next_ref, packed_ref, *refs
):
    field, edge, once, once_edge, factor, factor_edge = refs
    chunks = cols // tile
    part_rows = rows // parts
    factor[...] = site_factor(levels_ref[...].astype(jnp.float32))
    for k in range(rows // tile):
        factor_edge[k * tile : (k + 1) * tile, :] = site_factor(unpack_edges(beside_ref[parts], k))
    for row in range(rows):
        for chunk in range(chunks):
            part = pl.ds(chunk * tile, tile)
            field[row, part, :] = tile_at(start_ref, rows, row, chunk)
            edge[row, part, :] = unpack_edges(
                beside_ref[row // part_rows], row % part_rows * chunks + chunk
            )
    for row in range(rows):
        here, beside = field[row], edge[row]
        up, down = min(row + 1, rows - 1), max(row - 1, 0)
        once[row] = factor_at(factor, row, cols) * here - inverse * (
            sides(here, beside) + upward(row, field[up], field[down])
        )
        once_edge[row] = factor_at(factor_edge, row, cols) * beside - inverse * (
            sides(beside, here) + upward(row, edge[up], edge[down])
        )
    for row in range(1, rows - 1):
        here = once[row]
        twice = factor_at(factor, row, cols) * here - inverse * (
            sides(here, once_edge[row]) + upward(row, once[row + 1], once[row - 1])
        )
        done_ref[row] = 2.0 * twice - field[row]
    done_ref[0] = once[0]
    done_ref[rows - 1] = once[rows - 1]
    next_ref[0] = once[1]
    next_ref[1] = once[rows - 2]
    for at, k in enumerate(early):
        base = (lax.axis_index("col") ^ k) * part_rows
        packed_ref[at] = pack_edges(
            (row * chunks + chunk, done_ref[base + row, chunk * tile : (chunk + 1) * tile, :])
            for row in range(part_rows)
            for chunk in range(chunks)
        )


def outer_rows(cols, rows, start_ref, levels_ref, beside_ref, parts, before_ref, after_ref, next_ref):
    chunks = cols // tile
    part_rows = rows // parts

    def joined(tiles):
        return jnp.concatenate(list(tiles), axis=0)

    def field(row):
        return joined(tile_at(start_ref, rows, row, chunk) for chunk in range(chunks))

    def edge(row):
        return joined(
            unpack_edges(beside_ref[row // part_rows], row % part_rows * chunks + chunk)
            for chunk in range(chunks)
        )

    def factor(values):
        return jnp.broadcast_to(site_factor(values), (cols, lanes))

    for outer in (0, 1):
        if outer == 0:
            row, inside = 0, 1
            field_out = joined(before_ref[chunks + chunk] for chunk in range(chunks))
            edge_out = joined(
                unpack_edges(before_ref[2 * chunks + 2], (part_rows - 1) * chunks + chunk)
                for chunk in range(chunks)
            )
            factor_out = factor(before_ref[2 * chunks, 1:2, :])
        else:
            row, inside = rows - 1, rows - 2
            field_out = joined(after_ref[chunk] for chunk in range(chunks))
            edge_out = joined(
                unpack_edges(after_ref[2 * chunks + 1], chunk) for chunk in range(chunks)
            )
            factor_out = factor(after_ref[2 * chunks, 0:1, :])

        def vertical(within, without):
            return upward(row, *((within, without) if outer == 0 else (without, within)))

        here, beside = field(row), edge(row)
        here_factor = factor(levels_ref[row : row + 1, :].astype(jnp.float32))
        levels_edge = unpack_edges(beside_ref[parts], row // tile)
        edge_factor = factor(levels_edge[row % tile : row % tile + 1, :])
        once = here_factor * here - inverse * (
            sides(here, beside) + vertical(field(inside), field_out)
        )
        once_edge = edge_factor * beside - inverse * (
            sides(beside, here) + vertical(edge(inside), edge_out)
        )
        once_out = factor_out * field_out - inverse * (sides(field_out, edge_out) + here)
        twice = here_factor * once - inverse * (
            sides(once, once_edge) + vertical(next_ref[outer], once_out)
        )
        yield 2.0 * twice - here


def late_kernel(
    cols,
    rows,
    parts,
    early,
    order,
    start_ref,
    levels_ref,
    beside_ref,
    done_ref,
    next_ref,
    packed_ref,
    before_ref,
    after_ref,
    *out_refs,
):
    chunks = cols // tile
    part_rows = rows // parts
    first, last = outer_rows(
        cols, rows, start_ref, levels_ref, beside_ref, parts, before_ref, after_ref, next_ref
    )
    for k, out_ref in zip(order, out_refs):
        target = lax.axis_index("col") ^ k
        base = target * part_rows
        top = jnp.where(target == 0, first, done_ref[base])
        bottom = jnp.where(target == parts - 1, last, done_ref[base + part_rows - 1])
        if k not in early:
            out_ref[0] = top
            out_ref[1 : part_rows - 1] = done_ref[pl.ds(base + 1, part_rows - 2)]
            out_ref[part_rows - 1] = bottom
            continue
        for chunk in range(chunks):
            part = slice(chunk * tile, (chunk + 1) * tile)
            out_ref[chunk] = top[part]
            out_ref[chunks + chunk] = bottom[part]
        out_ref[2 * chunks] = packed_ref[early.index(k)]


def alone_kernel(cols, levels_ref, raw_ref, out_ref, once, factor):
    part_rows = raw_ref.shape[0]
    factor[...] = site_factor(levels_ref[...].astype(jnp.float32))
    base = lax.axis_index("col") * part_rows
    for row in range(part_rows):
        above, below = raw_ref[min(row + 1, part_rows - 1)], raw_ref[max(row - 1, 0)]
        here = raw_ref[row]
        once[row] = factor_at(factor, base + row, cols) * here - inverse * (
            sides(here, here) + upward(row, above, below)
        )
    for row in range(part_rows):
        above, below = once[min(row + 1, part_rows - 1)], once[max(row - 1, 0)]
        here = once[row]
        twice = factor_at(factor, base + row, cols) * here - inverse * (
            sides(here, here) + upward(row, above, below)
        )
        out_ref[row] = 2.0 * twice - raw_ref[row]


def gram_kernel(cols, parts, early, order, *refs):
    late_refs, refs = dict(zip(order, refs)), refs[parts:]
    alone_refs = dict(zip(early, refs))
    whole_ref, gram_ref = refs[len(early) :]
    chunks = cols // tile
    part_rows = whole_ref.shape[0]
    total = cols * parts
    place = lax.axis_index("col")
    lane = iota((cols, lanes), 1)
    outer_lanes = (lane < 2) | (lane >= lanes - 2)
    for k in range(parts):
        part = pl.ds(pl.multiple_of((place ^ k) * cols, tile), cols)
        late_ref = late_refs[k]
        if k not in early:
            whole_ref[:, part, :] = late_ref[...]
            continue
        packed = late_ref[2 * chunks]
        for row in range(part_rows):
            if row in (0, part_rows - 1):
                at = 0 if row == 0 else chunks
                sent = [late_ref[at + chunk] for chunk in range(chunks)]
                whole_ref[row, part, :] = jnp.concatenate(sent, axis=0)
            else:
                sent = [unpack_edges(packed, row * chunks + chunk) for chunk in range(chunks)]
                whole_ref[row, part, :] = jnp.where(
                    outer_lanes, jnp.concatenate(sent, axis=0), alone_refs[k][row]
                )
    products = jnp.zeros((3 * total, 3 * total), jnp.float32)
    for row in range(0, part_rows, 2):
        values = jnp.concatenate([whole_ref[row], whole_ref[row + 1]], axis=1)
        stack = jnp.concatenate(split(values), axis=0)
        products += lax.dot_general(
            stack, stack, (((1,), (1,)), ((), ())), preferred_element_type=jnp.float32
        )
    gram = jnp.zeros((total, total), jnp.float32)
    for i in reversed(range(3)):
        for j in reversed(range(3)):
            gram += products[i * total : (i + 1) * total, j * total : (j + 1) * total]
    half = total // 2
    gram_ref[...] = jnp.concatenate([gram[:half], gram[half:]], axis=1)


def split(values):
    high = values.astype(jnp.bfloat16)
    rest = values - high.astype(jnp.float32)
    middle = rest.astype(jnp.bfloat16)
    low = (rest - middle.astype(jnp.float32)).astype(jnp.bfloat16)
    return high, middle, low


def solve_kernel(scale, holder, whole_ref, gram_ref, other_ref, out_ref):
    part_rows, total, _ = whole_ref.shape
    blocks = total // tile
    half = total // 2
    holds = lax.axis_index("ly") % 2 == holder
    packed = jnp.where(holds, gram_ref[...], other_ref[...])
    lane = iota((tile, lanes), 1)
    sub = iota((tile, lanes), 0)
    shape = (tile, lanes)
    work = []
    for i in range(blocks):
        at = i * tile % half
        block = packed[at : at + tile, :]
        if i * tile >= half:
            block = pltpu.roll(block, total, 1)
        unit = jnp.where(lane - total == sub + i * tile, 1.0, 0.0)
        work.append(jnp.where(lane < total, block, unit))
    for b in range(blocks):
        column = {
            i: [
                jnp.broadcast_to(work[i][:, b * tile + m : b * tile + m + 1], shape)
                for m in range(tile)
            ]
            for i in range(b, blocks)
        }
        for m in range(tile):
            pivot = jnp.broadcast_to(column[b][m][m : m + 1, :], shape)
            root = lax.rsqrt(pivot)
            row = jnp.broadcast_to(work[b][m : m + 1, :], shape) * root
            heads = [
                jnp.broadcast_to(column[b][p][m : m + 1, :], shape) * root
                for p in range(m + 1, tile)
            ]
            for i in range(b, blocks):
                ratio = column[i][m] * root
                if i == b:
                    ratio = jnp.where(sub > m, ratio, 0.0)
                    work[i] = jnp.where(sub == m, row, work[i] - ratio * row)
                else:
                    work[i] = work[i] - ratio * row
                for p in range(m + 1, tile):
                    column[i][p] = column[i][p] - ratio * heads[p - m - 1]
    solver = jnp.concatenate(work, axis=0) * scale
    wide = iota((total, lanes), 1)
    high, middle, low = (piece.astype(jnp.float32) for piece in split(solver))

    def pair(left, right):
        return jnp.where(wide < total, pltpu.roll(left, total, 1), right).astype(jnp.bfloat16)

    left_main = jnp.concatenate([pair(high, high), pair(middle, middle)], axis=1)
    left_rest = pair(high, low)
    for row in range(0, part_rows, 2):
        values = jnp.concatenate([whole_ref[row], whole_ref[row + 1]], axis=1)
        f_high, f_middle, f_low = split(values)
        right_main = jnp.concatenate([f_high, f_middle, f_high, f_middle], axis=0)
        right_rest = jnp.concatenate([f_low, f_high], axis=0)
        result = jnp.dot(left_rest, right_rest, preferred_element_type=jnp.float32) + jnp.dot(
            left_main, right_main, preferred_element_type=jnp.float32
        )
        out_ref[pl.ds(row, total, stride=part_rows), :] = result[:, :lanes]
        out_ref[pl.ds(row + 1, total, stride=part_rows), :] = result[:, lanes:]


def call(kernel, outs, *operands, scratch=(), limit=32, **specs):
    return pl.pallas_call(
        kernel,
        out_shape=[
            jax.ShapeDtypeStruct(shape, jnp.float32) if isinstance(shape, tuple) else shape
            for shape in outs
        ],
        scratch_shapes=[
            pltpu.VMEM(shape, jnp.float32) if isinstance(shape, tuple) else shape
            for shape in scratch
        ],
        compiler_params=pltpu.CompilerParams(vmem_limit_bytes=limit * 1024 * 1024),
        **specs,
    )(*operands)


def exchange(values, axis, distance):
    count = lax.axis_size(axis)
    return lax.ppermute(values, axis, [(i, i ^ distance) for i in range(count)])


axes = ("lx", "ly", "col")


def pair_steps():
    steps = []
    for axis in ("ly", "lx", "col"):
        bit = 2 if axis == "ly" else 1
        while bit < lax.axis_size(axis):
            steps.append((axis, bit))
            bit *= 2
    return steps


def handover(holder, axis, bit):
    sizes = [lax.axis_size(name) for name in axes]
    pairs = []
    for at, (x, y, z) in enumerate(itertools.product(*map(range, sizes))):
        to = {"lx": x, "ly": y ^ 1, "col": z}
        if y % 2 == holder:
            to[axis] ^= bit
        pairs.append((at, (to["lx"] * sizes[1] + to["ly"]) * sizes[2] + to["col"]))
    return pairs


def shards(start, levels):
    cols, rows, _ = start.shape
    parts = lax.axis_size("col")
    chunks = cols // tile
    total = cols * parts
    part_rows = rows // parts
    sizes = (cols, rows, parts)
    early = (parts // 2,)
    order = (*sorted(range(1, parts), key=lambda k: (k in early, -k)), 0)
    flat = start.reshape(cols * rows, lanes)
    piece = (part_rows, cols, lanes)
    start_here, levels_here, edges, outer, *raws = call(
        functools.partial(pack_kernel, *sizes, early),
        [flat.shape, jax.ShapeDtypeStruct(levels.shape, levels.dtype), (parts + 1, tile, lanes), (2 * chunks + 1, tile, lanes)] + [piece] * len(early),
        pltpu.with_memory_space_constraint(flat, pltpu.HBM),
        pltpu.with_memory_space_constraint(levels, pltpu.HBM),
        scratch=[pltpu.SemaphoreType.DMA((chunks + 1,))],
        limit=32,
        in_specs=[pl.BlockSpec(memory_space=pl.ANY)] * 2,
    )
    count = lax.axis_size("ly")
    near = exchange(edges, "ly", 1)
    far_pairs = [(i, (i + 1) % count if i % 2 else (i - 1) % count) for i in range(count)]
    far = lax.ppermute(edges, "ly", far_pairs)
    raws = [exchange(values, "col", k) for k, values in zip(early, raws)]
    beside, outer = call(
        functools.partial(outer_kernel, parts),
        [(parts + 1, tile, lanes), (2 * chunks + 3, tile, lanes)],
        outer,
        near,
        far,
    )
    count = lax.axis_size("lx")
    before = lax.ppermute(outer, "lx", [(i, (i + 1) % count) for i in range(count)])
    after = before
    if count > 2:
        after = lax.ppermute(outer, "lx", [((i + 1) % count, i) for i in range(count)])
    inner = call(
        functools.partial(inner_kernel, *sizes, early),
        [(rows, cols, lanes), (2, cols, lanes), (len(early), tile, lanes)],
        start_here,
        levels_here,
        beside,
        scratch=[(rows, cols, lanes)] * 4 + [(rows, lanes)] * 2,
        cost_estimate=pl.CostEstimate(flops=10**11, bytes_accessed=10**9, transcendentals=0),
    )
    lates = call(
        functools.partial(late_kernel, *sizes, early, order),
        [(2 * chunks + 1, tile, lanes) if k in early else piece for k in order],
        start_here,
        levels_here,
        beside,
        *inner,
        before,
        after,
    )
    lates = [exchange(values, "col", k) if k else values for k, values in zip(order, lates)]
    alones = [
        call(
            functools.partial(alone_kernel, cols),
            [piece],
            levels_here,
            raw,
            scratch=[piece, (rows, lanes)],
            cost_estimate=pl.CostEstimate(flops=0, bytes_accessed=10**6, transcendentals=0),
        )[0]
        for raw in raws
    ]
    whole, gram = call(
        functools.partial(gram_kernel, cols, parts, early, order),
        [(part_rows, total, lanes), (total // 2, 2 * total)],
        *lates,
        *alones,
    )
    gram = gram + exchange(gram, "ly", 1)
    holder = 0
    for axis, bit in pair_steps():
        near = exchange(gram, "ly", 1)
        gram = near + lax.ppermute(gram, axes, handover(holder, axis, bit))
        holder = 1 - holder
    scale = math.sqrt(rows * lax.axis_size("lx") * lanes * lax.axis_size("ly"))
    (basis,) = call(
        functools.partial(solve_kernel, scale, holder),
        [(total * part_rows, lanes)],
        whole,
        gram,
        exchange(gram, "ly", 1),
    )
    return basis.reshape(total, part_rows, lanes)


def solution(mesh):
    placed = (P("col", "lx", "ly"), P("lx", "ly"))
    return jax.shard_map(
        shards, mesh=mesh, in_specs=placed, out_specs=P(None, ("lx", "col"), "ly"), check_vma=False
    )
```

```python
import functools
import itertools
import math

import jax
import jax.numpy as jnp
from jax import lax
from jax.experimental import pallas as pl
from jax.experimental.pallas import tpu as pltpu
from jax.sharding import PartitionSpec as P

center = 2.1
half_width = 3.1
spread_width = 4.0
level_top = 15.0
lanes = 128
tile = 8


def iota(shape, dim):
    return lax.broadcasted_iota(jnp.int32, shape, dim)


def site_factor(levels):
    onsite = spread_width * (levels / level_top - 0.5)
    return (onsite - center) / half_width


def tile_at(ref, rows, row, chunk):
    return ref[pl.ds(chunk * tile * rows + row, tile, stride=rows), :]


def pack_edges(tiles):
    lane = iota((tile, lanes), 1)
    packed = jnp.zeros((tile, lanes), jnp.float32)
    for k, values in tiles:
        moved = pltpu.roll(values, (4 * k + 2) % lanes, 1)
        packed = jnp.where(lane // 4 == k, moved, packed)
    return packed


def unpack_edges(packed, k):
    return pltpu.roll(packed, lanes - (4 * k + 2), 1)


def pack_kernel(
    cols, rows, parts, early, start_hbm, levels_hbm, start_ref, levels_ref, edges_ref, outer_ref, *refs
):
    piece_refs, (arrived,) = refs[: len(early)], refs[len(early) :]
    chunks = cols // tile
    part_rows = rows // parts
    span = tile * rows
    copies = [pltpu.make_async_copy(levels_hbm, levels_ref, arrived.at[chunks])] + [
        pltpu.make_async_copy(
            start_hbm.at[pl.ds(chunk * span, span)],
            start_ref.at[pl.ds(chunk * span, span)],
            arrived.at[chunk],
        )
        for chunk in range(chunks)
    ]
    for copy in copies:
        copy.start()
    copies[0].wait()
    edges_ref[parts] = pack_edges(
        (k, levels_ref[k * tile : (k + 1) * tile, :].astype(jnp.float32))
        for k in range(rows // tile)
    )
    first = levels_ref[0:1, :].astype(jnp.float32)
    last = levels_ref[rows - 1 : rows, :].astype(jnp.float32)
    outer_ref[2 * chunks] = jnp.where(iota((tile, lanes), 0) == 0, first, last)
    for chunk in range(chunks):
        copies[1 + chunk].wait()
        outer_ref[chunk] = tile_at(start_ref, rows, 0, chunk)
        outer_ref[chunks + chunk] = tile_at(start_ref, rows, rows - 1, chunk)
        for group in range(parts):
            packed = pack_edges(
                (row * chunks + chunk, tile_at(start_ref, rows, group * part_rows + row, chunk))
                for row in range(part_rows)
            )
            edges_ref[group] = packed if chunk == 0 else edges_ref[group] + packed
        for k, piece_ref in zip(early, piece_refs):
            copy_piece(cols, rows, parts, k, start_ref, piece_ref, (chunk,))


def copy_piece(cols, rows, parts, k, start_ref, piece_ref, which):
    part_rows = rows // parts
    base = (lax.axis_index("col") ^ k) * part_rows
    for row in range(part_rows):
        for chunk in which:
            piece_ref[row, chunk * tile : (chunk + 1) * tile, :] = tile_at(
                start_ref, rows, base + row, chunk
            )


def outer_kernel(parts, outer_ref, near_ref, far_ref, beside_ref, send_ref):
    from_left = iota((tile, lanes), 1) % 4 < 2
    even_place = lax.axis_index("ly") % 2 == 0
    for group in range(parts + 1):
        near, far = near_ref[group], far_ref[group]
        beside_ref[group] = jnp.where(
            even_place, jnp.where(from_left, far, near), jnp.where(from_left, near, far)
        )
    count = outer_ref.shape[0]
    send_ref[:count] = outer_ref[...]
    send_ref[count] = beside_ref[0]
    send_ref[count + 1] = beside_ref[parts - 1]


inverse = 1.0 / half_width


def sides(main, other):
    lane = iota(main.shape, 1)
    return pltpu.roll(jnp.where(lane == lanes - 1, other, main), 1, 1) + pltpu.roll(
        jnp.where(lane == 0, other, main), lanes - 1, 1
    )


def upward(row, above, below):
    even = iota(above.shape, 1) % 2 == row % 2
    return jnp.where(even, above, below)


def factor_at(ref, row, height):
    return jnp.broadcast_to(ref[pl.ds(row, 1), :], (height, lanes))


def inner_kernel(
    cols, rows, parts, early, start_ref, levels_ref, beside_ref, done_ref, next_ref, packed_ref, *refs
):
    field, edge, once, once_edge, factor, factor_edge = refs
    chunks = cols // tile
    part_rows = rows // parts
    factor[...] = site_factor(levels_ref[...].astype(jnp.float32))
    for k in range(rows // tile):
        factor_edge[k * tile : (k + 1) * tile, :] = site_factor(unpack_edges(beside_ref[parts], k))
    for row in range(rows):
        for chunk in range(chunks):
            part = pl.ds(chunk * tile, tile)
            field[row, part, :] = tile_at(start_ref, rows, row, chunk)
            edge[row, part, :] = unpack_edges(
                beside_ref[row // part_rows], row % part_rows * chunks + chunk
            )
    for row in range(rows):
        here, beside = field[row], edge[row]
        up, down = min(row + 1, rows - 1), max(row - 1, 0)
        once[row] = factor_at(factor, row, cols) * here - inverse * (
            sides(here, beside) + upward(row, field[up], field[down])
        )
        once_edge[row] = factor_at(factor_edge, row, cols) * beside - inverse * (
            sides(beside, here) + upward(row, edge[up], edge[down])
        )
    for row in range(1, rows - 1):
        here = once[row]
        twice = factor_at(factor, row, cols) * here - inverse * (
            sides(here, once_edge[row]) + upward(row, once[row + 1], once[row - 1])
        )
        done_ref[row] = 2.0 * twice - field[row]
    done_ref[0] = once[0]
    done_ref[rows - 1] = once[rows - 1]
    next_ref[0] = once[1]
    next_ref[1] = once[rows - 2]
    for at, k in enumerate(early):
        base = (lax.axis_index("col") ^ k) * part_rows
        packed_ref[at] = pack_edges(
            (row * chunks + chunk, done_ref[base + row, chunk * tile : (chunk + 1) * tile, :])
            for row in range(part_rows)
            for chunk in range(chunks)
        )


def outer_rows(cols, rows, start_ref, levels_ref, beside_ref, parts, before_ref, after_ref, next_ref):
    chunks = cols // tile
    part_rows = rows // parts

    def joined(tiles):
        return jnp.concatenate(list(tiles), axis=0)

    def field(row):
        return joined(tile_at(start_ref, rows, row, chunk) for chunk in range(chunks))

    def edge(row):
        return joined(
            unpack_edges(beside_ref[row // part_rows], row % part_rows * chunks + chunk)
            for chunk in range(chunks)
        )

    def factor(values):
        return jnp.broadcast_to(site_factor(values), (cols, lanes))

    for outer in (0, 1):
        if outer == 0:
            row, inside = 0, 1
            field_out = joined(before_ref[chunks + chunk] for chunk in range(chunks))
            edge_out = joined(
                unpack_edges(before_ref[2 * chunks + 2], (part_rows - 1) * chunks + chunk)
                for chunk in range(chunks)
            )
            factor_out = factor(before_ref[2 * chunks, 1:2, :])
        else:
            row, inside = rows - 1, rows - 2
            field_out = joined(after_ref[chunk] for chunk in range(chunks))
            edge_out = joined(
                unpack_edges(after_ref[2 * chunks + 1], chunk) for chunk in range(chunks)
            )
            factor_out = factor(after_ref[2 * chunks, 0:1, :])

        def vertical(within, without):
            return upward(row, *((within, without) if outer == 0 else (without, within)))

        here, beside = field(row), edge(row)
        here_factor = factor(levels_ref[row : row + 1, :].astype(jnp.float32))
        levels_edge = unpack_edges(beside_ref[parts], row // tile)
        edge_factor = factor(levels_edge[row % tile : row % tile + 1, :])
        once = here_factor * here - inverse * (
            sides(here, beside) + vertical(field(inside), field_out)
        )
        once_edge = edge_factor * beside - inverse * (
            sides(beside, here) + vertical(edge(inside), edge_out)
        )
        once_out = factor_out * field_out - inverse * (sides(field_out, edge_out) + here)
        twice = here_factor * once - inverse * (
            sides(once, once_edge) + vertical(next_ref[outer], once_out)
        )
        yield 2.0 * twice - here


def late_kernel(
    cols,
    rows,
    parts,
    early,
    order,
    start_ref,
    levels_ref,
    beside_ref,
    done_ref,
    next_ref,
    packed_ref,
    before_ref,
    after_ref,
    *out_refs,
):
    chunks = cols // tile
    part_rows = rows // parts
    first, last = outer_rows(
        cols, rows, start_ref, levels_ref, beside_ref, parts, before_ref, after_ref, next_ref
    )
    for k, out_ref in zip(order, out_refs):
        target = lax.axis_index("col") ^ k
        base = target * part_rows
        top = jnp.where(target == 0, first, done_ref[base])
        bottom = jnp.where(target == parts - 1, last, done_ref[base + part_rows - 1])
        if k not in early:
            out_ref[0] = top
            out_ref[1 : part_rows - 1] = done_ref[pl.ds(base + 1, part_rows - 2)]
            out_ref[part_rows - 1] = bottom
            continue
        for chunk in range(chunks):
            part = slice(chunk * tile, (chunk + 1) * tile)
            out_ref[chunk] = top[part]
            out_ref[chunks + chunk] = bottom[part]
        out_ref[2 * chunks] = packed_ref[early.index(k)]


def alone_kernel(cols, levels_ref, raw_ref, out_ref, once, factor):
    part_rows = raw_ref.shape[0]
    factor[...] = site_factor(levels_ref[...].astype(jnp.float32))
    base = lax.axis_index("col") * part_rows
    for row in range(part_rows):
        above, below = raw_ref[min(row + 1, part_rows - 1)], raw_ref[max(row - 1, 0)]
        here = raw_ref[row]
        once[row] = factor_at(factor, base + row, cols) * here - inverse * (
            sides(here, here) + upward(row, above, below)
        )
    for row in range(part_rows):
        above, below = once[min(row + 1, part_rows - 1)], once[max(row - 1, 0)]
        here = once[row]
        twice = factor_at(factor, base + row, cols) * here - inverse * (
            sides(here, here) + upward(row, above, below)
        )
        out_ref[row] = 2.0 * twice - raw_ref[row]


def gram_kernel(cols, parts, early, order, *refs):
    late_refs, refs = dict(zip(order, refs)), refs[parts:]
    alone_refs = dict(zip(early, refs))
    whole_ref, gram_ref = refs[len(early) :]
    chunks = cols // tile
    part_rows = whole_ref.shape[0]
    total = cols * parts
    place = lax.axis_index("col")
    lane = iota((cols, lanes), 1)
    outer_lanes = (lane < 2) | (lane >= lanes - 2)
    for k in range(parts):
        part = pl.ds(pl.multiple_of((place ^ k) * cols, tile), cols)
        late_ref = late_refs[k]
        if k not in early:
            whole_ref[:, part, :] = late_ref[...]
            continue
        packed = late_ref[2 * chunks]
        for row in range(part_rows):
            if row in (0, part_rows - 1):
                at = 0 if row == 0 else chunks
                sent = [late_ref[at + chunk] for chunk in range(chunks)]
                whole_ref[row, part, :] = jnp.concatenate(sent, axis=0)
            else:
                sent = [unpack_edges(packed, row * chunks + chunk) for chunk in range(chunks)]
                whole_ref[row, part, :] = jnp.where(
                    outer_lanes, jnp.concatenate(sent, axis=0), alone_refs[k][row]
                )
    products = jnp.zeros((3 * total, 3 * total), jnp.float32)
    for row in range(0, part_rows, 2):
        values = jnp.concatenate([whole_ref[row], whole_ref[row + 1]], axis=1)
        stack = jnp.concatenate(split(values), axis=0)
        products += lax.dot_general(
            stack, stack, (((1,), (1,)), ((), ())), preferred_element_type=jnp.float32
        )
    gram = jnp.zeros((total, total), jnp.float32)
    for i in reversed(range(3)):
        for j in reversed(range(3)):
            gram += products[i * total : (i + 1) * total, j * total : (j + 1) * total]
    half = total // 2
    gram_ref[...] = jnp.concatenate([gram[:half], gram[half:]], axis=1)


def split(values):
    high = values.astype(jnp.bfloat16)
    rest = values - high.astype(jnp.float32)
    middle = rest.astype(jnp.bfloat16)
    low = (rest - middle.astype(jnp.float32)).astype(jnp.bfloat16)
    return high, middle, low


def eliminate(work, b, columns_ref, rows_ref):
    shape = (tile, lanes)
    sub = iota(shape, 0)

    def spread(ref, *place):
        return jnp.broadcast_to(ref[(*place[:-1], pl.ds(place[-1], 1), slice(None))], shape)

    column = [
        [jnp.broadcast_to(rows[:, b * tile + m : b * tile + m + 1], shape) for m in range(tile)]
        for rows in work[b:]
    ]
    slot = b % 2
    for m in range(tile):
        columns_ref[slot, m] = column[0][m]
    rows_ref[slot] = work[b]
    factor = {(p, q): spread(columns_ref, slot, q, p) for p in range(tile) for q in range(p + 1)}
    pivots = [spread(rows_ref, slot, m) for m in range(tile)]
    roots = []
    for m in range(tile):
        roots.append(lax.rsqrt(factor[m, m]))
        for p in range(m + 1, tile):
            factor[p, m] = factor[p, m] * roots[m]
        for p in range(m + 1, tile):
            for q in range(m + 1, p + 1):
                factor[p, q] = factor[p, q] - factor[p, m] * factor[q, m]
    for m in range(tile):
        for p in range(m):
            pivots[m] = pivots[m] - factor[m, p] * pivots[p]
        pivots[m] = pivots[m] * roots[m]
    for m in range(tile):
        work[b] = jnp.where(sub == m, pivots[m], work[b])
    for i in range(b + 1, len(work)):
        ratio = column[i - b]
        for m in range(tile):
            for p in range(m):
                ratio[m] = ratio[m] - ratio[p] * factor[m, p]
            ratio[m] = ratio[m] * roots[m]
            work[i] = work[i] - ratio[m] * pivots[m]


def solve_kernel(
    scale, holder, whole_ref, gram_ref, other_ref, out_hbm, out_ref, columns_ref, rows_ref, copied
):
    part_rows, total, _ = whole_ref.shape
    blocks = total // tile
    half = total // 2
    holds = lax.axis_index("ly") % 2 == holder
    packed = jnp.where(holds, gram_ref[...], other_ref[...])
    lane = iota((tile, lanes), 1)
    sub = iota((tile, lanes), 0)
    work = []
    for i in range(blocks):
        at = i * tile % half
        block = packed[at : at + tile, :]
        if i * tile >= half:
            block = pltpu.roll(block, total, 1)
        unit = jnp.where(lane - total == sub + i * tile, 1.0, 0.0)
        work.append(jnp.where(lane < total, block, unit))
    copies = []
    cuts = (0, 3 * blocks // 4, blocks)
    for part, (first, last) in enumerate(zip(cuts, cuts[1:])):
        for b in range(first, last):
            eliminate(work, b, columns_ref, rows_ref)
        solver = jnp.concatenate(work[first:last], axis=0) * scale
        wide = iota(solver.shape, 1)
        high, middle, low = (piece.astype(jnp.float32) for piece in split(solver))

        def pair(left, right):
            return jnp.where(wide < total, pltpu.roll(left, total, 1), right).astype(jnp.bfloat16)

        left_main = jnp.concatenate([pair(high, high), pair(middle, middle)], axis=1)
        left_rest = pair(high, low)
        height = (last - first) * tile
        base = first * tile * part_rows
        for row in range(0, part_rows, 2):
            values = jnp.concatenate([whole_ref[row], whole_ref[row + 1]], axis=1)
            f_high, f_middle, f_low = split(values)
            right_main = jnp.concatenate([f_high, f_middle, f_high, f_middle], axis=0)
            right_rest = jnp.concatenate([f_low, f_high], axis=0)
            result = jnp.dot(left_rest, right_rest, preferred_element_type=jnp.float32) + jnp.dot(
                left_main, right_main, preferred_element_type=jnp.float32
            )
            out_ref[pl.ds(base + row, height, stride=part_rows), :] = result[:, :lanes]
            out_ref[pl.ds(base + row + 1, height, stride=part_rows), :] = result[:, lanes:]
        span = pl.ds(base, height * part_rows)
        copies.append(pltpu.make_async_copy(out_ref.at[span], out_hbm.at[span], copied.at[part]))
        copies[-1].start()
    for copy in copies:
        copy.wait()


def call(kernel, outs, *operands, scratch=(), limit=32, **specs):
    return pl.pallas_call(
        kernel,
        out_shape=[
            jax.ShapeDtypeStruct(shape, jnp.float32) if isinstance(shape, tuple) else shape
            for shape in outs
        ],
        scratch_shapes=[
            pltpu.VMEM(shape, jnp.float32) if isinstance(shape, tuple) else shape
            for shape in scratch
        ],
        compiler_params=pltpu.CompilerParams(vmem_limit_bytes=limit * 1024 * 1024),
        **specs,
    )(*operands)


def exchange(values, axis, distance):
    count = lax.axis_size(axis)
    return lax.ppermute(values, axis, [(i, i ^ distance) for i in range(count)])


axes = ("lx", "ly", "col")


def pair_steps():
    steps = []
    for axis in ("ly", "lx", "col"):
        bit = 2 if axis == "ly" else 1
        while bit < lax.axis_size(axis):
            steps.append((axis, bit))
            bit *= 2
    return steps


def handover(holder, axis, bit):
    sizes = [lax.axis_size(name) for name in axes]
    pairs = []
    for at, (x, y, z) in enumerate(itertools.product(*map(range, sizes))):
        to = {"lx": x, "ly": y ^ 1, "col": z}
        if y % 2 == holder:
            to[axis] ^= bit
        pairs.append((at, (to["lx"] * sizes[1] + to["ly"]) * sizes[2] + to["col"]))
    return pairs


def shards(start, levels):
    cols, rows, _ = start.shape
    parts = lax.axis_size("col")
    chunks = cols // tile
    total = cols * parts
    part_rows = rows // parts
    sizes = (cols, rows, parts)
    early = (parts // 2,)
    order = (*sorted(range(1, parts), key=lambda k: (k in early, -k)), 0)
    flat = start.reshape(cols * rows, lanes)
    piece = (part_rows, cols, lanes)
    start_here, levels_here, edges, outer, *raws = call(
        functools.partial(pack_kernel, *sizes, early),
        [flat.shape, jax.ShapeDtypeStruct(levels.shape, levels.dtype), (parts + 1, tile, lanes), (2 * chunks + 1, tile, lanes)] + [piece] * len(early),
        pltpu.with_memory_space_constraint(flat, pltpu.HBM),
        pltpu.with_memory_space_constraint(levels, pltpu.HBM),
        scratch=[pltpu.SemaphoreType.DMA((chunks + 1,))],
        limit=32,
        in_specs=[pl.BlockSpec(memory_space=pl.ANY)] * 2,
    )
    count = lax.axis_size("ly")
    near = exchange(edges, "ly", 1)
    far_pairs = [(i, (i + 1) % count if i % 2 else (i - 1) % count) for i in range(count)]
    far = lax.ppermute(edges, "ly", far_pairs)
    raws = [exchange(values, "col", k) for k, values in zip(early, raws)]
    beside, outer = call(
        functools.partial(outer_kernel, parts),
        [(parts + 1, tile, lanes), (2 * chunks + 3, tile, lanes)],
        outer,
        near,
        far,
    )
    count = lax.axis_size("lx")
    before = lax.ppermute(outer, "lx", [(i, (i + 1) % count) for i in range(count)])
    after = before
    if count > 2:
        after = lax.ppermute(outer, "lx", [((i + 1) % count, i) for i in range(count)])
    inner = call(
        functools.partial(inner_kernel, *sizes, early),
        [(rows, cols, lanes), (2, cols, lanes), (len(early), tile, lanes)],
        start_here,
        levels_here,
        beside,
        scratch=[(rows, cols, lanes)] * 4 + [(rows, lanes)] * 2,
        cost_estimate=pl.CostEstimate(flops=10**11, bytes_accessed=10**9, transcendentals=0),
    )
    lates = call(
        functools.partial(late_kernel, *sizes, early, order),
        [(2 * chunks + 1, tile, lanes) if k in early else piece for k in order],
        start_here,
        levels_here,
        beside,
        *inner,
        before,
        after,
    )
    lates = [exchange(values, "col", k) if k else values for k, values in zip(order, lates)]
    alones = [
        call(
            functools.partial(alone_kernel, cols),
            [piece],
            levels_here,
            raw,
            scratch=[piece, (rows, lanes)],
            cost_estimate=pl.CostEstimate(flops=0, bytes_accessed=10**6, transcendentals=0),
        )[0]
        for raw in raws
    ]
    whole, gram = call(
        functools.partial(gram_kernel, cols, parts, early, order),
        [(part_rows, total, lanes), (total // 2, 2 * total)],
        *lates,
        *alones,
    )
    gram = gram + exchange(gram, "ly", 1)
    holder = 0
    for axis, bit in pair_steps():
        near = exchange(gram, "ly", 1)
        gram = near + lax.ppermute(gram, axes, handover(holder, axis, bit))
        holder = 1 - holder
    scale = math.sqrt(rows * lax.axis_size("lx") * lanes * lax.axis_size("ly"))
    (basis,) = call(
        functools.partial(solve_kernel, scale, holder),
        [(total * part_rows, lanes)],
        whole,
        gram,
        exchange(gram, "ly", 1),
        scratch=[
            (total * part_rows, lanes),
            (2, tile, tile, lanes),
            (2, tile, lanes),
            pltpu.SemaphoreType.DMA((2,)),
        ],
        out_specs=[pl.BlockSpec(memory_space=pl.ANY)],
    )
    return basis.reshape(total, part_rows, lanes)


def solution(mesh):
    placed = (P("col", "lx", "ly"), P("lx", "ly"))
    return jax.shard_map(
        shards, mesh=mesh, in_specs=placed, out_specs=P(None, ("lx", "col"), "ly"), check_vma=False
    )
```

```python
import functools
import itertools
import math

import jax
import jax.numpy as jnp
from jax import lax
from jax.experimental import pallas as pl
from jax.experimental.pallas import tpu as pltpu
from jax.sharding import PartitionSpec as P

center = 2.1
half_width = 3.1
spread_width = 4.0
level_top = 15.0
lanes = 128
tile = 8


def iota(shape, dim):
    return lax.broadcasted_iota(jnp.int32, shape, dim)


def site_factor(levels):
    onsite = spread_width * (levels / level_top - 0.5)
    return (onsite - center) / half_width


def tile_at(ref, rows, row, chunk):
    return ref[pl.ds(chunk * tile * rows + row, tile, stride=rows), :]


def pack_edges(tiles):
    lane = iota((tile, lanes), 1)
    packed = jnp.zeros((tile, lanes), jnp.float32)
    for k, values in tiles:
        moved = pltpu.roll(values, (4 * k + 2) % lanes, 1)
        packed = jnp.where(lane // 4 == k, moved, packed)
    return packed


def unpack_edges(packed, k):
    return pltpu.roll(packed, lanes - (4 * k + 2), 1)


def pack_kernel(
    cols, rows, parts, early, start_hbm, levels_hbm, start_ref, levels_ref, edges_ref, outer_ref, *refs
):
    piece_refs, (arrived,) = refs[: len(early)], refs[len(early) :]
    chunks = cols // tile
    part_rows = rows // parts
    span = tile * rows
    copies = [pltpu.make_async_copy(levels_hbm, levels_ref, arrived.at[chunks])] + [
        pltpu.make_async_copy(
            start_hbm.at[pl.ds(chunk * span, span)],
            start_ref.at[pl.ds(chunk * span, span)],
            arrived.at[chunk],
        )
        for chunk in range(chunks)
    ]
    for copy in copies:
        copy.start()
    copies[0].wait()
    edges_ref[parts] = pack_edges(
        (k, levels_ref[k * tile : (k + 1) * tile, :].astype(jnp.float32))
        for k in range(rows // tile)
    )
    first = levels_ref[0:1, :].astype(jnp.float32)
    last = levels_ref[rows - 1 : rows, :].astype(jnp.float32)
    outer_ref[2 * chunks] = jnp.where(iota((tile, lanes), 0) == 0, first, last)
    for chunk in range(chunks):
        copies[1 + chunk].wait()
        outer_ref[chunk] = tile_at(start_ref, rows, 0, chunk)
        outer_ref[chunks + chunk] = tile_at(start_ref, rows, rows - 1, chunk)
        for group in range(parts):
            packed = pack_edges(
                (row * chunks + chunk, tile_at(start_ref, rows, group * part_rows + row, chunk))
                for row in range(part_rows)
            )
            edges_ref[group] = packed if chunk == 0 else edges_ref[group] + packed
        for k, piece_ref in zip(early, piece_refs):
            copy_piece(cols, rows, parts, k, start_ref, piece_ref, (chunk,))


def copy_piece(cols, rows, parts, k, start_ref, piece_ref, which):
    part_rows = rows // parts
    base = (lax.axis_index("col") ^ k) * part_rows
    for row in range(part_rows):
        for chunk in which:
            piece_ref[row, chunk * tile : (chunk + 1) * tile, :] = tile_at(
                start_ref, rows, base + row, chunk
            )


def outer_kernel(parts, outer_ref, near_ref, far_ref, beside_ref, send_ref):
    from_left = iota((tile, lanes), 1) % 4 < 2
    even_place = lax.axis_index("ly") % 2 == 0
    for group in range(parts + 1):
        near, far = near_ref[group], far_ref[group]
        beside_ref[group] = jnp.where(
            even_place, jnp.where(from_left, far, near), jnp.where(from_left, near, far)
        )
    count = outer_ref.shape[0]
    send_ref[:count] = outer_ref[...]
    send_ref[count] = beside_ref[0]
    send_ref[count + 1] = beside_ref[parts - 1]


inverse = 1.0 / half_width


def sides(main, other):
    lane = iota(main.shape, 1)
    return pltpu.roll(jnp.where(lane == lanes - 1, other, main), 1, 1) + pltpu.roll(
        jnp.where(lane == 0, other, main), lanes - 1, 1
    )


def upward(row, above, below):
    even = iota(above.shape, 1) % 2 == row % 2
    return jnp.where(even, above, below)


def factor_at(ref, row, height):
    return jnp.broadcast_to(ref[pl.ds(row, 1), :], (height, lanes))


def inner_kernel(
    cols, rows, parts, early, start_ref, levels_ref, beside_ref, done_ref, next_ref, packed_ref, *refs
):
    field, edge, once, once_edge, factor, factor_edge = refs
    chunks = cols // tile
    part_rows = rows // parts
    factor[...] = site_factor(levels_ref[...].astype(jnp.float32))
    for k in range(rows // tile):
        factor_edge[k * tile : (k + 1) * tile, :] = site_factor(unpack_edges(beside_ref[parts], k))
    for row in range(rows):
        for chunk in range(chunks):
            part = pl.ds(chunk * tile, tile)
            field[row, part, :] = tile_at(start_ref, rows, row, chunk)
            edge[row, part, :] = unpack_edges(
                beside_ref[row // part_rows], row % part_rows * chunks + chunk
            )
    for row in range(rows):
        here, beside = field[row], edge[row]
        up, down = min(row + 1, rows - 1), max(row - 1, 0)
        once[row] = factor_at(factor, row, cols) * here - inverse * (
            sides(here, beside) + upward(row, field[up], field[down])
        )
        once_edge[row] = factor_at(factor_edge, row, cols) * beside - inverse * (
            sides(beside, here) + upward(row, edge[up], edge[down])
        )
    for row in range(1, rows - 1):
        here = once[row]
        twice = factor_at(factor, row, cols) * here - inverse * (
            sides(here, once_edge[row]) + upward(row, once[row + 1], once[row - 1])
        )
        done_ref[row] = 2.0 * twice - field[row]
    done_ref[0] = once[0]
    done_ref[rows - 1] = once[rows - 1]
    next_ref[0] = once[1]
    next_ref[1] = once[rows - 2]
    for at, k in enumerate(early):
        base = (lax.axis_index("col") ^ k) * part_rows
        packed_ref[at] = pack_edges(
            (row * chunks + chunk, done_ref[base + row, chunk * tile : (chunk + 1) * tile, :])
            for row in range(part_rows)
            for chunk in range(chunks)
        )


def outer_rows(cols, rows, start_ref, levels_ref, beside_ref, parts, before_ref, after_ref, next_ref):
    chunks = cols // tile
    part_rows = rows // parts

    def joined(tiles):
        return jnp.concatenate(list(tiles), axis=0)

    def field(row):
        return joined(tile_at(start_ref, rows, row, chunk) for chunk in range(chunks))

    def edge(row):
        return joined(
            unpack_edges(beside_ref[row // part_rows], row % part_rows * chunks + chunk)
            for chunk in range(chunks)
        )

    def factor(values):
        return jnp.broadcast_to(site_factor(values), (cols, lanes))

    for outer in (0, 1):
        if outer == 0:
            row, inside = 0, 1
            field_out = joined(before_ref[chunks + chunk] for chunk in range(chunks))
            edge_out = joined(
                unpack_edges(before_ref[2 * chunks + 2], (part_rows - 1) * chunks + chunk)
                for chunk in range(chunks)
            )
            factor_out = factor(before_ref[2 * chunks, 1:2, :])
        else:
            row, inside = rows - 1, rows - 2
            field_out = joined(after_ref[chunk] for chunk in range(chunks))
            edge_out = joined(
                unpack_edges(after_ref[2 * chunks + 1], chunk) for chunk in range(chunks)
            )
            factor_out = factor(after_ref[2 * chunks, 0:1, :])

        def vertical(within, without):
            return upward(row, *((within, without) if outer == 0 else (without, within)))

        here, beside = field(row), edge(row)
        here_factor = factor(levels_ref[row : row + 1, :].astype(jnp.float32))
        levels_edge = unpack_edges(beside_ref[parts], row // tile)
        edge_factor = factor(levels_edge[row % tile : row % tile + 1, :])
        once = here_factor * here - inverse * (
            sides(here, beside) + vertical(field(inside), field_out)
        )
        once_edge = edge_factor * beside - inverse * (
            sides(beside, here) + vertical(edge(inside), edge_out)
        )
        once_out = factor_out * field_out - inverse * (sides(field_out, edge_out) + here)
        twice = here_factor * once - inverse * (
            sides(once, once_edge) + vertical(next_ref[outer], once_out)
        )
        yield 2.0 * twice - here


def late_kernel(
    cols,
    rows,
    parts,
    early,
    order,
    start_ref,
    levels_ref,
    beside_ref,
    done_ref,
    next_ref,
    packed_ref,
    before_ref,
    after_ref,
    *out_refs,
):
    chunks = cols // tile
    part_rows = rows // parts
    first, last = outer_rows(
        cols, rows, start_ref, levels_ref, beside_ref, parts, before_ref, after_ref, next_ref
    )
    for k, out_ref in zip(order, out_refs):
        target = lax.axis_index("col") ^ k
        base = target * part_rows
        top = jnp.where(target == 0, first, done_ref[base])
        bottom = jnp.where(target == parts - 1, last, done_ref[base + part_rows - 1])
        if k not in early:
            out_ref[0] = top
            out_ref[1 : part_rows - 1] = done_ref[pl.ds(base + 1, part_rows - 2)]
            out_ref[part_rows - 1] = bottom
            continue
        for chunk in range(chunks):
            part = slice(chunk * tile, (chunk + 1) * tile)
            out_ref[chunk] = top[part]
            out_ref[chunks + chunk] = bottom[part]
        out_ref[2 * chunks] = packed_ref[early.index(k)]


def alone_kernel(cols, levels_ref, raw_ref, out_ref, once, factor):
    part_rows = raw_ref.shape[0]
    factor[...] = site_factor(levels_ref[...].astype(jnp.float32))
    base = lax.axis_index("col") * part_rows
    for row in range(part_rows):
        above, below = raw_ref[min(row + 1, part_rows - 1)], raw_ref[max(row - 1, 0)]
        here = raw_ref[row]
        once[row] = factor_at(factor, base + row, cols) * here - inverse * (
            sides(here, here) + upward(row, above, below)
        )
    for row in range(part_rows):
        above, below = once[min(row + 1, part_rows - 1)], once[max(row - 1, 0)]
        here = once[row]
        twice = factor_at(factor, base + row, cols) * here - inverse * (
            sides(here, here) + upward(row, above, below)
        )
        out_ref[row] = 2.0 * twice - raw_ref[row]


def gram_kernel(cols, parts, early, order, *refs):
    late_refs, refs = dict(zip(order, refs)), refs[parts:]
    alone_refs = dict(zip(early, refs))
    whole_ref, gram_ref = refs[len(early) :]
    chunks = cols // tile
    part_rows = whole_ref.shape[0]
    total = cols * parts
    place = lax.axis_index("col")
    lane = iota((cols, lanes), 1)
    outer_lanes = (lane < 2) | (lane >= lanes - 2)
    for k in range(parts):
        part = pl.ds(pl.multiple_of((place ^ k) * cols, tile), cols)
        late_ref = late_refs[k]
        if k not in early:
            whole_ref[:, part, :] = late_ref[...]
            continue
        packed = late_ref[2 * chunks]
        for row in range(part_rows):
            if row in (0, part_rows - 1):
                at = 0 if row == 0 else chunks
                sent = [late_ref[at + chunk] for chunk in range(chunks)]
                whole_ref[row, part, :] = jnp.concatenate(sent, axis=0)
            else:
                sent = [unpack_edges(packed, row * chunks + chunk) for chunk in range(chunks)]
                whole_ref[row, part, :] = jnp.where(
                    outer_lanes, jnp.concatenate(sent, axis=0), alone_refs[k][row]
                )
    products = jnp.zeros((3 * total, 3 * total), jnp.float32)
    for row in range(0, part_rows, 2):
        values = jnp.concatenate([whole_ref[row], whole_ref[row + 1]], axis=1)
        stack = jnp.concatenate(split(values), axis=0)
        products += lax.dot_general(
            stack, stack, (((1,), (1,)), ((), ())), preferred_element_type=jnp.float32
        )
    gram = jnp.zeros((total, total), jnp.float32)
    for i in reversed(range(3)):
        for j in reversed(range(3)):
            gram += products[i * total : (i + 1) * total, j * total : (j + 1) * total]
    half = total // 2
    gram_ref[...] = jnp.concatenate([gram[:half], gram[half:]], axis=1)


def split(values):
    high = values.astype(jnp.bfloat16)
    rest = values - high.astype(jnp.float32)
    middle = rest.astype(jnp.bfloat16)
    low = (rest - middle.astype(jnp.float32)).astype(jnp.bfloat16)
    return high, middle, low


def eliminate(work, b, columns_ref, rows_ref):
    shape = (tile, lanes)
    sub = iota(shape, 0)

    def spread(ref, *place):
        return jnp.broadcast_to(ref[(*place[:-1], pl.ds(place[-1], 1), slice(None))], shape)

    column = [
        [jnp.broadcast_to(rows[:, b * tile + m : b * tile + m + 1], shape) for m in range(tile)]
        for rows in work[b:]
    ]
    slot = b % 2
    for m in range(tile):
        columns_ref[slot, m] = column[0][m]
    rows_ref[slot] = work[b]
    factor = {(p, q): spread(columns_ref, slot, q, p) for p in range(tile) for q in range(p + 1)}
    pivots = [spread(rows_ref, slot, m) for m in range(tile)]
    roots = []
    for m in range(tile):
        roots.append(lax.rsqrt(factor[m, m]))
        for p in range(m + 1, tile):
            factor[p, m] = factor[p, m] * roots[m]
        for p in range(m + 1, tile):
            for q in range(m + 1, p + 1):
                factor[p, q] = factor[p, q] - factor[p, m] * factor[q, m]
    for m in range(tile):
        for p in range(m):
            pivots[m] = pivots[m] - factor[m, p] * pivots[p]
        pivots[m] = pivots[m] * roots[m]
    for m in range(tile):
        work[b] = jnp.where(sub == m, pivots[m], work[b])
    for i in range(b + 1, len(work)):
        ratio = column[i - b]
        for m in range(tile):
            for p in range(m):
                ratio[m] = ratio[m] - ratio[p] * factor[m, p]
            ratio[m] = ratio[m] * roots[m]
            work[i] = work[i] - ratio[m] * pivots[m]


def solve_kernel(
    scale, holder, whole_ref, gram_ref, other_ref, out_hbm, out_ref, columns_ref, rows_ref, copied
):
    part_rows, total, _ = whole_ref.shape
    blocks = total // tile
    half = total // 2
    holds = lax.axis_index("ly") % 2 == holder
    packed = jnp.where(holds, gram_ref[...], other_ref[...])
    lane = iota((tile, lanes), 1)
    sub = iota((tile, lanes), 0)
    work = []
    for i in range(blocks):
        at = i * tile % half
        block = packed[at : at + tile, :]
        if i * tile >= half:
            block = pltpu.roll(block, total, 1)
        unit = jnp.where(lane - total == sub + i * tile, 1.0, 0.0)
        work.append(jnp.where(lane < total, block, unit))
    copies = []
    cuts = (0, 3 * blocks // 4, blocks)
    for part, (first, last) in enumerate(zip(cuts, cuts[1:])):
        for b in range(first, last):
            eliminate(work, b, columns_ref, rows_ref)
        solver = jnp.concatenate(work[first:last], axis=0) * scale
        wide = iota(solver.shape, 1)
        high, middle, low = (piece.astype(jnp.float32) for piece in split(solver))

        def pair(left, right):
            return jnp.where(wide < total, pltpu.roll(left, total, 1), right).astype(jnp.bfloat16)

        left_main = jnp.concatenate([pair(high, high), pair(middle, middle)], axis=1)
        left_rest = pair(high, low)
        height = (last - first) * tile
        base = first * tile * part_rows
        for row in range(0, part_rows, 2):
            values = jnp.concatenate([whole_ref[row], whole_ref[row + 1]], axis=1)
            f_high, f_middle, f_low = split(values)
            right_main = jnp.concatenate([f_high, f_middle, f_high, f_middle], axis=0)
            right_rest = jnp.concatenate([f_low, f_high], axis=0)
            result = jnp.dot(left_rest, right_rest, preferred_element_type=jnp.float32) + jnp.dot(
                left_main, right_main, preferred_element_type=jnp.float32
            )
            out_ref[pl.ds(base + row, height, stride=part_rows), :] = result[:, :lanes]
            out_ref[pl.ds(base + row + 1, height, stride=part_rows), :] = result[:, lanes:]
        span = pl.ds(base, height * part_rows)
        copies.append(pltpu.make_async_copy(out_ref.at[span], out_hbm.at[span], copied.at[part]))
        copies[-1].start()
    for copy in copies:
        copy.wait()


def call(kernel, outs, *operands, scratch=(), limit=32, **specs):
    return pl.pallas_call(
        kernel,
        out_shape=[
            jax.ShapeDtypeStruct(shape, jnp.float32) if isinstance(shape, tuple) else shape
            for shape in outs
        ],
        scratch_shapes=[
            pltpu.VMEM(shape, jnp.float32) if isinstance(shape, tuple) else shape
            for shape in scratch
        ],
        compiler_params=pltpu.CompilerParams(vmem_limit_bytes=limit * 1024 * 1024),
        **specs,
    )(*operands)


def exchange(values, axis, distance):
    count = lax.axis_size(axis)
    return lax.ppermute(values, axis, [(i, i ^ distance) for i in range(count)])


axes = ("lx", "ly", "col")


def pair_steps():
    steps = []
    for axis in ("ly", "lx", "col"):
        bit = 2 if axis == "ly" else 1
        while bit < lax.axis_size(axis):
            steps.append((axis, bit))
            bit *= 2
    return steps


def handover(holder, axis, bit):
    sizes = [lax.axis_size(name) for name in axes]
    pairs = []
    for at, (x, y, z) in enumerate(itertools.product(*map(range, sizes))):
        to = {"lx": x, "ly": y ^ 1, "col": z}
        if y % 2 == holder:
            to[axis] ^= bit
        pairs.append((at, (to["lx"] * sizes[1] + to["ly"]) * sizes[2] + to["col"]))
    return pairs


def shards(start, levels):
    cols, rows, _ = start.shape
    parts = lax.axis_size("col")
    chunks = cols // tile
    total = cols * parts
    part_rows = rows // parts
    sizes = (cols, rows, parts)
    early = (parts - 1,)
    order = (*sorted(range(1, parts), key=lambda k: (k in early, -k)), 0)
    flat = start.reshape(cols * rows, lanes)
    piece = (part_rows, cols, lanes)
    start_here, levels_here, edges, outer, *raws = call(
        functools.partial(pack_kernel, *sizes, early),
        [flat.shape, jax.ShapeDtypeStruct(levels.shape, levels.dtype), (parts + 1, tile, lanes), (2 * chunks + 1, tile, lanes)] + [piece] * len(early),
        pltpu.with_memory_space_constraint(flat, pltpu.HBM),
        pltpu.with_memory_space_constraint(levels, pltpu.HBM),
        scratch=[pltpu.SemaphoreType.DMA((chunks + 1,))],
        limit=32,
        in_specs=[pl.BlockSpec(memory_space=pl.ANY)] * 2,
    )
    count = lax.axis_size("ly")
    near = exchange(edges, "ly", 1)
    far_pairs = [(i, (i + 1) % count if i % 2 else (i - 1) % count) for i in range(count)]
    far = lax.ppermute(edges, "ly", far_pairs)
    raws = [exchange(values, "col", k) for k, values in zip(early, raws)]
    beside, outer = call(
        functools.partial(outer_kernel, parts),
        [(parts + 1, tile, lanes), (2 * chunks + 3, tile, lanes)],
        outer,
        near,
        far,
    )
    count = lax.axis_size("lx")
    before = lax.ppermute(outer, "lx", [(i, (i + 1) % count) for i in range(count)])
    after = before
    if count > 2:
        after = lax.ppermute(outer, "lx", [((i + 1) % count, i) for i in range(count)])
    inner = call(
        functools.partial(inner_kernel, *sizes, early),
        [(rows, cols, lanes), (2, cols, lanes), (len(early), tile, lanes)],
        start_here,
        levels_here,
        beside,
        scratch=[(rows, cols, lanes)] * 4 + [(rows, lanes)] * 2,
        cost_estimate=pl.CostEstimate(flops=10**11, bytes_accessed=10**9, transcendentals=0),
    )
    lates = call(
        functools.partial(late_kernel, *sizes, early, order),
        [(2 * chunks + 1, tile, lanes) if k in early else piece for k in order],
        start_here,
        levels_here,
        beside,
        *inner,
        before,
        after,
    )
    lates = [exchange(values, "col", k) if k else values for k, values in zip(order, lates)]
    alones = [
        call(
            functools.partial(alone_kernel, cols),
            [piece],
            levels_here,
            raw,
            scratch=[piece, (rows, lanes)],
            cost_estimate=pl.CostEstimate(flops=0, bytes_accessed=10**6, transcendentals=0),
        )[0]
        for raw in raws
    ]
    whole, gram = call(
        functools.partial(gram_kernel, cols, parts, early, order),
        [(part_rows, total, lanes), (total // 2, 2 * total)],
        *lates,
        *alones,
    )
    gram = gram + exchange(gram, "ly", 1)
    holder = 0
    for axis, bit in pair_steps():
        near = exchange(gram, "ly", 1)
        gram = near + lax.ppermute(gram, axes, handover(holder, axis, bit))
        holder = 1 - holder
    scale = math.sqrt(rows * lax.axis_size("lx") * lanes * lax.axis_size("ly"))
    (basis,) = call(
        functools.partial(solve_kernel, scale, holder),
        [(total * part_rows, lanes)],
        whole,
        gram,
        exchange(gram, "ly", 1),
        scratch=[
            (total * part_rows, lanes),
            (2, tile, tile, lanes),
            (2, tile, lanes),
            pltpu.SemaphoreType.DMA((2,)),
        ],
        out_specs=[pl.BlockSpec(memory_space=pl.ANY)],
    )
    return basis.reshape(total, part_rows, lanes)


def solution(mesh):
    placed = (P("col", "lx", "ly"), P("lx", "ly"))
    return jax.shard_map(
        shards, mesh=mesh, in_specs=placed, out_specs=P(None, ("lx", "col"), "ly"), check_vma=False
    )
```

```python
import functools
import itertools
import math

import jax
import jax.numpy as jnp
from jax import lax
from jax.experimental import pallas as pl
from jax.experimental.pallas import tpu as pltpu
from jax.sharding import PartitionSpec as P

center = 2.1
half_width = 3.1
spread_width = 4.0
level_top = 15.0
lanes = 128
tile = 8


def iota(shape, dim):
    return lax.broadcasted_iota(jnp.int32, shape, dim)


def site_factor(levels):
    onsite = spread_width * (levels / level_top - 0.5)
    return (onsite - center) / half_width


def tile_at(ref, rows, row, chunk):
    return ref[pl.ds(chunk * tile * rows + row, tile, stride=rows), :]


def pack_edges(tiles):
    lane = iota((tile, lanes), 1)
    packed = jnp.zeros((tile, lanes), jnp.float32)
    for k, values in tiles:
        moved = pltpu.roll(values, (4 * k + 2) % lanes, 1)
        packed = jnp.where(lane // 4 == k, moved, packed)
    return packed


def unpack_edges(packed, k):
    return pltpu.roll(packed, lanes - (4 * k + 2), 1)


def pack_kernel(
    cols,
    rows,
    parts,
    early,
    start_hbm,
    levels_hbm,
    whole_hbm,
    start_ref,
    levels_ref,
    edges_ref,
    outer_ref,
    *refs,
):
    piece_refs, (arrived,) = refs[: len(early)], refs[len(early) :]
    chunks = cols // tile
    part_rows = rows // parts
    span = tile * rows
    copies = [pltpu.make_async_copy(levels_hbm, levels_ref, arrived.at[chunks])] + [
        pltpu.make_async_copy(
            start_hbm.at[pl.ds(chunk * span, span)],
            start_ref.at[pl.ds(chunk * span, span)],
            arrived.at[chunk],
        )
        for chunk in range(chunks)
    ]
    for at, (k, piece_ref) in enumerate(zip(early, piece_refs)):
        base = pl.multiple_of((lax.axis_index("col") ^ k) * part_rows, part_rows)
        copies.append(
            pltpu.make_async_copy(
                whole_hbm.at[:, pl.ds(base, part_rows), :], piece_ref, arrived.at[chunks + 1 + at]
            )
        )
    for copy in copies:
        copy.start()
    copies[0].wait()
    edges_ref[parts] = pack_edges(
        (k, levels_ref[k * tile : (k + 1) * tile, :].astype(jnp.float32))
        for k in range(rows // tile)
    )
    first = levels_ref[0:1, :].astype(jnp.float32)
    last = levels_ref[rows - 1 : rows, :].astype(jnp.float32)
    outer_ref[2 * chunks] = jnp.where(iota((tile, lanes), 0) == 0, first, last)
    for chunk in range(chunks):
        copies[1 + chunk].wait()
        outer_ref[chunk] = tile_at(start_ref, rows, 0, chunk)
        outer_ref[chunks + chunk] = tile_at(start_ref, rows, rows - 1, chunk)
        for group in range(parts):
            packed = pack_edges(
                (row * chunks + chunk, tile_at(start_ref, rows, group * part_rows + row, chunk))
                for row in range(part_rows)
            )
            edges_ref[group] = packed if chunk == 0 else edges_ref[group] + packed
    for copy in copies[1 + chunks :]:
        copy.wait()


def outer_kernel(parts, outer_ref, near_ref, far_ref, beside_ref, send_ref):
    from_left = iota((tile, lanes), 1) % 4 < 2
    even_place = lax.axis_index("ly") % 2 == 0
    for group in range(parts + 1):
        near, far = near_ref[group], far_ref[group]
        beside_ref[group] = jnp.where(
            even_place, jnp.where(from_left, far, near), jnp.where(from_left, near, far)
        )
    count = outer_ref.shape[0]
    send_ref[:count] = outer_ref[...]
    first_row = iota((tile, lanes), 1) < 4 * (count // 2)
    send_ref[count] = jnp.where(first_row, beside_ref[0], beside_ref[parts - 1])


inverse = 1.0 / half_width


def sides(main, other):
    lane = iota(main.shape, 1)
    return pltpu.roll(jnp.where(lane == lanes - 1, other, main), 1, 1) + pltpu.roll(
        jnp.where(lane == 0, other, main), lanes - 1, 1
    )


def upward(row, above, below):
    even = iota(above.shape, 1) % 2 == row % 2
    return jnp.where(even, above, below)


def factor_at(ref, row, height):
    return jnp.broadcast_to(ref[pl.ds(row, 1), :], (height, lanes))


def inner_kernel(
    cols, rows, parts, early, start_ref, levels_ref, beside_ref, done_ref, next_ref, packed_ref, *refs
):
    field, edge, once, once_edge, factor, factor_edge = refs
    chunks = cols // tile
    part_rows = rows // parts
    factor[...] = site_factor(levels_ref[...].astype(jnp.float32))
    for k in range(rows // tile):
        factor_edge[k * tile : (k + 1) * tile, :] = site_factor(unpack_edges(beside_ref[parts], k))
    for row in range(rows):
        for chunk in range(chunks):
            part = pl.ds(chunk * tile, tile)
            field[row, part, :] = tile_at(start_ref, rows, row, chunk)
            edge[row, part, :] = unpack_edges(
                beside_ref[row // part_rows], row % part_rows * chunks + chunk
            )
    for row in range(rows):
        here, beside = field[row], edge[row]
        up, down = min(row + 1, rows - 1), max(row - 1, 0)
        once[row] = factor_at(factor, row, cols) * here - inverse * (
            sides(here, beside) + upward(row, field[up], field[down])
        )
        once_edge[row] = factor_at(factor_edge, row, cols) * beside - inverse * (
            sides(beside, here) + upward(row, edge[up], edge[down])
        )
    for row in range(1, rows - 1):
        here = once[row]
        twice = factor_at(factor, row, cols) * here - inverse * (
            sides(here, once_edge[row]) + upward(row, once[row + 1], once[row - 1])
        )
        done_ref[row] = 2.0 * twice - field[row]
    done_ref[0] = once[0]
    done_ref[rows - 1] = once[rows - 1]
    next_ref[0] = once[1]
    next_ref[1] = once[rows - 2]
    for at, k in enumerate(early):
        base = (lax.axis_index("col") ^ k) * part_rows
        packed_ref[at] = pack_edges(
            (row * chunks + chunk, done_ref[base + row, chunk * tile : (chunk + 1) * tile, :])
            for row in range(part_rows)
            for chunk in range(chunks)
        )


def outer_rows(cols, rows, start_ref, levels_ref, beside_ref, parts, before_ref, after_ref, next_ref):
    chunks = cols // tile
    part_rows = rows // parts

    def joined(tiles):
        return jnp.concatenate(list(tiles), axis=0)

    def field(row):
        return joined(tile_at(start_ref, rows, row, chunk) for chunk in range(chunks))

    def edge(row):
        return joined(
            unpack_edges(beside_ref[row // part_rows], row % part_rows * chunks + chunk)
            for chunk in range(chunks)
        )

    def factor(values):
        return jnp.broadcast_to(site_factor(values), (cols, lanes))

    for outer in (0, 1):
        if outer == 0:
            row, inside = 0, 1
            field_out = joined(before_ref[chunks + chunk] for chunk in range(chunks))
            edge_out = joined(
                unpack_edges(before_ref[2 * chunks + 1], (part_rows - 1) * chunks + chunk)
                for chunk in range(chunks)
            )
            factor_out = factor(before_ref[2 * chunks, 1:2, :])
        else:
            row, inside = rows - 1, rows - 2
            field_out = joined(after_ref[chunk] for chunk in range(chunks))
            edge_out = joined(
                unpack_edges(after_ref[2 * chunks + 1], chunk) for chunk in range(chunks)
            )
            factor_out = factor(after_ref[2 * chunks, 0:1, :])

        def vertical(within, without):
            return upward(row, *((within, without) if outer == 0 else (without, within)))

        here, beside = field(row), edge(row)
        here_factor = factor(levels_ref[row : row + 1, :].astype(jnp.float32))
        levels_edge = unpack_edges(beside_ref[parts], row // tile)
        edge_factor = factor(levels_edge[row % tile : row % tile + 1, :])
        once = here_factor * here - inverse * (
            sides(here, beside) + vertical(field(inside), field_out)
        )
        once_edge = edge_factor * beside - inverse * (
            sides(beside, here) + vertical(edge(inside), edge_out)
        )
        once_out = factor_out * field_out - inverse * (sides(field_out, edge_out) + here)
        twice = here_factor * once - inverse * (
            sides(once, once_edge) + vertical(next_ref[outer], once_out)
        )
        yield 2.0 * twice - here


def late_kernel(
    cols,
    rows,
    parts,
    early,
    order,
    start_ref,
    levels_ref,
    beside_ref,
    done_ref,
    next_ref,
    packed_ref,
    before_ref,
    after_ref,
    *out_refs,
):
    chunks = cols // tile
    part_rows = rows // parts
    first, last = outer_rows(
        cols, rows, start_ref, levels_ref, beside_ref, parts, before_ref, after_ref, next_ref
    )
    for k, out_ref in zip(order, out_refs):
        target = lax.axis_index("col") ^ k
        base = target * part_rows
        top = jnp.where(target == 0, first, done_ref[base])
        bottom = jnp.where(target == parts - 1, last, done_ref[base + part_rows - 1])
        if k not in early:
            out_ref[0] = top
            out_ref[1 : part_rows - 1] = done_ref[pl.ds(base + 1, part_rows - 2)]
            out_ref[part_rows - 1] = bottom
            continue
        for chunk in range(chunks):
            part = slice(chunk * tile, (chunk + 1) * tile)
            out_ref[chunk] = top[part]
            out_ref[chunks + chunk] = bottom[part]
        out_ref[2 * chunks] = packed_ref[early.index(k)]


def alone_kernel(cols, part_rows, levels_ref, raw_ref, out_ref, field, once, factor):
    factor[...] = site_factor(levels_ref[...].astype(jnp.float32))
    base = lax.axis_index("col") * part_rows
    for row in range(part_rows):
        field[row] = raw_ref[pl.ds(row, cols, stride=part_rows), :]
    for row in range(part_rows):
        above, below = field[min(row + 1, part_rows - 1)], field[max(row - 1, 0)]
        here = field[row]
        once[row] = factor_at(factor, base + row, cols) * here - inverse * (
            sides(here, here) + upward(row, above, below)
        )
    for row in range(part_rows):
        above, below = once[min(row + 1, part_rows - 1)], once[max(row - 1, 0)]
        here = once[row]
        twice = factor_at(factor, base + row, cols) * here - inverse * (
            sides(here, here) + upward(row, above, below)
        )
        out_ref[row] = 2.0 * twice - field[row]


def gram_kernel(cols, parts, early, order, *refs):
    late_refs, refs = dict(zip(order, refs)), refs[parts:]
    alone_refs = dict(zip(early, refs))
    whole_ref, gram_ref = refs[len(early) :]
    chunks = cols // tile
    part_rows = whole_ref.shape[0]
    total = cols * parts
    place = lax.axis_index("col")
    lane = iota((cols, lanes), 1)
    outer_lanes = (lane < 2) | (lane >= lanes - 2)
    for k in range(parts):
        part = pl.ds(pl.multiple_of((place ^ k) * cols, tile), cols)
        late_ref = late_refs[k]
        if k not in early:
            whole_ref[:, part, :] = late_ref[...]
            continue
        packed = late_ref[2 * chunks]
        for row in range(part_rows):
            if row in (0, part_rows - 1):
                at = 0 if row == 0 else chunks
                sent = [late_ref[at + chunk] for chunk in range(chunks)]
                whole_ref[row, part, :] = jnp.concatenate(sent, axis=0)
            else:
                sent = [unpack_edges(packed, row * chunks + chunk) for chunk in range(chunks)]
                whole_ref[row, part, :] = jnp.where(
                    outer_lanes, jnp.concatenate(sent, axis=0), alone_refs[k][row]
                )
    products = jnp.zeros((3 * total, 3 * total), jnp.float32)
    for row in range(0, part_rows, 2):
        values = jnp.concatenate([whole_ref[row], whole_ref[row + 1]], axis=1)
        stack = jnp.concatenate(split(values), axis=0)
        products += lax.dot_general(
            stack, stack, (((1,), (1,)), ((), ())), preferred_element_type=jnp.float32
        )
    gram = jnp.zeros((total, total), jnp.float32)
    for i in reversed(range(3)):
        for j in reversed(range(3)):
            gram += products[i * total : (i + 1) * total, j * total : (j + 1) * total]
    half = total // 2
    gram_ref[...] = jnp.concatenate([gram[:half], gram[half:]], axis=1)


def split(values):
    high = values.astype(jnp.bfloat16)
    rest = values - high.astype(jnp.float32)
    middle = rest.astype(jnp.bfloat16)
    low = (rest - middle.astype(jnp.float32)).astype(jnp.bfloat16)
    return high, middle, low


def eliminate(work, b, columns_ref, rows_ref):
    shape = (tile, lanes)
    sub = iota(shape, 0)

    def spread(ref, *place):
        return jnp.broadcast_to(ref[(*place[:-1], pl.ds(place[-1], 1), slice(None))], shape)

    column = [
        [jnp.broadcast_to(rows[:, b * tile + m : b * tile + m + 1], shape) for m in range(tile)]
        for rows in work[b:]
    ]
    slot = b % 2
    for m in range(tile):
        columns_ref[slot, m] = column[0][m]
    rows_ref[slot] = work[b]
    factor = {(p, q): spread(columns_ref, slot, q, p) for p in range(tile) for q in range(p + 1)}
    pivots = [spread(rows_ref, slot, m) for m in range(tile)]
    roots = []
    for m in range(tile):
        roots.append(lax.rsqrt(factor[m, m]))
        for p in range(m + 1, tile):
            factor[p, m] = factor[p, m] * roots[m]
        for p in range(m + 1, tile):
            for q in range(m + 1, p + 1):
                factor[p, q] = factor[p, q] - factor[p, m] * factor[q, m]
    for m in range(tile):
        for p in range(m):
            pivots[m] = pivots[m] - factor[m, p] * pivots[p]
        pivots[m] = pivots[m] * roots[m]
    for m in range(tile):
        work[b] = jnp.where(sub == m, pivots[m], work[b])
    for i in range(b + 1, len(work)):
        ratio = column[i - b]
        for m in range(tile):
            for p in range(m):
                ratio[m] = ratio[m] - ratio[p] * factor[m, p]
            ratio[m] = ratio[m] * roots[m]
            work[i] = work[i] - ratio[m] * pivots[m]


def solve_kernel(
    scale, holder, whole_ref, gram_ref, other_ref, out_hbm, out_ref, columns_ref, rows_ref, copied
):
    part_rows, total, _ = whole_ref.shape
    blocks = total // tile
    half = total // 2
    holds = lax.axis_index("ly") % 2 == holder
    packed = jnp.where(holds, gram_ref[...], other_ref[...])
    lane = iota((tile, lanes), 1)
    sub = iota((tile, lanes), 0)
    work = []
    for i in range(blocks):
        at = i * tile % half
        block = packed[at : at + tile, :]
        if i * tile >= half:
            block = pltpu.roll(block, total, 1)
        unit = jnp.where(lane - total == sub + i * tile, 1.0, 0.0)
        work.append(jnp.where(lane < total, block, unit))
    copies = []
    cuts = (0, 3 * blocks // 4, blocks)
    for part, (first, last) in enumerate(zip(cuts, cuts[1:])):
        for b in range(first, last):
            eliminate(work, b, columns_ref, rows_ref)
        solver = jnp.concatenate(work[first:last], axis=0) * scale
        wide = iota(solver.shape, 1)
        high, middle, low = (piece.astype(jnp.float32) for piece in split(solver))

        def pair(left, right):
            return jnp.where(wide < total, pltpu.roll(left, total, 1), right).astype(jnp.bfloat16)

        left_main = jnp.concatenate([pair(high, high), pair(middle, middle)], axis=1)
        left_rest = pair(high, low)
        height = (last - first) * tile
        base = first * tile * part_rows
        for row in range(0, part_rows, 2):
            values = jnp.concatenate([whole_ref[row], whole_ref[row + 1]], axis=1)
            f_high, f_middle, f_low = split(values)
            right_main = jnp.concatenate([f_high, f_middle, f_high, f_middle], axis=0)
            right_rest = jnp.concatenate([f_low, f_high], axis=0)
            result = jnp.dot(left_rest, right_rest, preferred_element_type=jnp.float32) + jnp.dot(
                left_main, right_main, preferred_element_type=jnp.float32
            )
            out_ref[pl.ds(base + row, height, stride=part_rows), :] = result[:, :lanes]
            out_ref[pl.ds(base + row + 1, height, stride=part_rows), :] = result[:, lanes:]
        span = pl.ds(base, height * part_rows)
        copies.append(pltpu.make_async_copy(out_ref.at[span], out_hbm.at[span], copied.at[part]))
        copies[-1].start()
    for copy in copies:
        copy.wait()


def call(kernel, outs, *operands, scratch=(), limit=32, **specs):
    return pl.pallas_call(
        kernel,
        out_shape=[
            jax.ShapeDtypeStruct(shape, jnp.float32) if isinstance(shape, tuple) else shape
            for shape in outs
        ],
        scratch_shapes=[
            pltpu.VMEM(shape, jnp.float32) if isinstance(shape, tuple) else shape
            for shape in scratch
        ],
        compiler_params=pltpu.CompilerParams(vmem_limit_bytes=limit * 1024 * 1024),
        **specs,
    )(*operands)


def exchange(values, axis, distance):
    count = lax.axis_size(axis)
    return lax.ppermute(values, axis, [(i, i ^ distance) for i in range(count)])


axes = ("lx", "ly", "col")


def pair_steps():
    steps = []
    for axis in ("ly", "lx", "col"):
        bit = 2 if axis == "ly" else 1
        while bit < lax.axis_size(axis):
            steps.append((axis, bit))
            bit *= 2
    return steps


def handover(holder, axis, bit):
    sizes = [lax.axis_size(name) for name in axes]
    pairs = []
    for at, (x, y, z) in enumerate(itertools.product(*map(range, sizes))):
        to = {"lx": x, "ly": y ^ 1, "col": z}
        if y % 2 == holder:
            to[axis] ^= bit
        pairs.append((at, (to["lx"] * sizes[1] + to["ly"]) * sizes[2] + to["col"]))
    return pairs


def shards(start, levels):
    cols, rows, _ = start.shape
    parts = lax.axis_size("col")
    chunks = cols // tile
    total = cols * parts
    part_rows = rows // parts
    sizes = (cols, rows, parts)
    early = (parts - 1,)
    order = (*sorted(range(1, parts), key=lambda k: (k in early, -k)), 0)
    flat = start.reshape(cols * rows, lanes)
    piece = (part_rows, cols, lanes)
    start_here, levels_here, edges, outer, *raws = call(
        functools.partial(pack_kernel, *sizes, early),
        [flat.shape, jax.ShapeDtypeStruct(levels.shape, levels.dtype), (parts + 1, tile, lanes), (2 * chunks + 1, tile, lanes)]
        + [(cols, part_rows, lanes)] * len(early),
        pltpu.with_memory_space_constraint(flat, pltpu.HBM),
        pltpu.with_memory_space_constraint(levels, pltpu.HBM),
        pltpu.with_memory_space_constraint(start, pltpu.HBM),
        scratch=[pltpu.SemaphoreType.DMA((chunks + 1 + len(early),))],
        limit=32,
        in_specs=[pl.BlockSpec(memory_space=pl.ANY)] * 3,
    )
    count = lax.axis_size("ly")
    near = exchange(edges, "ly", 1)
    far_pairs = [(i, (i + 1) % count if i % 2 else (i - 1) % count) for i in range(count)]
    far = lax.ppermute(edges, "ly", far_pairs)
    raws = [exchange(values, "col", k) for k, values in zip(early, raws)]
    beside, outer = call(
        functools.partial(outer_kernel, parts),
        [(parts + 1, tile, lanes), (2 * chunks + 2, tile, lanes)],
        outer,
        near,
        far,
    )
    count = lax.axis_size("lx")
    before = lax.ppermute(outer, "lx", [(i, (i + 1) % count) for i in range(count)])
    after = before
    if count > 2:
        after = lax.ppermute(outer, "lx", [((i + 1) % count, i) for i in range(count)])
    inner = call(
        functools.partial(inner_kernel, *sizes, early),
        [(rows, cols, lanes), (2, cols, lanes), (len(early), tile, lanes)],
        start_here,
        levels_here,
        beside,
        scratch=[(rows, cols, lanes)] * 4 + [(rows, lanes)] * 2,
        cost_estimate=pl.CostEstimate(flops=10**11, bytes_accessed=10**9, transcendentals=0),
    )
    lates = call(
        functools.partial(late_kernel, *sizes, early, order),
        [(2 * chunks + 1, tile, lanes) if k in early else piece for k in order],
        start_here,
        levels_here,
        beside,
        *inner,
        before,
        after,
    )
    lates = [exchange(values, "col", k) if k else values for k, values in zip(order, lates)]
    alones = [
        call(
            functools.partial(alone_kernel, cols, part_rows),
            [piece],
            levels_here,
            raw.reshape(cols * part_rows, lanes),
            scratch=[piece, piece, (rows, lanes)],
            cost_estimate=pl.CostEstimate(flops=0, bytes_accessed=10**6, transcendentals=0),
        )[0]
        for raw in raws
    ]
    whole, gram = call(
        functools.partial(gram_kernel, cols, parts, early, order),
        [(part_rows, total, lanes), (total // 2, 2 * total)],
        *lates,
        *alones,
    )
    gram = gram + exchange(gram, "ly", 1)
    holder = 0
    for axis, bit in pair_steps():
        near = exchange(gram, "ly", 1)
        gram = near + lax.ppermute(gram, axes, handover(holder, axis, bit))
        holder = 1 - holder
    scale = math.sqrt(rows * lax.axis_size("lx") * lanes * lax.axis_size("ly"))
    (basis,) = call(
        functools.partial(solve_kernel, scale, holder),
        [(total * part_rows, lanes)],
        whole,
        gram,
        exchange(gram, "ly", 1),
        scratch=[
            (total * part_rows, lanes),
            (2, tile, tile, lanes),
            (2, tile, lanes),
            pltpu.SemaphoreType.DMA((2,)),
        ],
        out_specs=[pl.BlockSpec(memory_space=pl.ANY)],
    )
    return basis.reshape(total, part_rows, lanes)


def solution(mesh):
    placed = (P("col", "lx", "ly"), P("lx", "ly"))
    return jax.shard_map(
        shards, mesh=mesh, in_specs=placed, out_specs=P(None, ("lx", "col"), "ly"), check_vma=False
    )
```

```python
import functools
import itertools
import math

import jax
import jax.numpy as jnp
from jax import lax
from jax.experimental import pallas as pl
from jax.experimental.pallas import tpu as pltpu
from jax.sharding import PartitionSpec as P

center = 2.1
half_width = 3.1
spread_width = 4.0
level_top = 15.0
lanes = 128
tile = 8


def iota(shape, dim):
    return lax.broadcasted_iota(jnp.int32, shape, dim)


def site_factor(levels):
    onsite = spread_width * (levels / level_top - 0.5)
    return (onsite - center) / half_width


def tile_at(ref, rows, row, chunk):
    return ref[pl.ds(chunk * tile * rows + row, tile, stride=rows), :]


def pack_edges(tiles):
    lane = iota((tile, lanes), 1)
    packed = jnp.zeros((tile, lanes), jnp.float32)
    for k, values in tiles:
        moved = pltpu.roll(values, (4 * k + 2) % lanes, 1)
        packed = jnp.where(lane // 4 == k, moved, packed)
    return packed


def unpack_edges(packed, k):
    return pltpu.roll(packed, lanes - (4 * k + 2), 1)


def pack_kernel(
    cols,
    rows,
    parts,
    early,
    start_hbm,
    levels_hbm,
    whole_hbm,
    start_ref,
    levels_ref,
    edges_ref,
    outer_ref,
    *refs,
):
    piece_refs, (arrived,) = refs[: len(early)], refs[len(early) :]
    chunks = cols // tile
    part_rows = rows // parts
    span = tile * rows
    copies = [pltpu.make_async_copy(levels_hbm, levels_ref, arrived.at[chunks])] + [
        pltpu.make_async_copy(
            start_hbm.at[pl.ds(chunk * span, span)],
            start_ref.at[pl.ds(chunk * span, span)],
            arrived.at[chunk],
        )
        for chunk in range(chunks)
    ]
    for at, (k, piece_ref) in enumerate(zip(early, piece_refs)):
        base = pl.multiple_of((lax.axis_index("col") ^ k) * part_rows, part_rows)
        copies.append(
            pltpu.make_async_copy(
                whole_hbm.at[:, pl.ds(base, part_rows), :], piece_ref, arrived.at[chunks + 1 + at]
            )
        )
    for copy in copies:
        copy.start()
    copies[0].wait()
    edges_ref[parts] = pack_edges(
        (k, levels_ref[k * tile : (k + 1) * tile, :].astype(jnp.float32))
        for k in range(rows // tile)
    )
    first = levels_ref[0:1, :].astype(jnp.float32)
    last = levels_ref[rows - 1 : rows, :].astype(jnp.float32)
    outer_ref[2 * chunks] = jnp.where(iota((tile, lanes), 0) == 0, first, last)
    for chunk in range(chunks):
        copies[1 + chunk].wait()
        outer_ref[chunk] = tile_at(start_ref, rows, 0, chunk)
        outer_ref[chunks + chunk] = tile_at(start_ref, rows, rows - 1, chunk)
        for group in range(parts):
            packed = pack_edges(
                (row * chunks + chunk, tile_at(start_ref, rows, group * part_rows + row, chunk))
                for row in range(part_rows)
            )
            edges_ref[group] = packed if chunk == 0 else edges_ref[group] + packed
    for copy in copies[1 + chunks :]:
        copy.wait()


def outer_kernel(parts, outer_ref, near_ref, far_ref, beside_ref, send_ref):
    from_left = iota((tile, lanes), 1) % 4 < 2
    even_place = lax.axis_index("ly") % 2 == 0
    for group in range(parts + 1):
        near, far = near_ref[group], far_ref[group]
        beside_ref[group] = jnp.where(
            even_place, jnp.where(from_left, far, near), jnp.where(from_left, near, far)
        )
    count = outer_ref.shape[0]
    send_ref[:count] = outer_ref[...]
    first_row = iota((tile, lanes), 1) < 4 * (count // 2)
    send_ref[count] = jnp.where(first_row, beside_ref[0], beside_ref[parts - 1])


inverse = 1.0 / half_width


def sides(main, other):
    lane = iota(main.shape, 1)
    return pltpu.roll(jnp.where(lane == lanes - 1, other, main), 1, 1) + pltpu.roll(
        jnp.where(lane == 0, other, main), lanes - 1, 1
    )


def upward(row, above, below):
    even = iota(above.shape, 1) % 2 == row % 2
    return jnp.where(even, above, below)


def factor_at(ref, row, height):
    return jnp.broadcast_to(ref[pl.ds(row, 1), :], (height, lanes))


def inner_kernel(
    cols, rows, parts, early, start_ref, levels_ref, beside_ref, done_ref, next_ref, packed_ref, *refs
):
    field, edge, once, once_edge, factor, factor_edge = refs
    chunks = cols // tile
    part_rows = rows // parts
    factor[...] = site_factor(levels_ref[...].astype(jnp.float32))
    for k in range(rows // tile):
        factor_edge[k * tile : (k + 1) * tile, :] = site_factor(unpack_edges(beside_ref[parts], k))
    for row in range(rows):
        for chunk in range(chunks):
            part = pl.ds(chunk * tile, tile)
            field[row, part, :] = tile_at(start_ref, rows, row, chunk)
            edge[row, part, :] = unpack_edges(
                beside_ref[row // part_rows], row % part_rows * chunks + chunk
            )
    for row in range(rows):
        here, beside = field[row], edge[row]
        up, down = min(row + 1, rows - 1), max(row - 1, 0)
        once[row] = factor_at(factor, row, cols) * here - inverse * (
            sides(here, beside) + upward(row, field[up], field[down])
        )
        once_edge[row] = factor_at(factor_edge, row, cols) * beside - inverse * (
            sides(beside, here) + upward(row, edge[up], edge[down])
        )
    for row in range(1, rows - 1):
        here = once[row]
        twice = factor_at(factor, row, cols) * here - inverse * (
            sides(here, once_edge[row]) + upward(row, once[row + 1], once[row - 1])
        )
        done_ref[row] = 2.0 * twice - field[row]
    done_ref[0] = once[0]
    done_ref[rows - 1] = once[rows - 1]
    next_ref[0] = once[1]
    next_ref[1] = once[rows - 2]
    for at, k in enumerate(early):
        base = (lax.axis_index("col") ^ k) * part_rows
        packed_ref[at] = pack_edges(
            (row * chunks + chunk, done_ref[base + row, chunk * tile : (chunk + 1) * tile, :])
            for row in range(part_rows)
            for chunk in range(chunks)
        )


def outer_rows(cols, rows, start_ref, levels_ref, beside_ref, parts, before_ref, after_ref, next_ref):
    chunks = cols // tile
    part_rows = rows // parts

    def joined(tiles):
        return jnp.concatenate(list(tiles), axis=0)

    def field(row):
        return joined(tile_at(start_ref, rows, row, chunk) for chunk in range(chunks))

    def edge(row):
        return joined(
            unpack_edges(beside_ref[row // part_rows], row % part_rows * chunks + chunk)
            for chunk in range(chunks)
        )

    def factor(values):
        return jnp.broadcast_to(site_factor(values), (cols, lanes))

    for outer in (0, 1):
        if outer == 0:
            row, inside = 0, 1
            field_out = joined(before_ref[chunks + chunk] for chunk in range(chunks))
            edge_out = joined(
                unpack_edges(before_ref[2 * chunks + 1], (part_rows - 1) * chunks + chunk)
                for chunk in range(chunks)
            )
            factor_out = factor(before_ref[2 * chunks, 1:2, :])
        else:
            row, inside = rows - 1, rows - 2
            field_out = joined(after_ref[chunk] for chunk in range(chunks))
            edge_out = joined(
                unpack_edges(after_ref[2 * chunks + 1], chunk) for chunk in range(chunks)
            )
            factor_out = factor(after_ref[2 * chunks, 0:1, :])

        def vertical(within, without):
            return upward(row, *((within, without) if outer == 0 else (without, within)))

        here, beside = field(row), edge(row)
        here_factor = factor(levels_ref[row : row + 1, :].astype(jnp.float32))
        levels_edge = unpack_edges(beside_ref[parts], row // tile)
        edge_factor = factor(levels_edge[row % tile : row % tile + 1, :])
        once = here_factor * here - inverse * (
            sides(here, beside) + vertical(field(inside), field_out)
        )
        once_edge = edge_factor * beside - inverse * (
            sides(beside, here) + vertical(edge(inside), edge_out)
        )
        once_out = factor_out * field_out - inverse * (sides(field_out, edge_out) + here)
        twice = here_factor * once - inverse * (
            sides(once, once_edge) + vertical(next_ref[outer], once_out)
        )
        yield 2.0 * twice - here


def late_kernel(
    cols,
    rows,
    parts,
    early,
    order,
    start_ref,
    levels_ref,
    beside_ref,
    done_ref,
    next_ref,
    packed_ref,
    before_ref,
    after_ref,
    *out_refs,
):
    chunks = cols // tile
    part_rows = rows // parts
    first, last = outer_rows(
        cols, rows, start_ref, levels_ref, beside_ref, parts, before_ref, after_ref, next_ref
    )
    for k, out_ref in zip(order, out_refs):
        target = lax.axis_index("col") ^ k
        base = target * part_rows
        top = jnp.where(target == 0, first, done_ref[base])
        bottom = jnp.where(target == parts - 1, last, done_ref[base + part_rows - 1])
        if k not in early:
            out_ref[0] = top
            out_ref[1 : part_rows - 1] = done_ref[pl.ds(base + 1, part_rows - 2)]
            out_ref[part_rows - 1] = bottom
            continue
        for chunk in range(chunks):
            part = slice(chunk * tile, (chunk + 1) * tile)
            out_ref[chunk] = top[part]
            out_ref[chunks + chunk] = bottom[part]
        out_ref[2 * chunks] = packed_ref[early.index(k)]


def alone_kernel(cols, part_rows, levels_ref, raw_ref, out_ref, field, once, factor):
    factor[...] = site_factor(levels_ref[...].astype(jnp.float32))
    base = lax.axis_index("col") * part_rows
    for row in range(part_rows):
        field[row] = raw_ref[pl.ds(row, cols, stride=part_rows), :]
    for row in range(part_rows):
        above, below = field[min(row + 1, part_rows - 1)], field[max(row - 1, 0)]
        here = field[row]
        once[row] = factor_at(factor, base + row, cols) * here - inverse * (
            sides(here, here) + upward(row, above, below)
        )
    for row in range(part_rows):
        above, below = once[min(row + 1, part_rows - 1)], once[max(row - 1, 0)]
        here = once[row]
        twice = factor_at(factor, base + row, cols) * here - inverse * (
            sides(here, here) + upward(row, above, below)
        )
        out_ref[row] = 2.0 * twice - field[row]


def gram_kernel(cols, parts, early, order, *refs):
    late_refs, refs = dict(zip(order, refs)), refs[parts:]
    alone_refs = dict(zip(early, refs))
    whole_ref, gram_ref = refs[len(early) :]
    chunks = cols // tile
    part_rows = whole_ref.shape[0]
    total = cols * parts
    place = lax.axis_index("col")
    lane = iota((cols, lanes), 1)
    outer_lanes = (lane < 2) | (lane >= lanes - 2)
    for k in range(parts):
        part = pl.ds(pl.multiple_of((place ^ k) * cols, tile), cols)
        late_ref = late_refs[k]
        if k not in early:
            whole_ref[:, part, :] = late_ref[...]
            continue
        packed = late_ref[2 * chunks]
        for row in range(part_rows):
            if row in (0, part_rows - 1):
                at = 0 if row == 0 else chunks
                sent = [late_ref[at + chunk] for chunk in range(chunks)]
                whole_ref[row, part, :] = jnp.concatenate(sent, axis=0)
            else:
                sent = [unpack_edges(packed, row * chunks + chunk) for chunk in range(chunks)]
                whole_ref[row, part, :] = jnp.where(
                    outer_lanes, jnp.concatenate(sent, axis=0), alone_refs[k][row]
                )
    products = jnp.zeros((3 * total, 3 * total), jnp.float32)
    for row in range(0, part_rows, 2):
        values = jnp.concatenate([whole_ref[row], whole_ref[row + 1]], axis=1)
        stack = jnp.concatenate(split(values), axis=0)
        products += lax.dot_general(
            stack, stack, (((1,), (1,)), ((), ())), preferred_element_type=jnp.float32
        )
    gram = jnp.zeros((total, total), jnp.float32)
    for i in reversed(range(3)):
        for j in reversed(range(3)):
            gram += products[i * total : (i + 1) * total, j * total : (j + 1) * total]
    half = total // 2
    gram_ref[...] = jnp.concatenate([gram[:half], gram[half:]], axis=1)


def split(values):
    high = values.astype(jnp.bfloat16)
    rest = values - high.astype(jnp.float32)
    middle = rest.astype(jnp.bfloat16)
    low = (rest - middle.astype(jnp.float32)).astype(jnp.bfloat16)
    return high, middle, low


def split_kernel(whole_ref, main_ref, rest_ref):
    for pair in range(whole_ref.shape[0] // 2):
        values = jnp.concatenate([whole_ref[2 * pair], whole_ref[2 * pair + 1]], axis=1)
        high, middle, low = split(values)
        main_ref[pair] = jnp.concatenate([high, middle], axis=0)
        rest_ref[pair] = jnp.concatenate([low, high], axis=0)


def eliminate(work, b, columns_ref, rows_ref):
    shape = (tile, lanes)
    sub = iota(shape, 0)

    def spread(ref, *place):
        return jnp.broadcast_to(ref[(*place[:-1], pl.ds(place[-1], 1), slice(None))], shape)

    column = [
        [jnp.broadcast_to(rows[:, b * tile + m : b * tile + m + 1], shape) for m in range(tile)]
        for rows in work[b:]
    ]
    slot = b % 2
    for m in range(tile):
        columns_ref[slot, m] = column[0][m]
    rows_ref[slot] = work[b]
    factor = {(p, q): spread(columns_ref, slot, q, p) for p in range(tile) for q in range(p + 1)}
    pivots = [spread(rows_ref, slot, m) for m in range(tile)]
    roots = []
    for m in range(0, tile, 2):
        n = m + 1
        first, cross = factor[m, m], factor[n, m]
        roots.append(lax.rsqrt(first))
        both = lax.rsqrt(first * factor[n, n] - cross * cross)
        roots.append(both * (first * roots[m]))
        both = both * roots[m]
        factor[n, m] = cross * roots[m]
        for p in range(n + 1, tile):
            factor[p, n] = (factor[p, n] * first - factor[p, m] * cross) * both
            factor[p, m] = factor[p, m] * roots[m]
        for p in range(n + 1, tile):
            for q in range(n + 1, p + 1):
                factor[p, q] = (
                    factor[p, q] - factor[p, m] * factor[q, m] - factor[p, n] * factor[q, n]
                )
    for m in range(tile):
        for p in range(m):
            pivots[m] = pivots[m] - factor[m, p] * pivots[p]
        pivots[m] = pivots[m] * roots[m]
    for m in range(tile):
        work[b] = jnp.where(sub == m, pivots[m], work[b])
    for i in range(b + 1, len(work)):
        ratio = column[i - b]
        for m in range(tile):
            for p in range(m):
                ratio[m] = ratio[m] - ratio[p] * factor[m, p]
            ratio[m] = ratio[m] * roots[m]
            work[i] = work[i] - ratio[m] * pivots[m]


def solve_kernel(
    scale, holder, main_ref, rest_ref, gram_ref, other_ref, out_hbm, out_ref, columns_ref, rows_ref, copied
):
    part_rows, total = 2 * main_ref.shape[0], main_ref.shape[1] // 2
    blocks = total // tile
    half = total // 2
    holds = lax.axis_index("ly") % 2 == holder
    packed = jnp.where(holds, gram_ref[...], other_ref[...])
    lane = iota((tile, lanes), 1)
    sub = iota((tile, lanes), 0)
    work = []
    diagonal = []
    for i in range(blocks):
        at = i * tile % half
        block = packed[at : at + tile, :]
        if i * tile >= half:
            block = pltpu.roll(block, total, 1)
        work.append(block)
        diagonal.append(jnp.where(lane == sub + i * tile, block, 0.0))
    across = jnp.sum(sum(diagonal), axis=0, keepdims=True)
    across = lax.rsqrt(jnp.where(lane[:1] < total, across, 1.0))
    for i in range(blocks):
        down = lax.rsqrt(jnp.sum(diagonal[i], axis=1, keepdims=True))
        unit = jnp.where(lane - total == sub + i * tile, down, 0.0)
        work[i] = jnp.where(lane < total, work[i] * down * across, unit)
    copies = []
    cuts = (0, 3 * blocks // 4, blocks)
    for part, (first, last) in enumerate(zip(cuts, cuts[1:])):
        for b in range(first, last):
            eliminate(work, b, columns_ref, rows_ref)
        solver = jnp.concatenate(work[first:last], axis=0) * scale
        wide = iota(solver.shape, 1)
        high, middle, low = (piece.astype(jnp.float32) for piece in split(solver))

        def pair(left, right):
            return jnp.where(wide < total, pltpu.roll(left, total, 1), right).astype(jnp.bfloat16)

        left_main = jnp.concatenate([pair(high, high), pair(middle, middle)], axis=1)
        left_rest = pair(high, low)
        height = (last - first) * tile
        base = first * tile * part_rows
        for row in range(0, part_rows, 2):
            right_main = jnp.concatenate([main_ref[row // 2], main_ref[row // 2]], axis=0)
            right_rest = rest_ref[row // 2]
            result = jnp.dot(left_rest, right_rest, preferred_element_type=jnp.float32) + jnp.dot(
                left_main, right_main, preferred_element_type=jnp.float32
            )
            out_ref[pl.ds(base + row, height, stride=part_rows), :] = result[:, :lanes]
            out_ref[pl.ds(base + row + 1, height, stride=part_rows), :] = result[:, lanes:]
        span = pl.ds(base, height * part_rows)
        copies.append(pltpu.make_async_copy(out_ref.at[span], out_hbm.at[span], copied.at[part]))
        copies[-1].start()
    for copy in copies:
        copy.wait()


def call(kernel, outs, *operands, scratch=(), limit=32, **specs):
    return pl.pallas_call(
        kernel,
        out_shape=[
            jax.ShapeDtypeStruct(shape, jnp.float32) if isinstance(shape, tuple) else shape
            for shape in outs
        ],
        scratch_shapes=[
            pltpu.VMEM(shape, jnp.float32) if isinstance(shape, tuple) else shape
            for shape in scratch
        ],
        compiler_params=pltpu.CompilerParams(vmem_limit_bytes=limit * 1024 * 1024),
        **specs,
    )(*operands)


def exchange(values, axis, distance):
    count = lax.axis_size(axis)
    return lax.ppermute(values, axis, [(i, i ^ distance) for i in range(count)])


axes = ("lx", "ly", "col")


def pair_steps():
    steps = []
    for axis in ("ly", "lx", "col"):
        bit = 2 if axis == "ly" else 1
        while bit < lax.axis_size(axis):
            steps.append((axis, bit))
            bit *= 2
    return steps


def handover(holder, axis, bit):
    sizes = [lax.axis_size(name) for name in axes]
    pairs = []
    for at, (x, y, z) in enumerate(itertools.product(*map(range, sizes))):
        to = {"lx": x, "ly": y ^ 1, "col": z}
        if y % 2 == holder:
            to[axis] ^= bit
        pairs.append((at, (to["lx"] * sizes[1] + to["ly"]) * sizes[2] + to["col"]))
    return pairs


def shards(start, levels):
    cols, rows, _ = start.shape
    parts = lax.axis_size("col")
    chunks = cols // tile
    total = cols * parts
    part_rows = rows // parts
    sizes = (cols, rows, parts)
    early = (parts - 1,)
    order = (*sorted(range(1, parts), key=lambda k: (k in early, -k)), 0)
    flat = start.reshape(cols * rows, lanes)
    piece = (part_rows, cols, lanes)
    start_here, levels_here, edges, outer, *raws = call(
        functools.partial(pack_kernel, *sizes, early),
        [flat.shape, jax.ShapeDtypeStruct(levels.shape, levels.dtype), (parts + 1, tile, lanes), (2 * chunks + 1, tile, lanes)]
        + [(cols, part_rows, lanes)] * len(early),
        pltpu.with_memory_space_constraint(flat, pltpu.HBM),
        pltpu.with_memory_space_constraint(levels, pltpu.HBM),
        pltpu.with_memory_space_constraint(start, pltpu.HBM),
        scratch=[pltpu.SemaphoreType.DMA((chunks + 1 + len(early),))],
        limit=32,
        in_specs=[pl.BlockSpec(memory_space=pl.ANY)] * 3,
    )
    count = lax.axis_size("ly")
    near = exchange(edges, "ly", 1)
    far_pairs = [(i, (i + 1) % count if i % 2 else (i - 1) % count) for i in range(count)]
    far = lax.ppermute(edges, "ly", far_pairs)
    raws = [exchange(values, "col", k) for k, values in zip(early, raws)]
    beside, outer = call(
        functools.partial(outer_kernel, parts),
        [(parts + 1, tile, lanes), (2 * chunks + 2, tile, lanes)],
        outer,
        near,
        far,
    )
    count = lax.axis_size("lx")
    before = lax.ppermute(outer, "lx", [(i, (i + 1) % count) for i in range(count)])
    after = before
    if count > 2:
        after = lax.ppermute(outer, "lx", [((i + 1) % count, i) for i in range(count)])
    inner = call(
        functools.partial(inner_kernel, *sizes, early),
        [(rows, cols, lanes), (2, cols, lanes), (len(early), tile, lanes)],
        start_here,
        levels_here,
        beside,
        scratch=[(rows, cols, lanes)] * 4 + [(rows, lanes)] * 2,
        cost_estimate=pl.CostEstimate(flops=10**11, bytes_accessed=10**9, transcendentals=0),
    )
    lates = call(
        functools.partial(late_kernel, *sizes, early, order),
        [(2 * chunks + 1, tile, lanes) if k in early else piece for k in order],
        start_here,
        levels_here,
        beside,
        *inner,
        before,
        after,
    )
    lates = [exchange(values, "col", k) if k else values for k, values in zip(order, lates)]
    alones = [
        call(
            functools.partial(alone_kernel, cols, part_rows),
            [piece],
            levels_here,
            raw.reshape(cols * part_rows, lanes),
            scratch=[piece, piece, (rows, lanes)],
            cost_estimate=pl.CostEstimate(flops=0, bytes_accessed=10**6, transcendentals=0),
        )[0]
        for raw in raws
    ]
    whole, gram = call(
        functools.partial(gram_kernel, cols, parts, early, order),
        [(part_rows, total, lanes), (total // 2, 2 * total)],
        *lates,
        *alones,
    )
    gram = gram + exchange(gram, "ly", 1)
    holder = 0
    for axis, bit in pair_steps():
        near = exchange(gram, "ly", 1)
        gram = near + lax.ppermute(gram, axes, handover(holder, axis, bit))
        holder = 1 - holder
    scale = math.sqrt(rows * lax.axis_size("lx") * lanes * lax.axis_size("ly"))
    halves = jax.ShapeDtypeStruct((part_rows // 2, 2 * total, 2 * lanes), jnp.bfloat16)
    split_whole = call(split_kernel, [halves, halves], whole)
    (basis,) = call(
        functools.partial(solve_kernel, scale, holder),
        [(total * part_rows, lanes)],
        *split_whole,
        gram,
        exchange(gram, "ly", 1),
        scratch=[
            (total * part_rows, lanes),
            (2, tile, tile, lanes),
            (2, tile, lanes),
            pltpu.SemaphoreType.DMA((2,)),
        ],
        out_specs=[pl.BlockSpec(memory_space=pl.ANY)],
    )
    return basis.reshape(total, part_rows, lanes)


def solution(mesh):
    placed = (P("col", "lx", "ly"), P("lx", "ly"))
    return jax.shard_map(
        shards, mesh=mesh, in_specs=placed, out_specs=P(None, ("lx", "col"), "ly"), check_vma=False
    )
```

```python
import functools
import itertools
import math

import jax
import jax.numpy as jnp
from jax import lax
from jax.experimental import pallas as pl
from jax.experimental.pallas import tpu as pltpu
from jax.sharding import PartitionSpec as P

center = 2.1
half_width = 3.1
spread_width = 4.0
level_top = 15.0
lanes = 128
tile = 8


def iota(shape, dim):
    return lax.broadcasted_iota(jnp.int32, shape, dim)


def site_factor(levels):
    onsite = spread_width * (levels / level_top - 0.5)
    return (onsite - center) / half_width


def tile_at(ref, rows, row, chunk):
    return ref[pl.ds(chunk * tile * rows + row, tile, stride=rows), :]


def pack_edges(tiles):
    lane = iota((tile, lanes), 1)
    packed = jnp.zeros((tile, lanes), jnp.float32)
    for k, values in tiles:
        moved = pltpu.roll(values, (4 * k + 2) % lanes, 1)
        packed = jnp.where(lane // 4 == k, moved, packed)
    return packed


def unpack_edges(packed, k):
    return pltpu.roll(packed, lanes - (4 * k + 2), 1)


def pack_kernel(
    cols,
    rows,
    parts,
    early,
    start_hbm,
    levels_hbm,
    whole_hbm,
    start_ref,
    levels_ref,
    edges_ref,
    half_ref,
    outer_ref,
    *refs,
):
    piece_refs, (arrived,) = refs[: len(early)], refs[len(early) :]
    chunks = cols // tile
    part_rows = rows // parts
    span = tile * rows
    copies = [pltpu.make_async_copy(levels_hbm, levels_ref, arrived.at[chunks])] + [
        pltpu.make_async_copy(
            start_hbm.at[pl.ds(chunk * span, span)],
            start_ref.at[pl.ds(chunk * span, span)],
            arrived.at[chunk],
        )
        for chunk in range(chunks)
    ]
    for at, (k, piece_ref) in enumerate(zip(early, piece_refs)):
        base = pl.multiple_of((lax.axis_index("col") ^ k) * part_rows, part_rows)
        copies.append(
            pltpu.make_async_copy(
                whole_hbm.at[:, pl.ds(base, part_rows), :], piece_ref, arrived.at[chunks + 1 + at]
            )
        )
    for copy in copies:
        copy.start()
    copies[0].wait()
    edges_ref[parts] = pack_edges(
        (k, levels_ref[k * tile : (k + 1) * tile, :].astype(jnp.float32))
        for k in range(rows // tile)
    )
    first = levels_ref[0:1, :].astype(jnp.float32)
    last = levels_ref[rows - 1 : rows, :].astype(jnp.float32)
    outer_ref[2 * chunks] = jnp.where(iota((tile, lanes), 0) == 0, first, last)
    for chunk in range(chunks):
        copies[1 + chunk].wait()
        outer_ref[chunk] = tile_at(start_ref, rows, 0, chunk)
        outer_ref[chunks + chunk] = tile_at(start_ref, rows, rows - 1, chunk)
        for group in range(parts):
            packed = pack_edges(
                (row * chunks + chunk, tile_at(start_ref, rows, group * part_rows + row, chunk))
                for row in range(part_rows)
            )
            edges_ref[group] = packed if chunk == 0 else edges_ref[group] + packed
    even_place = lax.axis_index("ly") % 2 == 0
    lower = iota((tile, lanes), 1) % 4 < 2
    for pair in range(parts // 2):
        left, right = edges_ref[2 * pair], edges_ref[2 * pair + 1]
        half_ref[pair] = jnp.where(
            even_place,
            jnp.where(lower, pltpu.roll(right, lanes - 2, 1), left),
            jnp.where(lower, left, pltpu.roll(right, 2, 1)),
        )
    half_ref[parts // 2] = edges_ref[parts]
    for copy in copies[1 + chunks :]:
        copy.wait()


def outer_kernel(parts, outer_ref, near_ref, far_ref, beside_ref, send_ref):
    from_left = iota((tile, lanes), 1) % 4 < 2
    even_place = lax.axis_index("ly") % 2 == 0
    for group in range(parts + 1):
        near, far = near_ref[group], far_ref[group // 2]
        if group % 2:
            far = jnp.where(even_place, pltpu.roll(far, lanes - 2, 1), pltpu.roll(far, 2, 1))
        beside_ref[group] = jnp.where(
            even_place, jnp.where(from_left, far, near), jnp.where(from_left, near, far)
        )
    count = outer_ref.shape[0]
    send_ref[:count] = outer_ref[...]
    first_row = iota((tile, lanes), 1) < 4 * (count // 2)
    send_ref[count] = jnp.where(first_row, beside_ref[0], beside_ref[parts - 1])


inverse = 1.0 / half_width


def sides(main, other):
    lane = iota(main.shape, 1)
    return pltpu.roll(jnp.where(lane == lanes - 1, other, main), 1, 1) + pltpu.roll(
        jnp.where(lane == 0, other, main), lanes - 1, 1
    )


def upward(row, above, below):
    even = iota(above.shape, 1) % 2 == row % 2
    return jnp.where(even, above, below)


def factor_at(ref, row, height):
    return jnp.broadcast_to(ref[pl.ds(row, 1), :], (height, lanes))


def inner_kernel(
    cols, rows, parts, early, start_ref, levels_ref, beside_ref, done_ref, next_ref, packed_ref, *refs
):
    field, edge, once, once_edge, factor, factor_edge = refs
    chunks = cols // tile
    part_rows = rows // parts
    factor[...] = site_factor(levels_ref[...].astype(jnp.float32))
    for k in range(rows // tile):
        factor_edge[k * tile : (k + 1) * tile, :] = site_factor(unpack_edges(beside_ref[parts], k))
    for row in range(rows):
        for chunk in range(chunks):
            part = pl.ds(chunk * tile, tile)
            field[row, part, :] = tile_at(start_ref, rows, row, chunk)
            edge[row, part, :] = unpack_edges(
                beside_ref[row // part_rows], row % part_rows * chunks + chunk
            )
    for row in range(rows):
        here, beside = field[row], edge[row]
        up, down = min(row + 1, rows - 1), max(row - 1, 0)
        once[row] = factor_at(factor, row, cols) * here - inverse * (
            sides(here, beside) + upward(row, field[up], field[down])
        )
        once_edge[row] = factor_at(factor_edge, row, cols) * beside - inverse * (
            sides(beside, here) + upward(row, edge[up], edge[down])
        )
    for row in range(1, rows - 1):
        here = once[row]
        twice = factor_at(factor, row, cols) * here - inverse * (
            sides(here, once_edge[row]) + upward(row, once[row + 1], once[row - 1])
        )
        done_ref[row] = 2.0 * twice - field[row]
    done_ref[0] = once[0]
    done_ref[rows - 1] = once[rows - 1]
    next_ref[0] = once[1]
    next_ref[1] = once[rows - 2]
    for at, k in enumerate(early):
        base = (lax.axis_index("col") ^ k) * part_rows
        packed_ref[at] = pack_edges(
            (row * chunks + chunk, done_ref[base + row, chunk * tile : (chunk + 1) * tile, :])
            for row in range(part_rows)
            for chunk in range(chunks)
        )


def outer_rows(cols, rows, start_ref, levels_ref, beside_ref, parts, before_ref, after_ref, next_ref):
    chunks = cols // tile
    part_rows = rows // parts

    def joined(tiles):
        return jnp.concatenate(list(tiles), axis=0)

    def field(row):
        return joined(tile_at(start_ref, rows, row, chunk) for chunk in range(chunks))

    def edge(row):
        return joined(
            unpack_edges(beside_ref[row // part_rows], row % part_rows * chunks + chunk)
            for chunk in range(chunks)
        )

    def factor(values):
        return jnp.broadcast_to(site_factor(values), (cols, lanes))

    for outer in (0, 1):
        if outer == 0:
            row, inside = 0, 1
            field_out = joined(before_ref[chunks + chunk] for chunk in range(chunks))
            edge_out = joined(
                unpack_edges(before_ref[2 * chunks + 1], (part_rows - 1) * chunks + chunk)
                for chunk in range(chunks)
            )
            factor_out = factor(before_ref[2 * chunks, 1:2, :])
        else:
            row, inside = rows - 1, rows - 2
            field_out = joined(after_ref[chunk] for chunk in range(chunks))
            edge_out = joined(
                unpack_edges(after_ref[2 * chunks + 1], chunk) for chunk in range(chunks)
            )
            factor_out = factor(after_ref[2 * chunks, 0:1, :])

        def vertical(within, without):
            return upward(row, *((within, without) if outer == 0 else (without, within)))

        here, beside = field(row), edge(row)
        here_factor = factor(levels_ref[row : row + 1, :].astype(jnp.float32))
        levels_edge = unpack_edges(beside_ref[parts], row // tile)
        edge_factor = factor(levels_edge[row % tile : row % tile + 1, :])
        once = here_factor * here - inverse * (
            sides(here, beside) + vertical(field(inside), field_out)
        )
        once_edge = edge_factor * beside - inverse * (
            sides(beside, here) + vertical(edge(inside), edge_out)
        )
        once_out = factor_out * field_out - inverse * (sides(field_out, edge_out) + here)
        twice = here_factor * once - inverse * (
            sides(once, once_edge) + vertical(next_ref[outer], once_out)
        )
        yield 2.0 * twice - here


def late_kernel(
    cols,
    rows,
    parts,
    early,
    order,
    start_ref,
    levels_ref,
    beside_ref,
    done_ref,
    next_ref,
    packed_ref,
    before_ref,
    after_ref,
    *out_refs,
):
    chunks = cols // tile
    part_rows = rows // parts
    first, last = outer_rows(
        cols, rows, start_ref, levels_ref, beside_ref, parts, before_ref, after_ref, next_ref
    )
    for k, out_ref in zip(order, out_refs):
        target = lax.axis_index("col") ^ k
        base = target * part_rows
        top = jnp.where(target == 0, first, done_ref[base])
        bottom = jnp.where(target == parts - 1, last, done_ref[base + part_rows - 1])
        if k not in early:
            out_ref[0] = top
            out_ref[1 : part_rows - 1] = done_ref[pl.ds(base + 1, part_rows - 2)]
            out_ref[part_rows - 1] = bottom
            continue
        for chunk in range(chunks):
            part = slice(chunk * tile, (chunk + 1) * tile)
            out_ref[chunk] = top[part]
            out_ref[chunks + chunk] = bottom[part]
        out_ref[2 * chunks] = packed_ref[early.index(k)]


def alone_kernel(cols, part_rows, levels_ref, raw_ref, out_ref, field, once, factor):
    factor[...] = site_factor(levels_ref[...].astype(jnp.float32))
    base = lax.axis_index("col") * part_rows
    for row in range(part_rows):
        field[row] = raw_ref[pl.ds(row, cols, stride=part_rows), :]
    for row in range(part_rows):
        above, below = field[min(row + 1, part_rows - 1)], field[max(row - 1, 0)]
        here = field[row]
        once[row] = factor_at(factor, base + row, cols) * here - inverse * (
            sides(here, here) + upward(row, above, below)
        )
    for row in range(part_rows):
        above, below = once[min(row + 1, part_rows - 1)], once[max(row - 1, 0)]
        here = once[row]
        twice = factor_at(factor, base + row, cols) * here - inverse * (
            sides(here, here) + upward(row, above, below)
        )
        out_ref[row] = 2.0 * twice - field[row]


def gram_kernel(cols, parts, early, order, *refs):
    late_refs, refs = dict(zip(order, refs)), refs[parts:]
    alone_refs = dict(zip(early, refs))
    whole_ref, gram_ref = refs[len(early) :]
    chunks = cols // tile
    part_rows = whole_ref.shape[0]
    total = cols * parts
    place = lax.axis_index("col")
    lane = iota((cols, lanes), 1)
    outer_lanes = (lane < 2) | (lane >= lanes - 2)
    for k in range(parts):
        part = pl.ds(pl.multiple_of((place ^ k) * cols, tile), cols)
        late_ref = late_refs[k]
        if k not in early:
            whole_ref[:, part, :] = late_ref[...]
            continue
        packed = late_ref[2 * chunks]
        for row in range(part_rows):
            if row in (0, part_rows - 1):
                at = 0 if row == 0 else chunks
                sent = [late_ref[at + chunk] for chunk in range(chunks)]
                whole_ref[row, part, :] = jnp.concatenate(sent, axis=0)
            else:
                sent = [unpack_edges(packed, row * chunks + chunk) for chunk in range(chunks)]
                whole_ref[row, part, :] = jnp.where(
                    outer_lanes, jnp.concatenate(sent, axis=0), alone_refs[k][row]
                )
    products = jnp.zeros((3 * total, 3 * total), jnp.float32)
    for row in range(0, part_rows, 2):
        values = jnp.concatenate([whole_ref[row], whole_ref[row + 1]], axis=1)
        stack = jnp.concatenate(split(values), axis=0)
        products += lax.dot_general(
            stack, stack, (((1,), (1,)), ((), ())), preferred_element_type=jnp.float32
        )
    gram = jnp.zeros((total, total), jnp.float32)
    for i in reversed(range(3)):
        for j in reversed(range(3)):
            gram += products[i * total : (i + 1) * total, j * total : (j + 1) * total]
    half = total // 2
    gram_ref[...] = jnp.concatenate([gram[:half], gram[half:]], axis=1)


def split(values):
    high = values.astype(jnp.bfloat16)
    rest = values - high.astype(jnp.float32)
    middle = rest.astype(jnp.bfloat16)
    low = (rest - middle.astype(jnp.float32)).astype(jnp.bfloat16)
    return high, middle, low


def split_kernel(whole_ref, main_ref, rest_ref):
    for pair in range(whole_ref.shape[0] // 2):
        values = jnp.concatenate([whole_ref[2 * pair], whole_ref[2 * pair + 1]], axis=1)
        high, middle, low = split(values)
        main_ref[pair] = jnp.concatenate([high, middle], axis=0)
        rest_ref[pair] = jnp.concatenate([low, high], axis=0)


def eliminate(work, b, columns_ref, rows_ref):
    shape = (tile, lanes)
    sub = iota(shape, 0)

    def spread(ref, *place):
        return jnp.broadcast_to(ref[(*place[:-1], pl.ds(place[-1], 1), slice(None))], shape)

    column = [
        [jnp.broadcast_to(rows[:, b * tile + m : b * tile + m + 1], shape) for m in range(tile)]
        for rows in work[b:]
    ]
    slot = b % 2
    for m in range(tile):
        columns_ref[slot, m] = column[0][m]
    rows_ref[slot] = work[b]
    factor = {(p, q): spread(columns_ref, slot, q, p) for p in range(tile) for q in range(p + 1)}
    pivots = [spread(rows_ref, slot, m) for m in range(tile)]
    roots = []
    for m in range(0, tile, 2):
        n = m + 1
        first, cross = factor[m, m], factor[n, m]
        roots.append(lax.rsqrt(first))
        both = lax.rsqrt(first * factor[n, n] - cross * cross)
        roots.append(both * (first * roots[m]))
        both = both * roots[m]
        factor[n, m] = cross * roots[m]
        for p in range(n + 1, tile):
            factor[p, n] = (factor[p, n] * first - factor[p, m] * cross) * both
            factor[p, m] = factor[p, m] * roots[m]
        for p in range(n + 1, tile):
            for q in range(n + 1, p + 1):
                factor[p, q] = (
                    factor[p, q] - factor[p, m] * factor[q, m] - factor[p, n] * factor[q, n]
                )
    for m in range(tile):
        for p in range(m):
            pivots[m] = pivots[m] - factor[m, p] * pivots[p]
        pivots[m] = pivots[m] * roots[m]
    for m in range(tile):
        work[b] = jnp.where(sub == m, pivots[m], work[b])
    for i in range(b + 1, len(work)):
        ratio = column[i - b]
        for m in range(tile):
            for p in range(m):
                ratio[m] = ratio[m] - ratio[p] * factor[m, p]
            ratio[m] = ratio[m] * roots[m]
            work[i] = work[i] - ratio[m] * pivots[m]


def solve_kernel(
    scale, holder, main_ref, rest_ref, gram_ref, other_ref, out_hbm, out_ref, columns_ref, rows_ref, copied
):
    part_rows, total = 2 * main_ref.shape[0], main_ref.shape[1] // 2
    blocks = total // tile
    half = total // 2
    holds = lax.axis_index("ly") % 2 == holder
    packed = jnp.where(holds, gram_ref[...], other_ref[...])
    lane = iota((tile, lanes), 1)
    sub = iota((tile, lanes), 0)
    work = []
    diagonal = []
    for i in range(blocks):
        at = i * tile % half
        block = packed[at : at + tile, :]
        if i * tile >= half:
            block = pltpu.roll(block, total, 1)
        work.append(block)
        diagonal.append(jnp.where(lane == sub + i * tile, block, 0.0))
    across = jnp.sum(sum(diagonal), axis=0, keepdims=True)
    across = lax.rsqrt(jnp.where(lane[:1] < total, across, 1.0))
    for i in range(blocks):
        down = lax.rsqrt(jnp.sum(diagonal[i], axis=1, keepdims=True))
        unit = jnp.where(lane - total == sub + i * tile, down, 0.0)
        work[i] = jnp.where(lane < total, work[i] * down * across, unit)
    copies = []
    cuts = (0, 3 * blocks // 4, blocks)
    for part, (first, last) in enumerate(zip(cuts, cuts[1:])):
        for b in range(first, last):
            eliminate(work, b, columns_ref, rows_ref)
        solver = jnp.concatenate(work[first:last], axis=0) * scale
        wide = iota(solver.shape, 1)
        high, middle, low = (piece.astype(jnp.float32) for piece in split(solver))

        def pair(left, right):
            return jnp.where(wide < total, pltpu.roll(left, total, 1), right).astype(jnp.bfloat16)

        left_main = jnp.concatenate([pair(high, high), pair(middle, middle)], axis=1)
        left_rest = pair(high, low)
        height = (last - first) * tile
        base = first * tile * part_rows
        for row in range(0, part_rows, 2):
            right_main = jnp.concatenate([main_ref[row // 2], main_ref[row // 2]], axis=0)
            right_rest = rest_ref[row // 2]
            result = jnp.dot(left_rest, right_rest, preferred_element_type=jnp.float32) + jnp.dot(
                left_main, right_main, preferred_element_type=jnp.float32
            )
            out_ref[pl.ds(base + row, height, stride=part_rows), :] = result[:, :lanes]
            out_ref[pl.ds(base + row + 1, height, stride=part_rows), :] = result[:, lanes:]
        span = pl.ds(base, height * part_rows)
        copies.append(pltpu.make_async_copy(out_ref.at[span], out_hbm.at[span], copied.at[part]))
        copies[-1].start()
    for copy in copies:
        copy.wait()


def call(kernel, outs, *operands, scratch=(), limit=32, **specs):
    return pl.pallas_call(
        kernel,
        out_shape=[
            jax.ShapeDtypeStruct(shape, jnp.float32) if isinstance(shape, tuple) else shape
            for shape in outs
        ],
        scratch_shapes=[
            pltpu.VMEM(shape, jnp.float32) if isinstance(shape, tuple) else shape
            for shape in scratch
        ],
        compiler_params=pltpu.CompilerParams(vmem_limit_bytes=limit * 1024 * 1024),
        **specs,
    )(*operands)


def exchange(values, axis, distance):
    count = lax.axis_size(axis)
    return lax.ppermute(values, axis, [(i, i ^ distance) for i in range(count)])


axes = ("lx", "ly", "col")


def pair_steps():
    steps = []
    for axis in ("ly", "lx", "col"):
        bit = 2 if axis == "ly" else 1
        while bit < lax.axis_size(axis):
            steps.append((axis, bit))
            bit *= 2
    return steps


def handover(holder, axis, bit):
    sizes = [lax.axis_size(name) for name in axes]
    pairs = []
    for at, (x, y, z) in enumerate(itertools.product(*map(range, sizes))):
        to = {"lx": x, "ly": y ^ 1, "col": z}
        if y % 2 == holder:
            to[axis] ^= bit
        pairs.append((at, (to["lx"] * sizes[1] + to["ly"]) * sizes[2] + to["col"]))
    return pairs


def shards(start, levels):
    cols, rows, _ = start.shape
    parts = lax.axis_size("col")
    chunks = cols // tile
    total = cols * parts
    part_rows = rows // parts
    sizes = (cols, rows, parts)
    early = (parts - 1,)
    order = (*sorted(range(1, parts), key=lambda k: (k in early, -k)), 0)
    flat = start.reshape(cols * rows, lanes)
    piece = (part_rows, cols, lanes)
    start_here, levels_here, edges, half, outer, *raws = call(
        functools.partial(pack_kernel, *sizes, early),
        [flat.shape, jax.ShapeDtypeStruct(levels.shape, levels.dtype), (parts + 1, tile, lanes), (parts // 2 + 1, tile, lanes), (2 * chunks + 1, tile, lanes)]
        + [(cols, part_rows, lanes)] * len(early),
        pltpu.with_memory_space_constraint(flat, pltpu.HBM),
        pltpu.with_memory_space_constraint(levels, pltpu.HBM),
        pltpu.with_memory_space_constraint(start, pltpu.HBM),
        scratch=[pltpu.SemaphoreType.DMA((chunks + 1 + len(early),))],
        limit=32,
        in_specs=[pl.BlockSpec(memory_space=pl.ANY)] * 3,
    )
    count = lax.axis_size("ly")
    near = exchange(edges, "ly", 1)
    far_pairs = [(i, (i + 1) % count if i % 2 else (i - 1) % count) for i in range(count)]
    far = lax.ppermute(half, "ly", far_pairs)
    raws = [exchange(values, "col", k) for k, values in zip(early, raws)]
    beside, outer = call(
        functools.partial(outer_kernel, parts),
        [(parts + 1, tile, lanes), (2 * chunks + 2, tile, lanes)],
        outer,
        near,
        far,
    )
    count = lax.axis_size("lx")
    before = lax.ppermute(outer, "lx", [(i, (i + 1) % count) for i in range(count)])
    after = before
    if count > 2:
        after = lax.ppermute(outer, "lx", [((i + 1) % count, i) for i in range(count)])
    inner = call(
        functools.partial(inner_kernel, *sizes, early),
        [(rows, cols, lanes), (2, cols, lanes), (len(early), tile, lanes)],
        start_here,
        levels_here,
        beside,
        scratch=[(rows, cols, lanes)] * 4 + [(rows, lanes)] * 2,
        cost_estimate=pl.CostEstimate(flops=10**11, bytes_accessed=10**9, transcendentals=0),
    )
    lates = call(
        functools.partial(late_kernel, *sizes, early, order),
        [(2 * chunks + 1, tile, lanes) if k in early else piece for k in order],
        start_here,
        levels_here,
        beside,
        *inner,
        before,
        after,
    )
    lates = [exchange(values, "col", k) if k else values for k, values in zip(order, lates)]
    alones = [
        call(
            functools.partial(alone_kernel, cols, part_rows),
            [piece],
            levels_here,
            raw.reshape(cols * part_rows, lanes),
            scratch=[piece, piece, (rows, lanes)],
            cost_estimate=pl.CostEstimate(flops=0, bytes_accessed=10**6, transcendentals=0),
        )[0]
        for raw in raws
    ]
    whole, gram = call(
        functools.partial(gram_kernel, cols, parts, early, order),
        [(part_rows, total, lanes), (total // 2, 2 * total)],
        *lates,
        *alones,
    )
    gram = gram + exchange(gram, "ly", 1)
    holder = 0
    for axis, bit in pair_steps():
        near = exchange(gram, "ly", 1)
        gram = near + lax.ppermute(gram, axes, handover(holder, axis, bit))
        holder = 1 - holder
    scale = math.sqrt(rows * lax.axis_size("lx") * lanes * lax.axis_size("ly"))
    halves = jax.ShapeDtypeStruct((part_rows // 2, 2 * total, 2 * lanes), jnp.bfloat16)
    split_whole = call(split_kernel, [halves, halves], whole)
    (basis,) = call(
        functools.partial(solve_kernel, scale, holder),
        [(total * part_rows, lanes)],
        *split_whole,
        gram,
        exchange(gram, "ly", 1),
        scratch=[
            (total * part_rows, lanes),
            (2, tile, tile, lanes),
            (2, tile, lanes),
            pltpu.SemaphoreType.DMA((2,)),
        ],
        out_specs=[pl.BlockSpec(memory_space=pl.ANY)],
    )
    return basis.reshape(total, part_rows, lanes)


def solution(mesh):
    placed = (P("col", "lx", "ly"), P("lx", "ly"))
    return jax.shard_map(
        shards, mesh=mesh, in_specs=placed, out_specs=P(None, ("lx", "col"), "ly"), check_vma=False
    )
```
